32 devices in a mesh: strike: 16 (over z, y, x), normal: 2 (over core).
Axes of the slice: x: 2, y: 2, z: 4, core: 2. Of those that a mesh axis runs over, the one named last changes fastest.
Arguments:
- displacement: float32 [3, 512, 16, 128], P(None, 'strike', 'normal'), may hold values from -6 to 6
- velocity: float32 [3, 512, 16, 128], P(None, 'strike', 'normal'), may hold values from -6 to 6
- stiffness: float32 [512, 16, 128], P('strike', 'normal'), may hold values from 0.4 to 1.3
- yield_flags: int32 [128, 16, 32], P('strike', 'normal'), may hold values from 0 to 1
- contact: int32 [2, 512, 128], P(None, 'strike'), may hold values 0 or 1
- history: bfloat16 [2, 8, 2, 3, 128, 512], P(None, None, None, None, 'strike'), may hold values from -6 to 6
- kernel: float32 [2, 8, 3, 512], replicated, may hold values from -1.8 to 1.8
Outputs:
- final_displacement: float32 [3, 512, 16, 128], P(None, 'strike', 'normal')
- final_velocity: float32 [3, 512, 16, 128], P(None, 'strike', 'normal')
The draws below stay inside these ranges and needn't reach their ends.
All inputs are finite; a program needn't handle non-finite values. No bound on the sum of `contact` on one device may be relied on, other than what follows from the above.
Results may differ from the reference program's by a relative error of at most 0.001.
Values may be sent and summed in bfloat16 or wider, within the bound.
No kernel may reach another device: no remote copies, remote signals or barrier semaphores. Data moves between devices by JAX's collectives and lax.ppermute only.
A program may use at most 64 MiB of HBM per device.

```python
import math
import jax
import jax.numpy as jnp
from jax import lax

ND = 128
HIST = 8
SUB = 3
BLK = 4
NS = 512
NN = 16


def plant(entries, rng, low, largest):
    place = [jax.random.randint(jax.random.fold_in(rng, axis), (), 0, length) for axis, length in enumerate(entries.shape)]
    main_axis = entries.shape.index(max(entries.shape))
    neighbour = place[:main_axis] + [(place[main_axis] + 1) % entries.shape[main_axis]] + place[main_axis + 1:]
    return entries.at[tuple(place)].set(low).at[tuple(neighbour)].set(largest)


def levels(key, extent, pieces, least, largest):
    gain = 1.0
    for dim, parts in pieces:
        draws = jax.random.uniform(jax.random.fold_in(jax.random.fold_in(key, 6), dim), (parts,), jnp.float32, least / len(pieces), largest / len(pieces))
        gain = gain * jnp.repeat(jnp.exp(draws), extent[dim] // parts).reshape((-1,) + (1,) * (len(extent) - 1 - dim))
    return gain


def gaussian(stream_key, dims, width, limit, split=(), kind=jnp.bfloat16):
    level = levels(stream_key, dims, split, -0.22, 0.18) if split else 1.0
    result = jax.random.normal(stream_key, dims, jnp.float32) * width * level
    return jnp.minimum(jnp.maximum(result, -limit), limit).astype(kind)


def setup_inputs(seed: int = 0) -> dict:
    splits = jax.random.split(jax.random.key(seed), 8)
    displacement = gaussian(splits[0], (3, NS, NN, ND), 1.0, 6.0, ((1, 16), (2, 2)), jnp.float32)
    velocity = gaussian(splits[1], (3, NS, NN, ND), 1.0, 6.0, ((1, 16), (2, 2)), jnp.float32)
    stiffness = jnp.clip(jnp.exp(math.log(1.3) - 1.1786549 * jax.random.uniform(splits[2], (NS, NN, ND), jnp.float32) ** levels(splits[2], (NS, NN, ND), ((0, 16), (1, 2)), -0.2, 0.2)), 0.4, 1.3)
    yield_flags = plant(jax.random.randint(splits[3], (NS // BLK, NN, ND // BLK), 0, 2), jax.random.fold_in(splits[3], 1), 0, 1).astype(jnp.int32)
    contact = plant((jax.random.randint(splits[4], (2, NS, ND), 0, 4) < 3).astype(jnp.int32), jax.random.fold_in(splits[4], 1), 0, 1)
    history = gaussian(splits[5], (2, HIST, 2, 3, ND, NS), 1.0, 6.0, ((4, 16),))
    kernel = gaussian(splits[6], (2, HIST, 3, NS), 0.3, 1.8, (), jnp.float32)
    return dict(displacement=displacement, velocity=velocity, stiffness=stiffness, yield_flags=yield_flags, contact=contact, history=history, kernel=kernel)


time_step = 0.5

def phase_tables(mode_count, first_mode, block_modes):
    node_ids = jnp.arange(mode_count, dtype=jnp.int32)[:, None]
    mode_ids = (first_mode + jnp.arange(block_modes, dtype=jnp.int32))[None, :]
    phases = (node_ids * mode_ids % mode_count).astype(jnp.float32) * (2.0 * math.pi / mode_count)
    return (jnp.cos(phases).astype(jnp.bfloat16), jnp.sin(phases).astype(jnp.bfloat16))

def blocks_expand(yield_map, block_size):
    strike_blocks, normal_layers, dip_blocks = yield_map.shape
    widened = jnp.broadcast_to(yield_map.astype(jnp.float32)[:, None, :, :, None], (strike_blocks, block_size, normal_layers, dip_blocks, block_size))
    return widened.reshape(strike_blocks * block_size, normal_layers, dip_blocks * block_size)

def laplace_single(values):
    strike_side = jnp.concatenate([values[-1:], values, values[:1]], axis=0)
    normal_side = jnp.pad(values, ((0, 0), (1, 1), (0, 0)))
    dip_padded = jnp.pad(values, ((0, 0), (0, 0), (1, 1)))
    return strike_side[2:] + strike_side[:-2] + (normal_side[:, 2:] + normal_side[:, :-2]) + (dip_padded[..., 2:] + dip_padded[..., :-2]) - 6.0 * values

def reference(displacement, velocity, stiffness, yield_flags, contact, history, kernel):
    modulus = stiffness * (1.0 - 0.5 * blocks_expand(yield_flags, BLK))
    cosines, sines = phase_tables(NS, 0, NS)
    normalizer = 1.0 / math.sqrt(NS)
    planes = jnp.stack([displacement[:, :, 0, :], displacement[:, :, NN - 1, :]]).astype(jnp.bfloat16)
    flat = jnp.swapaxes(planes, 2, 3).reshape(2 * 3 * ND, NS)
    real_part = normalizer * jnp.dot(flat, cosines, preferred_element_type=jnp.float32)
    imag_part = -(normalizer * jnp.dot(flat, sines, preferred_element_type=jnp.float32))
    current = jnp.stack([real_part.reshape(2, 3, ND, NS), imag_part.reshape(2, 3, ND, NS)], axis=1)
    lagged = jnp.concatenate([current[:, None], history[:, :-1].astype(jnp.float32)], axis=1)
    weights = kernel[:, :, None, :, None, :]
    modal_force = lax.optimization_barrier(jnp.sum(weights * lagged, axis=1)).astype(jnp.bfloat16)
    upper = modal_force[:, 0].reshape(2 * 3 * ND, NS)
    lower = modal_force[:, 1].reshape(2 * 3 * ND, NS)
    traction = normalizer * (jnp.dot(upper, cosines.T, preferred_element_type=jnp.float32) - jnp.dot(lower, sines.T, preferred_element_type=jnp.float32))
    traction = jnp.swapaxes(traction.reshape(2, 3, ND, NS), 2, 3)
    pushed = contact.astype(jnp.float32)[:, None] * traction
    force = jnp.zeros_like(displacement).at[:, :, 0, :].set(pushed[0]).at[:, :, NN - 1, :].set(pushed[1])

    def advance(items):
        moved, speed, loading = items
        for substep in range(SUB):
            acceleration = modulus * laplace_single(moved) + loading
            speed = speed + time_step * acceleration
            moved = moved + time_step * speed
        return (moved, speed)
    final_displacement, final_velocity = lax.map(advance, (displacement, velocity, force))
    return (final_displacement, final_velocity)
```

```python
import functools
import math

import jax
import jax.numpy as jnp
import numpy as np
from jax import lax
from jax.experimental import pallas as pl
from jax.experimental.pallas import tpu as pltpu
from jax.sharding import PartitionSpec as P

SUB = 3
BLK = 4
WIN = 4
EDGE = 8
PAD = 4
LANES = 128

time_step = 0.5

f32 = jnp.float32
bf16 = jnp.bfloat16
ANY = pl.BlockSpec(memory_space=pl.ANY)
VMEM = pl.BlockSpec(memory_space=pltpu.VMEM)


def round_up(value, step):
    return -(-value // step) * step


def phase_quarter(mode_count):
    phase = np.outer(np.arange(mode_count), np.arange(mode_count // 4)) % mode_count
    phase = phase * (2.0 * np.pi / mode_count)
    return np.concatenate([np.cos(phase), -np.sin(phase)]).astype(np.float32).astype(bf16)


class Sizes:
    def __init__(self, mesh, displacement, history):
        self.strike = mesh.shape["strike"]
        self.normal = mesh.shape["normal"]
        self.parts, self.nodes, self.layers, self.dips = displacement.shape
        self.lags = history.shape[1]
        self.rows = history.shape[4]
        self.modes = history.shape[5]
        self.chunks = self.modes // LANES
        self.spectral = round_up(self.parts * self.rows, 8)
        self.chunk_rows = round_up(self.spectral + 2 * self.parts, 16)
        self.plane_rows = self.parts * self.nodes
        self.common = self.plane_rows + self.chunks * self.chunk_rows
        self.halo_u = self.common
        self.halo_v = self.halo_u + self.parts * 3 * 2 * self.layers
        self.halo_m = self.halo_v + self.parts * 2 * self.layers
        self.halo_c = self.halo_m + 2 * self.layers
        self.whole = self.halo_c + 16
        self.block = self.nodes + 2 * EDGE
        self.targets = self.strike // WIN
        self.span = self.nodes + 2 * PAD
        self.stride = self.nodes * self.layers
        self.two_sided = self.normal > 2


def widen_flags(flags, dips):
    blocks = flags.shape[1]
    block_id = lax.broadcasted_iota(jnp.int32, (blocks, dips), 0)
    dip_id = lax.broadcasted_iota(jnp.int32, (blocks, dips), 1)
    spread = (dip_id // BLK == block_id).astype(bf16)
    wide = jnp.dot(flags.astype(f32).astype(bf16), spread, preferred_element_type=f32)
    return 1.0 - 0.5 * wide


def prep_kernel(z, u_hbm, v_hbm, s_hbm, y_hbm, c_hbm, h_hbm, k_hbm, t_hbm,
                right_ref, left_ref, far_ref, g_ref,
                u_ref, v_ref, s_ref, y_ref, c_ref, h_ref, k_ref, t_ref, re_ref, im_ref, sems):
    is_high = lax.axis_index("normal") == z.normal - 1
    face = is_high.astype(jnp.int32)
    last = z.nodes - 2
    pairs = [
        (h_hbm.at[face, pl.ds(0, z.lags - 1)], h_ref),
        (k_hbm.at[face], k_ref),
        (t_hbm, t_ref),
        (u_hbm, u_ref),
        (v_hbm.at[:, pl.ds(0, 2)], v_ref.at[0]),
        (v_hbm.at[:, pl.ds(last, 2)], v_ref.at[1]),
        (s_hbm.at[pl.ds(0, 2)], s_ref.at[0]),
        (s_hbm.at[pl.ds(last, 2)], s_ref.at[1]),
        (y_hbm, y_ref),
        (c_hbm.at[face], c_ref),
    ]
    copies = [pltpu.make_async_copy(a, b, sems.at[i]) for i, (a, b) in enumerate(pairs)]
    for copy in copies:
        copy.start()
    re_ref[...] = jnp.zeros_like(re_ref)
    im_ref[...] = jnp.zeros_like(im_ref)
    copies[0].wait()
    copies[1].wait()
    for c in range(z.parts):
        for q, dst in ((0, re_ref), (1, im_ref)):
            total = None
            for lag in range(1, z.lags):
                term = k_ref[lag, pl.ds(c, 1), :] * h_ref[lag - 1, q, c].astype(f32)
                total = term if total is None else total + term
            dst[pl.ds(c * z.rows, z.rows), :] = total
        newest = k_ref[0, pl.ds(c, 1), :]
        high = newest.astype(bf16).astype(f32)
        re_ref[pl.ds(z.spectral + c, 1), :] = high
        re_ref[pl.ds(z.spectral + z.parts + c, 1), :] = newest - high
    re, im = re_ref[...], im_ref[...]
    quarter = lax.broadcasted_iota(jnp.int32, (1, z.modes), 1) % 4
    one = (quarter == 0).astype(f32) - (quarter == 2).astype(f32)
    two = (quarter == 1).astype(f32) - (quarter == 3).astype(f32)
    flip = 1.0 - 2.0 * (quarter % 2).astype(f32)
    turned = jnp.concatenate(
        [
            jnp.concatenate([re, im], axis=1),
            jnp.concatenate([re * one - im * two, re * two + im * one], axis=1),
            jnp.concatenate([re * flip, im * flip], axis=1),
            jnp.concatenate([re * one + im * two, im * one - re * two], axis=1),
        ],
        axis=0,
    ).astype(bf16)
    copies[2].wait()
    lines = jnp.dot(turned, t_ref[...], preferred_element_type=f32) * (1.0 / math.sqrt(z.modes))
    per_quarter = z.chunks // 4
    for m in range(4):
        for q in range(per_quarter):
            piece = lines[m * z.chunk_rows:(m + 1) * z.chunk_rows, q * LANES:(q + 1) * LANES]
            chunk = m * per_quarter + q
            at = pl.ds(z.plane_rows + chunk * z.chunk_rows, z.chunk_rows)
            for ref in (right_ref, left_ref, far_ref):
                ref[at, :] = piece.astype(bf16)
            g_ref[chunk] = piece[z.spectral:z.spectral + 8]
    for copy in copies[3:]:
        copy.wait()
    layer = face * (z.layers - 1)
    for c in range(z.parts):
        plane = u_ref[pl.ds(c * z.stride + layer, z.nodes, stride=z.layers), :].astype(bf16)
        for ref in (right_ref, left_ref, far_ref):
            ref[pl.ds(c * z.nodes, z.nodes), :] = plane
    soft = widen_flags(y_ref[...], z.dips)
    for ref, side, first in ((left_ref, 0, 0), (right_ref, 1, z.nodes - 3)):
        for c in range(z.parts):
            for j in range(3):
                tile = u_ref[pl.ds(c * z.stride + (first + j) * z.layers, z.layers), :]
                high = tile.astype(bf16).astype(f32)
                both = jnp.concatenate([high, tile - high], axis=0).astype(bf16)
                ref[pl.ds(z.halo_u + (c * 3 + j) * 2 * z.layers, 2 * z.layers), :] = both
            both = jnp.concatenate([v_ref[side, c, 0], v_ref[side, c, 1]], axis=0).astype(bf16)
            ref[pl.ds(z.halo_v + c * 2 * z.layers, 2 * z.layers), :] = both
        start = 0 if side == 0 else soft.shape[0] - z.layers
        part = soft[start:start + z.layers]
        both = jnp.concatenate([s_ref[side, 0] * part, s_ref[side, 1] * part], axis=0)
        ref[pl.ds(z.halo_m, 2 * z.layers), :] = both.astype(bf16)
        start = 0 if side == 0 else z.nodes - 16
        ref[pl.ds(z.halo_c, 16), :] = c_ref[pl.ds(start, 16), :].astype(f32).astype(bf16)


def toeplitz_kernel(z, g_ref, out_ref):
    for c in range(z.parts):
        line = jnp.concatenate(
            [
                g_ref[j, pl.ds(c, 1), :] + g_ref[j, pl.ds(z.parts + c, 1), :]
                for j in range(z.chunks)
            ],
            axis=1,
        ) * (1.0 / math.sqrt(z.modes))
        shift = 2 * z.nodes - EDGE
        wide = pltpu.roll(
            jnp.broadcast_to(line, (z.block, z.modes)), shift, 1, stride=1, stride_axis=0
        )
        for s in range(z.targets):
            j = (-s * WIN * z.nodes // LANES) % z.chunks
            out_ref[c, pl.ds(s * z.block, z.block), :] = wide[:, j * LANES:(j + 1) * LANES].astype(bf16)


def middle_kernel(z, toeplitz_ref, far_ref, left_ref, own_ref, right_ref, mine_ref, *out_refs):
    me = lax.axis_index("strike")
    window = (far_ref, left_ref, own_ref, right_ref)
    total = z.targets * z.block
    lines = jnp.concatenate(
        [
            jnp.concatenate(
                [ref[pl.ds(z.plane_rows + j * z.chunk_rows, z.chunk_rows), :] for ref in window],
                axis=0,
            )
            for j in range(z.chunks)
        ],
        axis=1,
    )
    row = lax.broadcasted_iota(jnp.int32, (z.block, z.modes), 0)
    node = lax.broadcasted_iota(jnp.int32, (z.block, z.modes), 1)
    wanted = []
    for s in range(z.targets):
        start = (me + WIN * s) * z.nodes - EDGE + z.modes
        wanted.append((node == (row + start) % z.modes).astype(f32).astype(bf16))
    picked = lax.dot_general(
        jnp.concatenate(wanted, axis=0), lines, (((1,), (1,)), ((), ())), preferred_element_type=f32
    ).astype(bf16)
    row = lax.broadcasted_iota(jnp.int32, (z.chunk_rows, z.dips), 0)
    dip = lax.broadcasted_iota(jnp.int32, (z.chunk_rows, z.dips), 1)
    for c in range(z.parts):
        inside = (row >= c * z.rows) & (row < (c + 1) * z.rows)
        stack = [ref[pl.ds(c * z.nodes, z.nodes), :] for ref in window]
        for w in range(WIN):
            first = z.rows * ((me + w - 2 + z.strike) % z.strike)
            place = inside & (dip - first == row - c * z.rows)
            stack.append(place.astype(f32).astype(bf16))
        factors = jnp.concatenate([toeplitz_ref[c], picked], axis=1)
        part = jnp.dot(factors, jnp.concatenate(stack, axis=0), preferred_element_type=f32)
        at = pl.ds(c * z.block, z.block)
        mine_ref[at, :] = part[:z.block]
        for s, ref in enumerate(out_refs, 1):
            ref[at, :] = part[s * z.block:(s + 1) * z.block].astype(bf16)


def assemble(z, u_hbm, v_hbm, s_hbm, y_hbm, left_ref, right_ref,
             u_ref, v_ref, m_ref, s_ref, y_ref, sems):
    top = PAD * z.layers
    copies = []
    for c in range(z.parts):
        for k, (src, dst) in enumerate(((u_hbm, u_ref), (v_hbm, v_ref))):
            copies.append(
                pltpu.make_async_copy(
                    src.at[pl.ds(c * z.stride, z.stride)],
                    dst.at[c, pl.ds(top, z.stride)],
                    sems.at[2 * c + k],
                )
            )
    copies.append(pltpu.make_async_copy(s_hbm, s_ref, sems.at[2 * z.parts]))
    copies.append(pltpu.make_async_copy(y_hbm, y_ref, sems.at[2 * z.parts + 1]))
    for copy in copies:
        copy.start()
    size = z.layers
    end = (PAD + z.nodes) * size
    blank = jnp.zeros((size, z.dips), f32)
    for ref, at_u, at_v in ((left_ref, PAD - 3, PAD - 2), (right_ref, PAD + z.nodes, PAD + z.nodes)):
        for c in range(z.parts):
            for j in range(3):
                both = ref[pl.ds(z.halo_u + (c * 3 + j) * 2 * size, 2 * size), :].astype(f32)
                u_ref[c, pl.ds((at_u + j) * size, size), :] = both[:size] + both[size:]
            both = ref[pl.ds(z.halo_v + c * 2 * size, 2 * size), :].astype(f32)
            v_ref[c, pl.ds(at_v * size, 2 * size), :] = both
        m_ref[pl.ds(at_v * size, 2 * size), :] = ref[pl.ds(z.halo_m, 2 * size), :].astype(f32)
    for c in range(z.parts):
        u_ref[c, pl.ds(0, size), :] = blank
        u_ref[c, pl.ds(end + 3 * size, size), :] = blank
        for at in (0, size, end + 2 * size, end + 3 * size):
            v_ref[c, pl.ds(at, size), :] = blank
    for at in (0, size, end + 2 * size, end + 3 * size):
        m_ref[pl.ds(at, size), :] = blank
    for copy in copies:
        copy.wait()
    soft = widen_flags(y_ref[...], z.dips)
    for n in range(z.nodes):
        at = n // BLK * size
        m_ref[pl.ds(top + n * size, size), :] = s_ref[pl.ds(n * size, size), :] * soft[at:at + size]


def layer_of(z, level):
    is_high = lax.axis_index("normal") == z.normal - 1
    return jnp.where(is_high, z.layers - 1 - level, level)


def edge_kernel(z, u_hbm, v_hbm, s_hbm, y_hbm, c_hbm, left_ref, right_ref, *rest):
    outs = rest[:-7]
    (u_ref, v_ref, m_ref, s_ref, y_ref, c_ref, sems) = rest[-7:]
    modulus_ref, contact_ref = outs[:2]
    place = lax.axis_index("normal")
    is_high = place == z.normal - 1
    face = is_high.astype(jnp.int32)
    touch = pltpu.make_async_copy(c_hbm.at[face], c_ref, sems.at[2 * z.parts + 2])
    touch.start()
    assemble(z, u_hbm, v_hbm, s_hbm, y_hbm, left_ref, right_ref, u_ref, v_ref, m_ref, s_ref, y_ref, sems)
    for out, levels in zip(outs[2:], ((7, 6, 5), (0, 1, 2))):
        levels = tuple(z.layers - 8 + f if f > 2 else f for f in levels)
        for j, level in enumerate(levels):
            at = pl.ds(layer_of(z, level), z.span, stride=z.layers)
            for c in range(z.parts):
                out[3 * c + j] = u_ref[c, at, :]
                if j < 2:
                    out[3 * z.parts + 2 * c + j] = v_ref[c, at, :]
            if j < 2:
                out[5 * z.parts + j] = m_ref[at, :]
    modulus_ref[...] = jnp.zeros_like(modulus_ref)
    for j in range(3):
        at = pl.ds(layer_of(z, j), z.span, stride=z.layers)
        modulus_ref[j, pl.ds(EDGE - PAD, z.span), :] = m_ref[at, :]
    touch.wait()
    is_face = (is_high | (place == 0)).astype(f32)
    contact_ref[...] = jnp.zeros_like(contact_ref)
    contact_ref[pl.ds(EDGE, z.nodes), :] = c_ref[...].astype(f32) * is_face
    before = left_ref[pl.ds(z.halo_c, 16), :].astype(f32) * is_face
    after = right_ref[pl.ds(z.halo_c, 16), :].astype(f32) * is_face
    contact_ref[pl.ds(0, EDGE), :] = before[16 - EDGE:]
    contact_ref[pl.ds(EDGE + z.nodes, EDGE), :] = after[:EDGE]


def in_plane(values, first_dip, last_dip):
    count, dips = values.shape
    around = pltpu.roll(values, 1, 0) + pltpu.roll(values, count - 1, 0)
    around += jnp.where(first_dip, 0.0, pltpu.roll(values, 1, 1))
    around += jnp.where(last_dip, 0.0, pltpu.roll(values, dips - 1, 1))
    return around - 6.0 * values


def base_kernel(z, u_hbm, v_hbm, s_hbm, y_hbm, left_ref, right_ref, *rest):
    (out_u, out_v, u_ref, v_ref, m_ref, s_ref, y_ref, sems) = rest[-8:]
    sides = rest[:-8]
    assemble(z, u_hbm, v_hbm, s_hbm, y_hbm, left_ref, right_ref, u_ref, v_ref, m_ref, s_ref, y_ref, sems)
    dip = lax.broadcasted_iota(jnp.int32, (z.span, z.dips), 1)
    first_dip, last_dip = dip == 0, dip == z.dips - 1
    low = -2 if z.two_sided else 0
    top = z.layers

    def fetch(kind, c, level):
        if 0 <= level < top:
            at = pl.ds(layer_of(z, level), z.span, stride=z.layers)
            return m_ref[at, :] if kind == "m" else (u_ref if kind == "u" else v_ref)[c, at, :]
        side, j = (sides[0], level - top) if level >= top else (sides[1], -1 - level)
        base = {"u": 3 * c, "v": 3 * z.parts + 2 * c, "m": 5 * z.parts}[kind]
        return side[base + j]

    def one_part(c, unused):
        u = {f: fetch("u", c, f) for f in range(low - 1 if z.two_sided else 0, top + 3)}
        v = {f: fetch("v", c, f) for f in range(low, top + 2)}
        for step in range(SUB):
            levels = range(low + step if z.two_sided else 0, top + 2 - step)
            for f in levels:
                lap = in_plane(u[f], first_dip, last_dip) + u[f + 1]
                if f - 1 in u:
                    lap += u[f - 1]
                v[f] = v[f] + time_step * (fetch("m", c, f) * lap)
            u = {f: u[f] + time_step * v[f] for f in levels}
        for f in range(top):
            at = pl.ds(c * z.stride + layer_of(z, f), z.nodes, stride=z.layers)
            out_u[at, :] = u[f][PAD:PAD + z.nodes]
            out_v[at, :] = v[f][PAD:PAD + z.nodes]
        return unused

    lax.fori_loop(0, z.parts, one_part, 0)


def final_kernel(z, mine_ref, contact_ref, modulus_ref, base_u, base_v, *rest):
    out_u, out_v = rest[-2:]
    dip = lax.broadcasted_iota(jnp.int32, (z.block, z.dips), 1)
    first_dip, last_dip = dip == 0, dip == z.dips - 1
    out_u[...] = base_u[...]
    out_v[...] = base_v[...]
    contact = contact_ref[...]
    m0, m1, m2 = modulus_ref[0], modulus_ref[1], modulus_ref[2]
    h = time_step
    for c in range(z.parts):
        at = pl.ds(c * z.block, z.block)
        force = mine_ref[at, :]
        for ref in rest[:-2]:
            force = force + ref[at, :].astype(f32)
        force = force * contact
        v0 = h * force
        u0 = h * v0
        v1 = h * (m1 * u0)
        v0 = v0 + h * (m0 * in_plane(u0, first_dip, last_dip) + force)
        u0 = u0 + h * v0
        u1 = h * v1
        v2 = h * (m2 * u1)
        w0 = v0 + h * (m0 * (in_plane(u0, first_dip, last_dip) + u1) + force)
        v1 = v1 + h * (m1 * (in_plane(u1, first_dip, last_dip) + u0))
        pairs = ((u0 + h * w0, w0), (u1 + h * v1, v1), (h * v2, v2))
        for f, (du, dv) in enumerate(pairs):
            at = pl.ds(c * z.stride + layer_of(z, f), z.nodes, stride=z.layers)
            out_u[at, :] = out_u[at, :] + du[EDGE:EDGE + z.nodes]
            out_v[at, :] = out_v[at, :] + dv[EDGE:EDGE + z.nodes]


PARAMS = pltpu.CompilerParams(vmem_limit_bytes=32 * 2**20)


def shape(dims, kind):
    return jax.ShapeDtypeStruct(dims, kind)


def body(mesh, displacement, velocity, stiffness, yield_flags, contact, history, kernel):
    z = Sizes(mesh, displacement, history)
    u = displacement.reshape(-1, z.dips)
    v = velocity.reshape(-1, z.dips)
    s = stiffness.reshape(-1, z.dips)
    y = yield_flags.reshape(-1, yield_flags.shape[2])
    dma = pltpu.SemaphoreType.DMA
    ring = lambda step: [(i, (i + step) % z.strike) for i in range(z.strike)]

    to_right, to_left, to_far, response = pl.pallas_call(
        functools.partial(prep_kernel, z),
        out_shape=(
            shape((z.whole, LANES), bf16),
            shape((z.whole, LANES), bf16),
            shape((z.common, LANES), bf16),
            shape((z.chunks, 8, LANES), f32),
        ),
        in_specs=[ANY] * 8,
        out_specs=(VMEM,) * 4,
        scratch_shapes=[
            pltpu.VMEM(u.shape, f32),
            pltpu.VMEM((2, z.parts, 2, z.layers, z.dips), f32),
            pltpu.VMEM((2, 2, z.layers, z.dips), f32),
            pltpu.VMEM(y.shape, jnp.int32),
            pltpu.VMEM(contact.shape[1:], jnp.int32),
            pltpu.VMEM((z.lags - 1, 2, z.parts, z.rows, z.modes), bf16),
            pltpu.VMEM((z.lags, z.parts, z.modes), f32),
            pltpu.VMEM((2 * z.modes, z.modes // 4), bf16),
            pltpu.VMEM((z.chunk_rows, z.modes), f32),
            pltpu.VMEM((z.chunk_rows, z.modes), f32),
            dma((10,)),
        ],
        compiler_params=PARAMS,
        name="prepare",
    )(u, velocity, stiffness, y, contact, history, kernel, phase_quarter(z.modes))

    from_left = lax.ppermute(to_right, "strike", ring(1))
    from_right = lax.ppermute(to_left, "strike", ring(-1))
    from_far = lax.ppermute(to_far, "strike", ring(2))

    toeplitz = pl.pallas_call(
        functools.partial(toeplitz_kernel, z),
        out_shape=shape((z.parts, z.targets * z.block, LANES), bf16),
        in_specs=[VMEM],
        out_specs=VMEM,
        compiler_params=PARAMS,
        name="toeplitz",
    )(response)

    block = (z.parts * z.block, z.dips)
    mine, *parcels = pl.pallas_call(
        functools.partial(middle_kernel, z),
        out_shape=(shape(block, f32),) + (shape(block, bf16),) * (z.targets - 1),
        in_specs=[VMEM] * 5,
        out_specs=(VMEM,) * z.targets,
        compiler_params=PARAMS,
        name="partial_tractions",
    )(toeplitz, from_far, from_left, to_far, from_right)

    arrived = [lax.ppermute(p, "strike", ring(WIN * (k + 1))) for k, p in enumerate(parcels)]

    tiles = [
        pltpu.VMEM((z.parts, z.span * z.layers, z.dips), f32),
        pltpu.VMEM((z.parts, z.span * z.layers, z.dips), f32),
        pltpu.VMEM((z.span * z.layers, z.dips), f32),
        pltpu.VMEM(s.shape, f32),
        pltpu.VMEM(y.shape, jnp.int32),
    ]
    edge = (5 * z.parts + 2, z.span, z.dips)
    sides = 2 if z.two_sided else 1
    modulus, touching, *edges = pl.pallas_call(
        functools.partial(edge_kernel, z),
        out_shape=(shape((3, z.block, z.dips), f32), shape((z.block, z.dips), f32))
        + (shape(edge, f32),) * sides,
        in_specs=[ANY] * 5 + [VMEM] * 2,
        out_specs=(VMEM,) * (2 + sides),
        scratch_shapes=tiles + [pltpu.VMEM(contact.shape[1:], jnp.int32), dma((2 * z.parts + 3,))],
        compiler_params=PARAMS,
        name="normal_edges",
    )(u, v, s, y, contact, from_left, from_right)

    if z.two_sided:
        is_high = lax.axis_index("normal") == z.normal - 1
        above, below = edges
        steps = [(i, i + 1) for i in range(z.normal - 1)]
        from_below = lax.ppermute(above, "normal", steps)
        from_above = lax.ppermute(
            jnp.where(is_high, above, below), "normal", [(j, i) for i, j in steps]
        )
        sided = [
            jnp.where(is_high, from_below, from_above),
            jnp.where(is_high, from_above, from_below),
        ]
    else:
        sided = [lax.ppermute(edges[0], "normal", [(0, 1), (1, 0)])]

    base = pl.pallas_call(
        functools.partial(base_kernel, z),
        out_shape=(shape(u.shape, f32),) * 2,
        in_specs=[ANY] * 4 + [VMEM] * (2 + sides),
        out_specs=(VMEM,) * 2,
        scratch_shapes=tiles + [dma((2 * z.parts + 2,))],
        compiler_params=PARAMS,
        name="unloaded_substeps",
    )(u, v, s, y, from_left, from_right, *sided)

    moved, speed = pl.pallas_call(
        functools.partial(final_kernel, z),
        out_shape=(shape(u.shape, f32),) * 2,
        in_specs=[VMEM] * (5 + len(arrived)),
        out_specs=(VMEM,) * 2,
        compiler_params=PARAMS,
        name="add_force_response",
    )(mine, touching, modulus, *base, *arrived)
    return (moved.reshape(displacement.shape), speed.reshape(displacement.shape))


def solution(mesh):
    return jax.shard_map(
        functools.partial(body, mesh),
        mesh=mesh,
        in_specs=(
            P(None, "strike", "normal", None),
            P(None, "strike", "normal", None),
            P("strike", "normal", None),
            P("strike", "normal", None),
            P(None, "strike", None),
            P(None, None, None, None, "strike", None),
            P(),
        ),
        out_specs=(P(None, "strike", "normal", None), P(None, "strike", "normal", None)),
        check_vma=False,
    )
```

```python
import functools
import math

import jax
import jax.numpy as jnp
import numpy as np
from jax import lax
from jax.experimental import pallas as pl
from jax.experimental.pallas import tpu as pltpu
from jax.sharding import PartitionSpec as P

SUB = 3
BLK = 4
WIN = 4
TAIL = 8
LANES = 128

time_step = 0.5

f32 = jnp.float32
bf16 = jnp.bfloat16
VMEM = pl.BlockSpec(memory_space=pltpu.VMEM)


def round_up(value, step):
    return -(-value // step) * step


def phase_quarter(mode_count):
    phase = np.outer(np.arange(mode_count), np.arange(mode_count // 4)) % mode_count
    phase = phase * (2.0 * np.pi / mode_count)
    return np.concatenate([np.cos(phase), -np.sin(phase)]).astype(np.float32).astype(bf16)


class Sizes:
    def __init__(self, mesh, displacement, history):
        self.strike = mesh.shape["strike"]
        self.normal = mesh.shape["normal"]
        self.parts, self.nodes, self.layers, self.dips = displacement.shape
        self.lags = history.shape[1]
        self.rows = history.shape[4]
        self.modes = history.shape[5]
        self.chunks = self.modes // LANES
        self.spectral = round_up(self.parts * self.rows, 8)
        self.chunk_rows = round_up(self.spectral + 2 * self.parts, 16)
        self.plane_rows = self.parts * self.nodes
        self.common = self.plane_rows + self.chunks * self.chunk_rows
        self.halo_v = self.parts * 3 * 2 * self.layers
        self.halo_m = self.halo_v + self.parts * 2 * self.layers
        self.halo_c = self.halo_m + 2 * self.layers
        self.corner = self.halo_c + 16
        self.span = self.nodes + TAIL
        self.targets = self.strike // WIN
        self.stride = self.nodes * self.layers
        self.sides = 1 if self.normal == 2 else 2
        self.halo = self.corner + round_up(self.sides * self.parts * 8, 16)


def widen_flags(flags, dips):
    blocks = flags.shape[1]
    block_id = lax.broadcasted_iota(jnp.int32, (blocks, dips), 0)
    dip_id = lax.broadcasted_iota(jnp.int32, (blocks, dips), 1)
    spread = (dip_id // BLK == block_id).astype(bf16)
    wide = jnp.dot(flags.astype(f32).astype(bf16), spread, preferred_element_type=f32)
    return 1.0 - 0.5 * wide


def node_offset(rows):
    return jnp.where(rows < rows.shape[0] - TAIL // 2, rows, rows - rows.shape[0])


def layer_of(z, level):
    is_high = lax.axis_index("normal") == z.normal - 1
    return jnp.where(is_high, z.layers - 1 - level, level)


def start_all(pairs, sems):
    copies = [pltpu.make_async_copy(a, b, sems.at[i]) for i, (a, b) in enumerate(pairs)]
    for copy in copies:
        copy.start()
    return copies


def set_modulus(z, s_ref, y_ref, out_ref):
    soft = widen_flags(y_ref[...], z.dips)
    for n in range(z.nodes):
        at = n // BLK * z.layers
        rows = pl.ds(n * z.layers, z.layers)
        out_ref[rows, :] = s_ref[rows, :] * soft[at:at + z.layers]


def common_kernel(z, u_hbm, h_hbm, k_hbm, t_hbm, v_hbm, s_hbm, y_hbm, out_ref, g_ref, *rest):
    edges = rest[:z.sides]
    u_ref, h_ref, k_ref, t_ref, v_ref, s_ref, y_ref, re_ref, im_ref, sems = rest[z.sides:]
    is_high = lax.axis_index("normal") == z.normal - 1
    face = is_high.astype(jnp.int32)
    copies = start_all(
        [
            (h_hbm.at[face, pl.ds(0, z.lags - 1)], h_ref),
            (k_hbm.at[face], k_ref),
            (t_hbm, t_ref),
            (u_hbm, u_ref),
            (v_hbm, v_ref),
            (s_hbm, s_ref),
            (y_hbm, y_ref),
        ],
        sems,
    )
    re_ref[...] = jnp.zeros_like(re_ref)
    im_ref[...] = jnp.zeros_like(im_ref)
    copies[1].wait()
    copies[0].wait()
    for c in range(z.parts):
        for q, dst in ((0, re_ref), (1, im_ref)):
            total = None
            for lag in range(1, z.lags):
                term = k_ref[c, pl.ds(lag, 1), :] * h_ref[lag - 1, q, c].astype(f32)
                total = term if total is None else total + term
            dst[pl.ds(c * z.rows, z.rows), :] = total
        newest = k_ref[c, pl.ds(0, 1), :]
        high = newest.astype(bf16).astype(f32)
        re_ref[pl.ds(z.spectral + c, 1), :] = high
        re_ref[pl.ds(z.spectral + z.parts + c, 1), :] = newest - high
    re, im = re_ref[...], im_ref[...]
    quarter = lax.broadcasted_iota(jnp.int32, (1, z.modes), 1) % 4
    one = (quarter == 0).astype(f32) - (quarter == 2).astype(f32)
    two = (quarter == 1).astype(f32) - (quarter == 3).astype(f32)
    flip = 1.0 - 2.0 * (quarter % 2).astype(f32)
    turned = jnp.concatenate(
        [
            jnp.concatenate([re, im], axis=1),
            jnp.concatenate([re * one - im * two, re * two + im * one], axis=1),
            jnp.concatenate([re * flip, im * flip], axis=1),
            jnp.concatenate([re * one + im * two, im * one - re * two], axis=1),
        ],
        axis=0,
    ).astype(bf16)
    copies[2].wait()
    lines = jnp.dot(turned, t_ref[...], preferred_element_type=f32) * (1.0 / math.sqrt(z.modes))
    per_quarter = z.chunks // 4
    for m in range(4):
        for q in range(per_quarter):
            piece = lines[m * z.chunk_rows:(m + 1) * z.chunk_rows, q * LANES:(q + 1) * LANES]
            chunk = m * per_quarter + q
            out_ref[pl.ds(z.plane_rows + chunk * z.chunk_rows, z.chunk_rows), :] = piece.astype(bf16)
            g_ref[chunk] = piece[z.spectral:z.spectral + 8]
    copies[3].wait()
    layer = face * (z.layers - 1)
    for c in range(z.parts):
        plane = u_ref[pl.ds(c * z.stride + layer, z.nodes, stride=z.layers), :]
        out_ref[pl.ds(c * z.nodes, z.nodes), :] = plane.astype(bf16)
    for copy in copies[4:]:
        copy.wait()
    set_modulus(z, s_ref, y_ref, s_ref)
    size = z.layers
    for out, levels in zip(edges, ((size - 1, size - 2, size - 3), (0, 1, 2))):
        for j, f in enumerate(levels):
            layer = layer_of(z, f)
            for c in range(z.parts):
                at = pl.ds(c * z.stride + layer, z.nodes, stride=size)
                out[3 * c + j] = u_ref[at, :]
                if j < 2:
                    out[3 * z.parts + 2 * c + j] = v_ref[at, :]
            if j < 2:
                out[5 * z.parts + j] = s_ref[pl.ds(layer, z.nodes, stride=size), :]


def halo_kernel(z, u_hbm, v_hbm, s_hbm, y_hbm, c_hbm, *rest):
    beside = rest[:z.sides]
    right_ref, left_ref, u_ref, v_ref, s_ref, y_ref, c_ref, sems = rest[z.sides:]
    is_high = lax.axis_index("normal") == z.normal - 1
    face = is_high.astype(jnp.int32)
    copies = start_all(
        [
            (u_hbm.at[:, pl.ds(0, 3)], u_ref.at[0]),
            (u_hbm.at[:, pl.ds(z.nodes - 3, 3)], u_ref.at[1]),
            (v_hbm.at[:, pl.ds(0, 2)], v_ref.at[0]),
            (v_hbm.at[:, pl.ds(z.nodes - 2, 2)], v_ref.at[1]),
            (s_hbm.at[pl.ds(0, 2)], s_ref.at[0]),
            (s_hbm.at[pl.ds(z.nodes - 2, 2)], s_ref.at[1]),
            (y_hbm, y_ref),
            (c_hbm.at[face], c_ref),
        ],
        sems,
    )
    for copy in copies:
        copy.wait()
    soft = widen_flags(y_ref[...], z.dips)
    for ref, side in ((left_ref, 0), (right_ref, 1)):
        for c in range(z.parts):
            for j in range(3):
                tile = u_ref[side, c, j]
                high = tile.astype(bf16).astype(f32)
                both = jnp.concatenate([high, tile - high], axis=0).astype(bf16)
                ref[pl.ds((c * 3 + j) * 2 * z.layers, 2 * z.layers), :] = both
            both = jnp.concatenate([v_ref[side, c, 0], v_ref[side, c, 1]], axis=0).astype(bf16)
            ref[pl.ds(z.halo_v + c * 2 * z.layers, 2 * z.layers), :] = both
        start = 0 if side == 0 else soft.shape[0] - z.layers
        part = soft[start:start + z.layers]
        both = jnp.concatenate([s_ref[side, 0] * part, s_ref[side, 1] * part], axis=0)
        ref[pl.ds(z.halo_m, 2 * z.layers), :] = both.astype(bf16)
        start = 0 if side == 0 else z.nodes - 16
        ref[pl.ds(z.halo_c, 16), :] = c_ref[pl.ds(start, 16), :].astype(f32).astype(bf16)
        pieces = []
        near = 0 if side == 0 else z.nodes - 1
        pair = 0 if side == 0 else z.nodes - 2
        for edge in beside:
            for c in range(z.parts):
                some = jnp.concatenate(
                    [edge[3 * c, pl.ds(pair, 2), :], edge[3 * c + 1, pl.ds(near, 1), :]], axis=0
                )
                high = some.astype(bf16).astype(f32)
                speed = edge[3 * z.parts + 2 * c, pl.ds(near, 1), :]
                pieces += [high, some - high, speed, edge[5 * z.parts, pl.ds(near, 1), :]]
        spare = z.halo - z.corner - 8 * z.sides * z.parts
        if spare:
            pieces.append(jnp.zeros((spare, z.dips), f32))
        ref[pl.ds(z.corner, z.halo - z.corner), :] = jnp.concatenate(pieces, axis=0).astype(bf16)


def tables_kernel(z, g_ref, s_ref, y_ref, out_ref, m_ref, wide_ref):
    me = lax.axis_index("strike")
    place, group = me % WIN, me // WIN
    for c in range(z.parts):
        line = jnp.concatenate(
            [
                g_ref[j, pl.ds(c, 1), :] + g_ref[j, pl.ds(z.parts + c, 1), :]
                for j in range(z.chunks)
            ],
            axis=1,
        ) * (1.0 / math.sqrt(z.modes))
        wide = jnp.broadcast_to(line, (z.span, z.modes))
        wide = pltpu.roll(wide, 0, 1, stride=1, stride_axis=0)
        last = jnp.broadcast_to(line, (TAIL, z.modes))
        last = pltpu.roll(last, z.modes - TAIL, 1, stride=1, stride_axis=0)
        row = lax.broadcasted_iota(jnp.int32, (TAIL, z.modes), 0)
        last = jnp.where(row < TAIL // 2, wide[z.nodes:], last)
        wide = jnp.concatenate([wide[:z.nodes], last], axis=0)
        wide = pltpu.roll(wide, place * z.nodes, 1)
        for j in range(z.chunks):
            wide_ref[j] = wide[:, j * LANES:(j + 1) * LANES]
        for s in range(z.targets):
            j = (group - (group ^ s) + z.chunks) % z.chunks
            out_ref[c, pl.ds(s * z.span, z.span), :] = wide_ref[j]
    set_modulus(z, s_ref, y_ref, m_ref)


def middle_kernel(z, toeplitz_ref, *rest):
    window, mine_ref, out_refs, stack_ref = rest[:WIN], rest[WIN], rest[WIN + 1:-1], rest[-1]
    me = lax.axis_index("strike")
    place, group = me % WIN, me // WIN
    lines = jnp.concatenate(
        [
            jnp.concatenate(
                [ref[pl.ds(z.plane_rows + j * z.chunk_rows, z.chunk_rows), :] for ref in window],
                axis=0,
            )
            for j in range(z.chunks)
        ],
        axis=1,
    )
    offset = node_offset(lax.broadcasted_iota(jnp.int32, (z.span, z.modes), 0))
    away = lax.broadcasted_iota(jnp.int32, (z.span, z.modes), 1) - offset
    away = jnp.where(away < 0, away + z.modes, away)
    away = jnp.where(away >= z.modes, away - z.modes, away)
    wanted = [
        (away == ((group ^ s) * WIN + place) * z.nodes).astype(f32) for s in range(z.targets)
    ]
    picked = lax.dot_general(
        jnp.concatenate(wanted, axis=0).astype(bf16),
        lines,
        (((1,), (1,)), ((), ())),
        preferred_element_type=f32,
    )
    row = lax.broadcasted_iota(jnp.int32, (z.chunk_rows, z.dips), 0)
    ahead = lax.broadcasted_iota(jnp.int32, (z.chunk_rows, z.dips), 1) - row
    own_rows = WIN * z.nodes
    parts = []
    for c in range(z.parts):
        inside = (row >= c * z.rows) & (row < (c + 1) * z.rows)
        for w, ref in enumerate(window):
            at = pl.multiple_of((place ^ w) * z.nodes, z.nodes)
            stack_ref[c, pl.ds(at, z.nodes), :] = ref[pl.ds(c * z.nodes, z.nodes), :]
            spot = inside & (ahead == z.rows * (me ^ w) - c * z.rows)
            at = pl.ds(own_rows + w * z.chunk_rows, z.chunk_rows)
            stack_ref[c, at, :] = spot.astype(f32).astype(bf16)
        factors = jnp.concatenate([toeplitz_ref[c], picked], axis=1).astype(bf16)
        parts.append(jnp.dot(factors, stack_ref[c], preferred_element_type=f32))
        mine_ref[pl.ds(c * z.span, z.span), :] = parts[c][:z.span]
    for s, ref in enumerate(out_refs, 1):
        ref[...] = jnp.concatenate(
            [part[s * z.span:(s + 1) * z.span] for part in parts], axis=0
        ).astype(bf16)


def unpack(z, left_ref, right_ref, uh_ref, vh_ref, mh_ref):
    size = z.layers
    for ref, at_u, at_v in ((right_ref, 0, 0), (left_ref, TAIL - 3, TAIL - 2)):
        for c in range(z.parts):
            for j in range(3):
                both = ref[pl.ds((c * 3 + j) * 2 * size, 2 * size), :].astype(f32)
                uh_ref[c, pl.ds((at_u + j) * size, size), :] = both[:size] + both[size:]
            both = ref[pl.ds(z.halo_v + c * 2 * size, 2 * size), :].astype(f32)
            vh_ref[c, pl.ds(at_v * size, 2 * size), :] = both
        mh_ref[pl.ds(at_v * size, 2 * size), :] = ref[pl.ds(z.halo_m, 2 * size), :].astype(f32)
    for c in range(z.parts):
        uh_ref[c, pl.ds(3 * size, 2 * size), :] = jnp.zeros((2 * size, z.dips), f32)
        vh_ref[c, pl.ds(2 * size, 4 * size), :] = jnp.zeros((4 * size, z.dips), f32)
    mh_ref[pl.ds(2 * size, 4 * size), :] = jnp.zeros((4 * size, z.dips), f32)


def corner_tiles(z, left_ref, right_ref, tile_ref):
    rows = pl.ds(z.corner, z.halo - z.corner)
    after, before = right_ref[rows, :].astype(f32), left_ref[rows, :].astype(f32)
    blank = jnp.zeros((TAIL, z.dips), f32)

    def tile(head, tail):
        return jnp.concatenate([head, blank[:TAIL - head.shape[0] - tail.shape[0]], tail], axis=0)

    for side in range(z.sides):
        for c in range(z.parts):
            at = 8 * (side * z.parts + c)
            a, b = after[at:at + 8], before[at:at + 8]
            head, tail = a[0:3] + a[3:6], b[0:3] + b[3:6]
            tile_ref[side, 3 * c] = tile(head[:2], tail[:2])
            tile_ref[side, 3 * c + 1] = tile(head[2:], tail[2:])
            tile_ref[side, 3 * c + 2] = blank
            tile_ref[side, 3 * z.parts + 2 * c] = tile(a[6:7], b[6:7])
            tile_ref[side, 3 * z.parts + 2 * c + 1] = blank
            if c == 0:
                tile_ref[side, 5 * z.parts] = tile(a[7:8], b[7:8])
                tile_ref[side, 5 * z.parts + 1] = blank


def in_plane(values, first_dip, last_dip):
    count, dips = values.shape
    around = pltpu.roll(values, 1, 0) + pltpu.roll(values, count - 1, 0)
    around += jnp.where(first_dip, 0.0, pltpu.roll(values, 1, 1))
    around += jnp.where(last_dip, 0.0, pltpu.roll(values, dips - 1, 1))
    return around - 6.0 * values


def base_kernel(z, u_ref, v_ref, m_ref, c_ref, left_ref, right_ref, *rest):
    sides = rest[:z.sides]
    out_u, out_v, mh_ref, ch_ref, uh_ref, vh_ref, tile_ref = rest[z.sides:]
    unpack(z, left_ref, right_ref, uh_ref, vh_ref, mh_ref)
    corner_tiles(z, left_ref, right_ref, tile_ref)
    place = lax.axis_index("normal")
    is_high = place == z.normal - 1
    is_face = (is_high | (place == 0)).astype(f32)
    row = lax.broadcasted_iota(jnp.int32, (TAIL, z.dips), 0)
    before = left_ref[pl.ds(z.halo_c, 16), :].astype(f32)[16 - TAIL:]
    after = right_ref[pl.ds(z.halo_c, 16), :].astype(f32)[:TAIL]
    own = jnp.where(is_high, c_ref[1], c_ref[0]).astype(f32)
    tail = jnp.where(row < TAIL // 2, after, before)
    ch_ref[...] = jnp.concatenate([own, tail], axis=0) * is_face
    dip = lax.broadcasted_iota(jnp.int32, (z.span, z.dips), 1)
    first_dip, last_dip = dip == 0, dip == z.dips - 1
    low = -2 if z.sides == 2 else 0
    top = z.layers

    def fetch(kind, c, f):
        if 0 <= f < top:
            layer = layer_of(z, f)
            own = {"u": u_ref, "v": v_ref, "m": m_ref}[kind]
            first = 0 if kind == "m" else c * z.stride
            tail = mh_ref if kind == "m" else (uh_ref if kind == "u" else vh_ref).at[c]
            return jnp.concatenate(
                [
                    own[pl.ds(first + layer, z.nodes, stride=top), :],
                    tail[pl.ds(layer, TAIL, stride=top), :],
                ],
                axis=0,
            )
        side, j = (0, f - top) if f >= top else (1, -1 - f)
        at = {"u": 3 * c, "v": 3 * z.parts + 2 * c, "m": 5 * z.parts}[kind] + j
        return jnp.concatenate([sides[side][at], tile_ref[side, at]], axis=0)

    def one_part(c, unused):
        u = {f: fetch("u", c, f) for f in range(low - 1 if z.sides == 2 else 0, top + 3)}
        v = {f: fetch("v", c, f) for f in range(low, top + 2)}
        for step in range(SUB):
            levels = range(low + step if z.sides == 2 else 0, top + 2 - step)
            for f in levels:
                lap = in_plane(u[f], first_dip, last_dip) + u[f + 1]
                if f - 1 in u:
                    lap += u[f - 1]
                v[f] = v[f] + time_step * (fetch("m", c, f) * lap)
            u = {f: u[f] + time_step * v[f] for f in levels}
        for f in range(top):
            at = pl.ds(c * z.stride + layer_of(z, f), z.nodes, stride=z.layers)
            out_u[at, :] = u[f][:z.nodes]
            out_v[at, :] = v[f][:z.nodes]
        return unused

    lax.fori_loop(0, z.parts, one_part, 0)


def final_kernel(z, mine_ref, contact_ref, m_ref, mh_ref, base_u, base_v, *rest):
    out_u, out_v = rest[-2:]
    dip = lax.broadcasted_iota(jnp.int32, (z.span, z.dips), 1)
    first_dip, last_dip = dip == 0, dip == z.dips - 1
    out_u[...] = base_u[...]
    out_v[...] = base_v[...]
    contact = contact_ref[...]
    m0, m1, m2 = (
        jnp.concatenate(
            [
                m_ref[pl.ds(layer_of(z, f), z.nodes, stride=z.layers), :],
                mh_ref[pl.ds(layer_of(z, f), TAIL, stride=z.layers), :],
            ],
            axis=0,
        )
        for f in range(3)
    )
    h = time_step
    arrived = [ref[...].astype(f32) for ref in rest[:-2]]
    for c in range(z.parts):
        force = mine_ref[pl.ds(c * z.span, z.span), :]
        for other in arrived:
            force = force + other[c * z.span:(c + 1) * z.span]
        force = force * contact
        v0 = h * force
        u0 = h * v0
        v1 = h * (m1 * u0)
        v0 = v0 + h * (m0 * in_plane(u0, first_dip, last_dip) + force)
        u0 = u0 + h * v0
        u1 = h * v1
        v2 = h * (m2 * u1)
        w0 = v0 + h * (m0 * (in_plane(u0, first_dip, last_dip) + u1) + force)
        v1 = v1 + h * (m1 * (in_plane(u1, first_dip, last_dip) + u0))
        pairs = ((u0 + h * w0, w0), (u1 + h * v1, v1), (h * v2, v2))
        for f, (du, dv) in enumerate(pairs):
            at = pl.ds(c * z.stride + layer_of(z, f), z.nodes, stride=z.layers)
            out_u[at, :] = out_u[at, :] + du[:z.nodes]
            out_v[at, :] = out_v[at, :] + dv[:z.nodes]


PARAMS = pltpu.CompilerParams(vmem_limit_bytes=32 * 2**20)
FIRST = pltpu.CompilerParams(vmem_limit_bytes=63 * 2**20)
HBM = pl.BlockSpec(memory_space=pltpu.HBM)


def shape(dims, kind):
    return jax.ShapeDtypeStruct(dims, kind)


def body(mesh, displacement, velocity, stiffness, yield_flags, contact, history, kernel):
    z = Sizes(mesh, displacement, history)
    u = displacement.reshape(-1, z.dips)
    v = velocity.reshape(-1, z.dips)
    s = stiffness.reshape(-1, z.dips)
    y = yield_flags.reshape(-1, yield_flags.shape[2])
    dma = pltpu.SemaphoreType.DMA
    ring = lambda step: [(i, (i + step) % z.strike) for i in range(z.strike)]
    swap = lambda mask: [(i, i ^ mask) for i in range(z.strike)]

    edge = (5 * z.parts + 2, z.nodes, z.dips)
    common, response, *edges = pl.pallas_call(
        functools.partial(common_kernel, z),
        out_shape=(shape((z.common, LANES), bf16), shape((z.chunks, 8, LANES), f32))
        + (shape(edge, f32),) * z.sides,
        in_specs=[HBM] * 7,
        out_specs=(VMEM,) * (2 + z.sides),
        scratch_shapes=[
            pltpu.VMEM(u.shape, f32),
            pltpu.VMEM((z.lags - 1, 2, z.parts, z.rows, z.modes), bf16),
            pltpu.VMEM((z.parts, z.lags, z.modes), f32),
            pltpu.VMEM((2 * z.modes, z.modes // 4), bf16),
            pltpu.VMEM(v.shape, f32),
            pltpu.VMEM(s.shape, f32),
            pltpu.VMEM(y.shape, jnp.int32),
            pltpu.VMEM((z.chunk_rows, z.modes), f32),
            pltpu.VMEM((z.chunk_rows, z.modes), f32),
            dma((7,)),
        ],
        compiler_params=FIRST,
        name="plane_and_history",
    )(u, history, kernel.transpose(0, 2, 1, 3), phase_quarter(z.modes), v, s, y)

    window = [common] + [lax.ppermute(common, "strike", swap(w)) for w in range(1, WIN)]

    if z.sides == 2:
        is_high = lax.axis_index("normal") == z.normal - 1
        above, below = edges
        steps = [(i, i + 1) for i in range(z.normal - 1)]
        from_below = lax.ppermute(above, "normal", steps)
        from_above = lax.ppermute(
            jnp.where(is_high, above, below), "normal", [(j, i) for i, j in steps]
        )
        beside = [
            jnp.where(is_high, from_below, from_above),
            jnp.where(is_high, from_above, from_below),
        ]
    else:
        beside = [lax.ppermute(edges[0], "normal", [(0, 1), (1, 0)])]

    to_right, to_left = pl.pallas_call(
        functools.partial(halo_kernel, z),
        out_shape=(shape((z.halo, LANES), bf16),) * 2,
        in_specs=[HBM] * 5 + [VMEM] * z.sides,
        out_specs=(VMEM,) * 2,
        scratch_shapes=[
            pltpu.VMEM((2, z.parts, 3, z.layers, z.dips), f32),
            pltpu.VMEM((2, z.parts, 2, z.layers, z.dips), f32),
            pltpu.VMEM((2, 2, z.layers, z.dips), f32),
            pltpu.VMEM(y.shape, jnp.int32),
            pltpu.VMEM(contact.shape[1:], jnp.int32),
            dma((8,)),
        ],
        compiler_params=PARAMS,
        name="strike_edges",
    )(displacement, velocity, stiffness, y, contact, *beside)
    from_left = lax.ppermute(to_right, "strike", ring(1))
    from_right = lax.ppermute(to_left, "strike", ring(-1))

    toeplitz, modulus = pl.pallas_call(
        functools.partial(tables_kernel, z),
        out_shape=(shape((z.parts, z.targets * z.span, LANES), f32), shape(s.shape, f32)),
        in_specs=[VMEM] * 3,
        out_specs=(VMEM,) * 2,
        scratch_shapes=[pltpu.VMEM((z.chunks, z.span, LANES), f32)],
        compiler_params=PARAMS,
        name="toeplitz_and_modulus",
    )(response, s, y)

    block = (z.parts * z.span, z.dips)
    mine, *parcels = pl.pallas_call(
        functools.partial(middle_kernel, z),
        out_shape=(shape(block, f32),) + (shape(block, bf16),) * (z.targets - 1),
        in_specs=[VMEM] * (1 + WIN),
        out_specs=(VMEM,) * z.targets,
        scratch_shapes=[pltpu.VMEM((z.parts, WIN * (z.nodes + z.chunk_rows), z.dips), bf16)],
        compiler_params=PARAMS,
        name="partial_tractions",
    )(toeplitz, *window)

    arrived = [lax.ppermute(p, "strike", swap(WIN * (k + 1))) for k, p in enumerate(parcels)]
    tail = (z.parts, TAIL * z.layers, z.dips)
    base_u, base_v, tail_modulus, touching = pl.pallas_call(
        functools.partial(base_kernel, z),
        out_shape=(
            shape(u.shape, f32),
            shape(u.shape, f32),
            shape(tail[1:], f32),
            shape((z.span, z.dips), f32),
        ),
        in_specs=[VMEM] * (6 + z.sides),
        out_specs=(VMEM,) * 4,
        scratch_shapes=[
            pltpu.VMEM(tail, f32),
            pltpu.VMEM(tail, f32),
            pltpu.VMEM((z.sides, edge[0], TAIL, z.dips), f32),
        ],
        compiler_params=PARAMS,
        name="unloaded_substeps",
    )(u, v, modulus, contact, from_left, from_right, *beside)

    moved, speed = pl.pallas_call(
        functools.partial(final_kernel, z),
        out_shape=(shape(u.shape, f32),) * 2,
        in_specs=[VMEM] * (6 + len(arrived)),
        out_specs=(VMEM,) * 2,
        compiler_params=PARAMS,
        name="add_force_response",
    )(mine, touching, modulus, tail_modulus, base_u, base_v, *arrived)
    return (moved.reshape(displacement.shape), speed.reshape(displacement.shape))


def solution(mesh):
    return jax.shard_map(
        functools.partial(body, mesh),
        mesh=mesh,
        in_specs=(
            P(None, "strike", "normal", None),
            P(None, "strike", "normal", None),
            P("strike", "normal", None),
            P("strike", "normal", None),
            P(None, "strike", None),
            P(None, None, None, None, "strike", None),
            P(),
        ),
        out_specs=(P(None, "strike", "normal", None), P(None, "strike", "normal", None)),
        check_vma=False,
    )
```

```python
import functools
import math

import jax
import jax.numpy as jnp
import numpy as np
from jax import lax
from jax.experimental import pallas as pl
from jax.experimental.pallas import tpu as pltpu
from jax.sharding import PartitionSpec as P

SUB = 3
BLK = 4
WIN = 4
TAIL = 8
LANES = 128

time_step = 0.5

f32 = jnp.float32
bf16 = jnp.bfloat16
VMEM = pl.BlockSpec(memory_space=pltpu.VMEM)


def round_up(value, step):
    return -(-value // step) * step


def phase_quarter(mode_count):
    phase = np.outer(np.arange(mode_count), np.arange(mode_count // 4)) % mode_count
    phase = phase * (2.0 * np.pi / mode_count)
    return np.concatenate([np.cos(phase), -np.sin(phase)]).astype(np.float32).astype(bf16)


class Sizes:
    def __init__(self, mesh, displacement, history):
        self.strike = mesh.shape["strike"]
        self.normal = mesh.shape["normal"]
        self.parts, self.nodes, self.layers, self.dips = displacement.shape
        self.lags = history.shape[1]
        self.rows = history.shape[4]
        self.modes = history.shape[5]
        self.chunks = self.modes // LANES
        self.spectral = round_up(self.parts * self.rows, 8)
        self.chunk_rows = round_up(self.spectral + 2 * self.parts, 16)
        self.plane_rows = self.parts * self.nodes
        self.common = self.plane_rows + self.chunks * self.chunk_rows
        self.halo_v = self.parts * 3 * 2 * self.layers
        self.halo_m = self.halo_v + self.parts * 2 * self.layers
        self.halo_c = self.halo_m + 2 * self.layers
        self.corner = self.halo_c + 16
        self.span = self.nodes + TAIL
        self.targets = self.strike // WIN
        self.stride = self.nodes * self.layers
        self.sides = 1 if self.normal == 2 else 2
        self.halo = self.corner + round_up(self.sides * self.parts * 8, 16)


def widen_flags(flags, dips):
    blocks = flags.shape[1]
    block_id = lax.broadcasted_iota(jnp.int32, (blocks, dips), 0)
    dip_id = lax.broadcasted_iota(jnp.int32, (blocks, dips), 1)
    spread = (dip_id // BLK == block_id).astype(bf16)
    wide = jnp.dot(flags.astype(f32).astype(bf16), spread, preferred_element_type=f32)
    return 1.0 - 0.5 * wide


def node_offset(rows):
    return jnp.where(rows < rows.shape[0] - TAIL // 2, rows, rows - rows.shape[0])


def layer_of(z, level):
    is_high = lax.axis_index("normal") == z.normal - 1
    return jnp.where(is_high, z.layers - 1 - level, level)


def start_all(pairs, sems):
    copies = [pltpu.make_async_copy(a, b, sems.at[i]) for i, (a, b) in enumerate(pairs)]
    for copy in copies:
        copy.start()
    return copies


def set_modulus(z, s_ref, y_ref, out_ref):
    soft = widen_flags(y_ref[...], z.dips)
    for n in range(z.nodes):
        at = n // BLK * z.layers
        rows = pl.ds(n * z.layers, z.layers)
        out_ref[rows, :] = s_ref[rows, :] * soft[at:at + z.layers]


def common_kernel(z, u_hbm, h_hbm, k_hbm, t_hbm, v_hbm, s_hbm, y_hbm, out_ref, g_ref, *rest):
    edges = rest[:z.sides]
    u_ref, h_ref, k_ref, t_ref, v_ref, s_ref, y_ref, re_ref, im_ref, sems = rest[z.sides:]
    is_high = lax.axis_index("normal") == z.normal - 1
    face = is_high.astype(jnp.int32)
    copies = start_all(
        [
            (h_hbm.at[face, pl.ds(0, z.lags - 1)], h_ref),
            (k_hbm.at[face], k_ref),
            (t_hbm, t_ref),
            (u_hbm, u_ref),
            (v_hbm, v_ref),
            (s_hbm, s_ref),
            (y_hbm, y_ref),
        ],
        sems,
    )
    re_ref[...] = jnp.zeros_like(re_ref)
    im_ref[...] = jnp.zeros_like(im_ref)
    copies[1].wait()
    copies[0].wait()
    for c in range(z.parts):
        for q, dst in ((0, re_ref), (1, im_ref)):
            total = None
            for lag in range(1, z.lags):
                term = k_ref[c, pl.ds(lag, 1), :] * h_ref[lag - 1, q, c].astype(f32)
                total = term if total is None else total + term
            dst[pl.ds(c * z.rows, z.rows), :] = total
        newest = k_ref[c, pl.ds(0, 1), :]
        high = newest.astype(bf16).astype(f32)
        re_ref[pl.ds(z.spectral + c, 1), :] = high
        re_ref[pl.ds(z.spectral + z.parts + c, 1), :] = newest - high
    re, im = re_ref[...], im_ref[...]
    quarter = lax.broadcasted_iota(jnp.int32, (1, z.modes), 1) % 4
    one = (quarter == 0).astype(f32) - (quarter == 2).astype(f32)
    two = (quarter == 1).astype(f32) - (quarter == 3).astype(f32)
    flip = 1.0 - 2.0 * (quarter % 2).astype(f32)
    turned = jnp.concatenate(
        [
            jnp.concatenate([re, im], axis=1),
            jnp.concatenate([re * one - im * two, re * two + im * one], axis=1),
            jnp.concatenate([re * flip, im * flip], axis=1),
            jnp.concatenate([re * one + im * two, im * one - re * two], axis=1),
        ],
        axis=0,
    ).astype(bf16)
    copies[2].wait()
    lines = jnp.dot(turned, t_ref[...], preferred_element_type=f32) * (1.0 / math.sqrt(z.modes))
    per_quarter = z.chunks // 4
    for m in range(4):
        for q in range(per_quarter):
            piece = lines[m * z.chunk_rows:(m + 1) * z.chunk_rows, q * LANES:(q + 1) * LANES]
            chunk = m * per_quarter + q
            out_ref[pl.ds(z.plane_rows + chunk * z.chunk_rows, z.chunk_rows), :] = piece.astype(bf16)
            g_ref[chunk] = piece[z.spectral:z.spectral + 8]
    copies[3].wait()
    layer = face * (z.layers - 1)
    for c in range(z.parts):
        plane = u_ref[pl.ds(c * z.stride + layer, z.nodes, stride=z.layers), :]
        out_ref[pl.ds(c * z.nodes, z.nodes), :] = plane.astype(bf16)
    for copy in copies[4:]:
        copy.wait()
    set_modulus(z, s_ref, y_ref, s_ref)
    size = z.layers
    for out, levels in zip(edges, ((size - 1, size - 2, size - 3), (0, 1, 2))):
        for j, f in enumerate(levels):
            layer = layer_of(z, f)
            for c in range(z.parts):
                at = pl.ds(c * z.stride + layer, z.nodes, stride=size)
                out[3 * c + j] = u_ref[at, :]
                if j < 2:
                    out[3 * z.parts + 2 * c + j] = v_ref[at, :]
            if j < 2:
                out[5 * z.parts + j] = s_ref[pl.ds(layer, z.nodes, stride=size), :]


def halo_kernel(z, u_hbm, v_hbm, s_hbm, y_hbm, c_hbm, *rest):
    beside = rest[:z.sides]
    right_ref, left_ref, u_ref, v_ref, s_ref, y_ref, c_ref, sems = rest[z.sides:]
    is_high = lax.axis_index("normal") == z.normal - 1
    face = is_high.astype(jnp.int32)
    copies = start_all(
        [
            (u_hbm.at[:, pl.ds(0, 3)], u_ref.at[0]),
            (u_hbm.at[:, pl.ds(z.nodes - 3, 3)], u_ref.at[1]),
            (v_hbm.at[:, pl.ds(0, 2)], v_ref.at[0]),
            (v_hbm.at[:, pl.ds(z.nodes - 2, 2)], v_ref.at[1]),
            (s_hbm.at[pl.ds(0, 2)], s_ref.at[0]),
            (s_hbm.at[pl.ds(z.nodes - 2, 2)], s_ref.at[1]),
            (y_hbm, y_ref),
            (c_hbm.at[face], c_ref),
        ],
        sems,
    )
    for copy in copies:
        copy.wait()
    soft = widen_flags(y_ref[...], z.dips)
    for ref, side in ((left_ref, 0), (right_ref, 1)):
        for c in range(z.parts):
            for j in range(3):
                tile = u_ref[side, c, j]
                high = tile.astype(bf16).astype(f32)
                both = jnp.concatenate([high, tile - high], axis=0).astype(bf16)
                ref[pl.ds((c * 3 + j) * 2 * z.layers, 2 * z.layers), :] = both
            both = jnp.concatenate([v_ref[side, c, 0], v_ref[side, c, 1]], axis=0).astype(bf16)
            ref[pl.ds(z.halo_v + c * 2 * z.layers, 2 * z.layers), :] = both
        start = 0 if side == 0 else soft.shape[0] - z.layers
        part = soft[start:start + z.layers]
        both = jnp.concatenate([s_ref[side, 0] * part, s_ref[side, 1] * part], axis=0)
        ref[pl.ds(z.halo_m, 2 * z.layers), :] = both.astype(bf16)
        start = 0 if side == 0 else z.nodes - 16
        ref[pl.ds(z.halo_c, 16), :] = c_ref[pl.ds(start, 16), :].astype(f32).astype(bf16)
        pieces = []
        near = 0 if side == 0 else z.nodes - 1
        pair = 0 if side == 0 else z.nodes - 2
        for edge in beside:
            for c in range(z.parts):
                some = jnp.concatenate(
                    [edge[3 * c, pl.ds(pair, 2), :], edge[3 * c + 1, pl.ds(near, 1), :]], axis=0
                )
                high = some.astype(bf16).astype(f32)
                speed = edge[3 * z.parts + 2 * c, pl.ds(near, 1), :]
                pieces += [high, some - high, speed, edge[5 * z.parts, pl.ds(near, 1), :]]
        spare = z.halo - z.corner - 8 * z.sides * z.parts
        if spare:
            pieces.append(jnp.zeros((spare, z.dips), f32))
        ref[pl.ds(z.corner, z.halo - z.corner), :] = jnp.concatenate(pieces, axis=0).astype(bf16)


def toeplitz_kernel(z, g_ref, out_ref, wide_ref):
    me = lax.axis_index("strike")
    place, group = me % WIN, me // WIN
    for c in range(z.parts):
        line = jnp.concatenate(
            [
                g_ref[j, pl.ds(c, 1), :] + g_ref[j, pl.ds(z.parts + c, 1), :]
                for j in range(z.chunks)
            ],
            axis=1,
        ) * (1.0 / math.sqrt(z.modes))
        wide = jnp.broadcast_to(line, (z.span, z.modes))
        wide = pltpu.roll(wide, 0, 1, stride=1, stride_axis=0)
        last = jnp.broadcast_to(line, (TAIL, z.modes))
        last = pltpu.roll(last, z.modes - TAIL, 1, stride=1, stride_axis=0)
        row = lax.broadcasted_iota(jnp.int32, (TAIL, z.modes), 0)
        last = jnp.where(row < TAIL // 2, wide[z.nodes:], last)
        wide = jnp.concatenate([wide[:z.nodes], last], axis=0)
        wide = pltpu.roll(wide, place * z.nodes, 1)
        for j in range(z.chunks):
            wide_ref[j] = wide[:, j * LANES:(j + 1) * LANES]
        for s in range(z.targets):
            j = (group - (group ^ s) + z.chunks) % z.chunks
            out_ref[c, pl.ds(s * z.span, z.span), :] = wide_ref[j]


def middle_kernel(z, toeplitz_ref, *rest):
    window, mine_ref, out_refs, stack_ref = rest[:WIN], rest[WIN], rest[WIN + 1:-1], rest[-1]
    me = lax.axis_index("strike")
    place, group = me % WIN, me // WIN
    lines = jnp.concatenate(
        [
            jnp.concatenate(
                [ref[pl.ds(z.plane_rows + j * z.chunk_rows, z.chunk_rows), :] for ref in window],
                axis=0,
            )
            for j in range(z.chunks)
        ],
        axis=1,
    )
    offset = node_offset(lax.broadcasted_iota(jnp.int32, (z.span, z.modes), 0))
    away = lax.broadcasted_iota(jnp.int32, (z.span, z.modes), 1) - offset
    away = jnp.where(away < 0, away + z.modes, away)
    away = jnp.where(away >= z.modes, away - z.modes, away)
    wanted = [
        (away == ((group ^ s) * WIN + place) * z.nodes).astype(f32) for s in range(z.targets)
    ]
    picked = lax.dot_general(
        jnp.concatenate(wanted, axis=0).astype(bf16),
        lines,
        (((1,), (1,)), ((), ())),
        preferred_element_type=f32,
    )
    row = lax.broadcasted_iota(jnp.int32, (z.chunk_rows, z.dips), 0)
    ahead = lax.broadcasted_iota(jnp.int32, (z.chunk_rows, z.dips), 1) - row
    own_rows = WIN * z.nodes
    parts = []
    for c in range(z.parts):
        inside = (row >= c * z.rows) & (row < (c + 1) * z.rows)
        for w, ref in enumerate(window):
            at = pl.multiple_of((place ^ w) * z.nodes, z.nodes)
            stack_ref[c, pl.ds(at, z.nodes), :] = ref[pl.ds(c * z.nodes, z.nodes), :]
            spot = inside & (ahead == z.rows * (me ^ w) - c * z.rows)
            at = pl.ds(own_rows + w * z.chunk_rows, z.chunk_rows)
            stack_ref[c, at, :] = spot.astype(f32).astype(bf16)
        factors = jnp.concatenate([toeplitz_ref[c], picked], axis=1).astype(bf16)
        parts.append(jnp.dot(factors, stack_ref[c], preferred_element_type=f32))
        mine_ref[pl.ds(c * z.span, z.span), :] = parts[c][:z.span]
    for s, ref in enumerate(out_refs, 1):
        ref[...] = jnp.concatenate(
            [part[s * z.span:(s + 1) * z.span] for part in parts], axis=0
        ).astype(bf16)


def unpack(z, left_ref, right_ref, uh_ref, vh_ref, mh_ref):
    size = z.layers
    for ref, at_u, at_v in ((right_ref, 0, 0), (left_ref, TAIL - 3, TAIL - 2)):
        for c in range(z.parts):
            for j in range(3):
                both = ref[pl.ds((c * 3 + j) * 2 * size, 2 * size), :].astype(f32)
                uh_ref[c, pl.ds((at_u + j) * size, size), :] = both[:size] + both[size:]
            both = ref[pl.ds(z.halo_v + c * 2 * size, 2 * size), :].astype(f32)
            vh_ref[c, pl.ds(at_v * size, 2 * size), :] = both
        mh_ref[pl.ds(at_v * size, 2 * size), :] = ref[pl.ds(z.halo_m, 2 * size), :].astype(f32)
    for c in range(z.parts):
        uh_ref[c, pl.ds(3 * size, 2 * size), :] = jnp.zeros((2 * size, z.dips), f32)
        vh_ref[c, pl.ds(2 * size, 4 * size), :] = jnp.zeros((4 * size, z.dips), f32)
    mh_ref[pl.ds(2 * size, 4 * size), :] = jnp.zeros((4 * size, z.dips), f32)


def corner_tiles(z, left_ref, right_ref, tile_ref):
    rows = pl.ds(z.corner, z.halo - z.corner)
    after, before = right_ref[rows, :].astype(f32), left_ref[rows, :].astype(f32)
    blank = jnp.zeros((TAIL, z.dips), f32)

    def tile(head, tail):
        return jnp.concatenate([head, blank[:TAIL - head.shape[0] - tail.shape[0]], tail], axis=0)

    for side in range(z.sides):
        for c in range(z.parts):
            at = 8 * (side * z.parts + c)
            a, b = after[at:at + 8], before[at:at + 8]
            head, tail = a[0:3] + a[3:6], b[0:3] + b[3:6]
            tile_ref[side, 3 * c] = tile(head[:2], tail[:2])
            tile_ref[side, 3 * c + 1] = tile(head[2:], tail[2:])
            tile_ref[side, 3 * c + 2] = blank
            tile_ref[side, 3 * z.parts + 2 * c] = tile(a[6:7], b[6:7])
            tile_ref[side, 3 * z.parts + 2 * c + 1] = blank
            if c == 0:
                tile_ref[side, 5 * z.parts] = tile(a[7:8], b[7:8])
                tile_ref[side, 5 * z.parts + 1] = blank


def in_plane(values, first_dip, last_dip):
    count, dips = values.shape
    around = pltpu.roll(values, 1, 0) + pltpu.roll(values, count - 1, 0)
    around += jnp.where(first_dip, 0.0, pltpu.roll(values, 1, 1))
    around += jnp.where(last_dip, 0.0, pltpu.roll(values, dips - 1, 1))
    return around - 6.0 * values


def base_kernel(z, u_ref, v_ref, s_ref, y_ref, c_ref, left_ref, right_ref, *rest):
    sides = rest[:z.sides]
    out_u, out_v, mf_ref, ch_ref, m_ref, uh_ref, vh_ref, mh_ref, tile_ref = rest[z.sides:]
    set_modulus(z, s_ref, y_ref, m_ref)
    unpack(z, left_ref, right_ref, uh_ref, vh_ref, mh_ref)
    corner_tiles(z, left_ref, right_ref, tile_ref)
    place = lax.axis_index("normal")
    is_high = place == z.normal - 1
    is_face = (is_high | (place == 0)).astype(f32)
    row = lax.broadcasted_iota(jnp.int32, (TAIL, z.dips), 0)
    before = left_ref[pl.ds(z.halo_c, 16), :].astype(f32)[16 - TAIL:]
    after = right_ref[pl.ds(z.halo_c, 16), :].astype(f32)[:TAIL]
    own = jnp.where(is_high, c_ref[1], c_ref[0]).astype(f32)
    tail = jnp.where(row < TAIL // 2, after, before)
    ch_ref[...] = jnp.concatenate([own, tail], axis=0) * is_face
    dip = lax.broadcasted_iota(jnp.int32, (z.span, z.dips), 1)
    first_dip, last_dip = dip == 0, dip == z.dips - 1
    low = -2 if z.sides == 2 else 0
    top = z.layers

    def fetch(kind, c, f):
        if 0 <= f < top:
            layer = layer_of(z, f)
            own = {"u": u_ref, "v": v_ref, "m": m_ref}[kind]
            first = 0 if kind == "m" else c * z.stride
            tail = mh_ref if kind == "m" else (uh_ref if kind == "u" else vh_ref).at[c]
            return jnp.concatenate(
                [
                    own[pl.ds(first + layer, z.nodes, stride=top), :],
                    tail[pl.ds(layer, TAIL, stride=top), :],
                ],
                axis=0,
            )
        side, j = (0, f - top) if f >= top else (1, -1 - f)
        at = {"u": 3 * c, "v": 3 * z.parts + 2 * c, "m": 5 * z.parts}[kind] + j
        return jnp.concatenate([sides[side][at], tile_ref[side, at]], axis=0)

    def one_part(c, unused):
        u = {f: fetch("u", c, f) for f in range(low - 1 if z.sides == 2 else 0, top + 3)}
        v = {f: fetch("v", c, f) for f in range(low, top + 2)}
        for step in range(SUB):
            levels = range(low + step if z.sides == 2 else 0, top + 2 - step)
            for f in levels:
                lap = in_plane(u[f], first_dip, last_dip) + u[f + 1]
                if f - 1 in u:
                    lap += u[f - 1]
                v[f] = v[f] + time_step * (fetch("m", c, f) * lap)
            u = {f: u[f] + time_step * v[f] for f in levels}
        for f in range(top):
            at = pl.ds(c * z.stride + layer_of(z, f), z.nodes, stride=z.layers)
            out_u[at, :] = u[f][:z.nodes]
            out_v[at, :] = v[f][:z.nodes]
        return unused

    lax.fori_loop(0, z.parts, one_part, 0)
    for f in range(3):
        mf_ref[f] = fetch("m", 0, f)


def final_kernel(z, mine_ref, contact_ref, m_ref, base_u, base_v, *rest):
    arrived, (out_u, out_v, u_ref, v_ref, sems) = rest[:-5], rest[-5:]
    dip = lax.broadcasted_iota(jnp.int32, (z.span, z.dips), 1)
    first_dip, last_dip = dip == 0, dip == z.dips - 1
    contact = contact_ref[...]
    m0, m1, m2 = m_ref[0], m_ref[1], m_ref[2]
    h = time_step
    arrived = [ref[...].astype(f32) for ref in arrived]
    copies = []
    for c in range(z.parts):
        force = mine_ref[pl.ds(c * z.span, z.span), :]
        for other in arrived:
            force = force + other[c * z.span:(c + 1) * z.span]
        force = force * contact
        v0 = h * force
        u0 = h * v0
        v1 = h * (m1 * u0)
        v0 = v0 + h * (m0 * in_plane(u0, first_dip, last_dip) + force)
        u0 = u0 + h * v0
        u1 = h * v1
        v2 = h * (m2 * u1)
        w0 = v0 + h * (m0 * (in_plane(u0, first_dip, last_dip) + u1) + force)
        v1 = v1 + h * (m1 * (in_plane(u1, first_dip, last_dip) + u0))
        pairs = ((u0 + h * w0, w0), (u1 + h * v1, v1), (h * v2, v2))
        part = pl.ds(c * z.stride, z.stride)
        for k, (base, sums, out) in enumerate(((base_u, u_ref, out_u), (base_v, v_ref, out_v))):
            sums[part, :] = base[part, :]
            for f in range(3):
                at = pl.ds(c * z.stride + layer_of(z, f), z.nodes, stride=z.layers)
                sums[at, :] = sums[at, :] + pairs[f][k][:z.nodes]
            copies.append(
                pltpu.make_async_copy(sums.at[part, :], out.at[part, :], sems.at[2 * c + k])
            )
            copies[-1].start()
    for copy in copies:
        copy.wait()


PARAMS = pltpu.CompilerParams(vmem_limit_bytes=32 * 2**20)
FIRST = pltpu.CompilerParams(vmem_limit_bytes=32 * 2**20)
HBM = pl.BlockSpec(memory_space=pltpu.HBM)


def in_hbm(*arrays):
    return [pltpu.with_memory_space_constraint(x, pltpu.HBM) for x in arrays]


def shape(dims, kind):
    return jax.ShapeDtypeStruct(dims, kind)


def body(mesh, displacement, velocity, stiffness, yield_flags, contact, history, kernel):
    z = Sizes(mesh, displacement, history)
    u = displacement.reshape(-1, z.dips)
    v = velocity.reshape(-1, z.dips)
    s = stiffness.reshape(-1, z.dips)
    y = yield_flags.reshape(-1, yield_flags.shape[2])
    dma = pltpu.SemaphoreType.DMA
    ring = lambda step: [(i, (i + step) % z.strike) for i in range(z.strike)]
    swap = lambda mask: [(i, i ^ mask) for i in range(z.strike)]

    edge = (5 * z.parts + 2, z.nodes, z.dips)
    common, response, *edges = pl.pallas_call(
        functools.partial(common_kernel, z),
        out_shape=(shape((z.common, LANES), bf16), shape((z.chunks, 8, LANES), f32))
        + (shape(edge, f32),) * z.sides,
        in_specs=[HBM] * 7,
        out_specs=(VMEM,) * (2 + z.sides),
        scratch_shapes=[
            pltpu.VMEM(u.shape, f32),
            pltpu.VMEM((z.lags - 1, 2, z.parts, z.rows, z.modes), bf16),
            pltpu.VMEM((z.parts, z.lags, z.modes), f32),
            pltpu.VMEM((2 * z.modes, z.modes // 4), bf16),
            pltpu.VMEM(v.shape, f32),
            pltpu.VMEM(s.shape, f32),
            pltpu.VMEM(y.shape, jnp.int32),
            pltpu.VMEM((z.chunk_rows, z.modes), f32),
            pltpu.VMEM((z.chunk_rows, z.modes), f32),
            dma((7,)),
        ],
        compiler_params=FIRST,
        name="plane_and_history",
    )(*in_hbm(u, history, kernel.transpose(0, 2, 1, 3), phase_quarter(z.modes), v, s, y))

    window = [common] + [lax.ppermute(common, "strike", swap(w)) for w in range(1, WIN)]

    if z.sides == 2:
        is_high = lax.axis_index("normal") == z.normal - 1
        above, below = edges
        steps = [(i, i + 1) for i in range(z.normal - 1)]
        from_below = lax.ppermute(above, "normal", steps)
        from_above = lax.ppermute(
            jnp.where(is_high, above, below), "normal", [(j, i) for i, j in steps]
        )
        beside = [
            jnp.where(is_high, from_below, from_above),
            jnp.where(is_high, from_above, from_below),
        ]
    else:
        beside = [lax.ppermute(edges[0], "normal", [(0, 1), (1, 0)])]

    to_right, to_left = pl.pallas_call(
        functools.partial(halo_kernel, z),
        out_shape=(shape((z.halo, LANES), bf16),) * 2,
        in_specs=[HBM] * 5 + [VMEM] * z.sides,
        out_specs=(VMEM,) * 2,
        scratch_shapes=[
            pltpu.VMEM((2, z.parts, 3, z.layers, z.dips), f32),
            pltpu.VMEM((2, z.parts, 2, z.layers, z.dips), f32),
            pltpu.VMEM((2, 2, z.layers, z.dips), f32),
            pltpu.VMEM(y.shape, jnp.int32),
            pltpu.VMEM(contact.shape[1:], jnp.int32),
            dma((8,)),
        ],
        compiler_params=PARAMS,
        name="strike_edges",
    )(displacement, velocity, stiffness, y, contact, *beside)
    from_left = lax.ppermute(to_right, "strike", ring(1))
    from_right = lax.ppermute(to_left, "strike", ring(-1))

    toeplitz = pl.pallas_call(
        functools.partial(toeplitz_kernel, z),
        out_shape=shape((z.parts, z.targets * z.span, LANES), f32),
        in_specs=[VMEM],
        out_specs=VMEM,
        scratch_shapes=[pltpu.VMEM((z.chunks, z.span, LANES), f32)],
        compiler_params=PARAMS,
        name="toeplitz",
    )(response)

    block = (z.parts * z.span, z.dips)
    mine, *parcels = pl.pallas_call(
        functools.partial(middle_kernel, z),
        out_shape=(shape(block, f32),) + (shape(block, bf16),) * (z.targets - 1),
        in_specs=[VMEM] * (1 + WIN),
        out_specs=(VMEM,) * z.targets,
        scratch_shapes=[pltpu.VMEM((z.parts, WIN * (z.nodes + z.chunk_rows), z.dips), bf16)],
        compiler_params=PARAMS,
        name="partial_tractions",
    )(toeplitz, *window)

    arrived = [
        lax.ppermute(p, "strike", swap(WIN * (k + 1))) for k, p in reversed(list(enumerate(parcels)))
    ]
    tail = (z.parts, TAIL * z.layers, z.dips)
    base_u, base_v, face_modulus, touching = pl.pallas_call(
        functools.partial(base_kernel, z),
        out_shape=(
            shape(u.shape, f32),
            shape(u.shape, f32),
            shape((3, z.span, z.dips), f32),
            shape((z.span, z.dips), f32),
        ),
        in_specs=[VMEM] * (7 + z.sides),
        out_specs=(VMEM,) * 4,
        scratch_shapes=[
            pltpu.VMEM(s.shape, f32),
            pltpu.VMEM(tail, f32),
            pltpu.VMEM(tail, f32),
            pltpu.VMEM(tail[1:], f32),
            pltpu.VMEM((z.sides, edge[0], TAIL, z.dips), f32),
        ],
        compiler_params=PARAMS,
        name="unloaded_substeps",
    )(u, v, s, y, contact, from_left, from_right, *beside)

    moved, speed = pl.pallas_call(
        functools.partial(final_kernel, z),
        out_shape=(shape(u.shape, f32),) * 2,
        in_specs=[VMEM] * (5 + len(arrived)),
        out_specs=(HBM,) * 2,
        scratch_shapes=[pltpu.VMEM(u.shape, f32), pltpu.VMEM(u.shape, f32), dma((2 * z.parts,))],
        compiler_params=PARAMS,
        name="add_force_response",
    )(mine, touching, face_modulus, base_u, base_v, *arrived)
    return (moved.reshape(displacement.shape), speed.reshape(displacement.shape))


def solution(mesh):
    return jax.shard_map(
        functools.partial(body, mesh),
        mesh=mesh,
        in_specs=(
            P(None, "strike", "normal", None),
            P(None, "strike", "normal", None),
            P("strike", "normal", None),
            P("strike", "normal", None),
            P(None, "strike", None),
            P(None, None, None, None, "strike", None),
            P(),
        ),
        out_specs=(P(None, "strike", "normal", None), P(None, "strike", "normal", None)),
        check_vma=False,
    )
```

```python
import functools
import math

import jax
import jax.numpy as jnp
import numpy as np
from jax import lax
from jax.experimental import pallas as pl
from jax.experimental.pallas import tpu as pltpu
from jax.sharding import PartitionSpec as P

SUB = 3
BLK = 4
WIN = 4
TAIL = 8
LANES = 128

time_step = 0.5

f32 = jnp.float32
bf16 = jnp.bfloat16
VMEM = pl.BlockSpec(memory_space=pltpu.VMEM)


def round_up(value, step):
    return -(-value // step) * step


def phase_quarter(mode_count):
    phase = np.outer(np.arange(mode_count), np.arange(mode_count // 4)) % mode_count
    phase = phase * (2.0 * np.pi / mode_count)
    return np.concatenate([np.cos(phase), -np.sin(phase)]).astype(np.float32).astype(bf16)


class Sizes:
    def __init__(self, mesh, displacement, history):
        self.strike = mesh.shape["strike"]
        self.normal = mesh.shape["normal"]
        self.parts, self.nodes, self.layers, self.dips = displacement.shape
        self.lags = history.shape[1]
        self.rows = history.shape[4]
        self.modes = history.shape[5]
        self.chunks = self.modes // LANES
        self.spectral = round_up(self.parts * self.rows, 8)
        self.chunk_rows = round_up(self.spectral + 2 * self.parts, 16)
        self.plane_rows = self.parts * self.nodes
        self.common = self.plane_rows + 2 * self.spectral
        self.halo_v = self.parts * 3 * 2 * self.layers
        self.halo_m = self.halo_v + self.parts * 2 * self.layers
        self.halo_c = self.halo_m + 2 * self.layers
        self.corner = self.halo_c + 16
        self.span = self.nodes + TAIL
        self.targets = self.strike // WIN
        self.stride = self.nodes * self.layers
        self.sides = 1 if self.normal == 2 else 2
        self.halo = self.corner + round_up(self.sides * self.parts * 8, 16)


def widen_flags(flags, dips):
    blocks = flags.shape[1]
    block_id = lax.broadcasted_iota(jnp.int32, (blocks, dips), 0)
    dip_id = lax.broadcasted_iota(jnp.int32, (blocks, dips), 1)
    spread = (dip_id // BLK == block_id).astype(bf16)
    wide = jnp.dot(flags.astype(f32).astype(bf16), spread, preferred_element_type=f32)
    return 1.0 - 0.5 * wide


def node_offset(rows):
    return jnp.where(rows < rows.shape[0] - TAIL // 2, rows, rows - rows.shape[0])


def layer_of(z, level):
    is_high = lax.axis_index("normal") == z.normal - 1
    return jnp.where(is_high, z.layers - 1 - level, level)


def beside_me(place):
    turn = place ^ (place >> 1)
    ahead, behind = (turn + 1) % WIN, (turn + WIN - 1) % WIN
    return (place, ahead ^ (ahead >> 1), behind ^ (behind >> 1), place ^ 3)


def start_all(pairs, sems):
    copies = [pltpu.make_async_copy(a, b, sems.at[i]) for i, (a, b) in enumerate(pairs)]
    for copy in copies:
        copy.start()
    return copies


def set_modulus(z, s_ref, y_ref, out_ref):
    soft = widen_flags(y_ref[...], z.dips)
    for n in range(z.nodes):
        at = n // BLK * z.layers
        rows = pl.ds(n * z.layers, z.layers)
        out_ref[rows, :] = s_ref[rows, :] * soft[at:at + z.layers]


def common_kernel(z, u_hbm, h_hbm, k_hbm, t_hbm, v_hbm, s_hbm, y_hbm, out_ref, g_ref, *rest):
    edges, others = rest[:z.sides], rest[z.sides:z.sides + z.targets - 1]
    u_ref, h_ref, k_ref, t_ref, v_ref, s_ref, y_ref, re_ref, im_ref, line_ref, sems = rest[-11:]
    is_high = lax.axis_index("normal") == z.normal - 1
    face = is_high.astype(jnp.int32)
    copies = start_all(
        [
            (h_hbm.at[face, pl.ds(0, z.lags - 1)], h_ref),
            (k_hbm.at[face], k_ref),
            (t_hbm, t_ref),
            (u_hbm, u_ref),
            (v_hbm, v_ref),
            (s_hbm, s_ref),
            (y_hbm, y_ref),
        ],
        sems,
    )
    re_ref[...] = jnp.zeros_like(re_ref)
    im_ref[...] = jnp.zeros_like(im_ref)
    copies[1].wait()
    copies[0].wait()
    for c in range(z.parts):
        for q, dst in ((0, re_ref), (1, im_ref)):
            total = None
            for lag in range(1, z.lags):
                term = k_ref[c, pl.ds(lag, 1), :] * h_ref[lag - 1, q, c].astype(f32)
                total = term if total is None else total + term
            dst[pl.ds(c * z.rows, z.rows), :] = total
        newest = k_ref[c, pl.ds(0, 1), :]
        high = newest.astype(bf16).astype(f32)
        re_ref[pl.ds(z.spectral + c, 1), :] = high
        re_ref[pl.ds(z.spectral + z.parts + c, 1), :] = newest - high
    re, im = re_ref[...], im_ref[...]
    quarter = lax.broadcasted_iota(jnp.int32, (1, z.modes), 1) % 4
    one = (quarter == 0).astype(f32) - (quarter == 2).astype(f32)
    two = (quarter == 1).astype(f32) - (quarter == 3).astype(f32)
    flip = 1.0 - 2.0 * (quarter % 2).astype(f32)
    turned = jnp.concatenate(
        [
            jnp.concatenate([re, im], axis=1),
            jnp.concatenate([re * one - im * two, re * two + im * one], axis=1),
            jnp.concatenate([re * flip, im * flip], axis=1),
            jnp.concatenate([re * one + im * two, im * one - re * two], axis=1),
        ],
        axis=0,
    ).astype(bf16)
    copies[2].wait()
    lines = jnp.dot(turned, t_ref[...], preferred_element_type=f32) * (1.0 / math.sqrt(z.modes))
    per_quarter = z.chunks // 4
    for m in range(4):
        for q in range(per_quarter):
            piece = lines[m * z.chunk_rows:(m + 1) * z.chunk_rows, q * LANES:(q + 1) * LANES]
            chunk = m * per_quarter + q
            line_ref[chunk] = piece[:z.spectral]
            g_ref[chunk] = piece[z.spectral:z.spectral + 8]
    group = lax.axis_index("strike") // WIN
    lane = lax.broadcasted_iota(jnp.int32, (z.spectral, LANES), 1)
    for s, ref in enumerate((out_ref,) + others):
        chunk = (group + s) % z.targets
        after, before = line_ref[(chunk + 1) % z.chunks], line_ref[(chunk + z.chunks - 1) % z.chunks]
        both = jnp.concatenate(
            [line_ref[chunk], jnp.where(lane < LANES // 2, after, before)], axis=0
        )
        ref[pl.ds(z.plane_rows, 2 * z.spectral), :] = both.astype(bf16)
    copies[3].wait()
    layer = face * (z.layers - 1)
    for c in range(z.parts):
        plane = u_ref[pl.ds(c * z.stride + layer, z.nodes, stride=z.layers), :].astype(bf16)
        for ref in (out_ref,) + others:
            ref[pl.ds(c * z.nodes, z.nodes), :] = plane
    for copy in copies[4:]:
        copy.wait()
    set_modulus(z, s_ref, y_ref, s_ref)
    size = z.layers
    for out, levels in zip(edges, ((size - 1, size - 2, size - 3), (0, 1, 2))):
        for j, f in enumerate(levels):
            layer = layer_of(z, f)
            for c in range(z.parts):
                at = pl.ds(c * z.stride + layer, z.nodes, stride=size)
                out[3 * c + j] = u_ref[at, :]
                if j < 2:
                    out[3 * z.parts + 2 * c + j] = v_ref[at, :]
            if j < 2:
                out[5 * z.parts + j] = s_ref[pl.ds(layer, z.nodes, stride=size), :]


def toeplitz_factors(z, g_ref, out_ref, turned_ref):
    me = lax.axis_index("strike")
    place, group = me % WIN, me // WIN
    lane = lax.broadcasted_iota(jnp.int32, (z.span, LANES), 1)
    for c in range(z.parts):
        line = jnp.concatenate(
            [
                g_ref[j, pl.ds(c, 1), :] + g_ref[j, pl.ds(z.parts + c, 1), :]
                for j in range(z.chunks)
            ],
            axis=1,
        ) * (1.0 / math.sqrt(z.modes))
        wide = jnp.broadcast_to(line, (z.span, z.modes))
        wide = pltpu.roll(wide, 0, 1, stride=1, stride_axis=0)
        last = jnp.broadcast_to(line, (TAIL, z.modes))
        last = pltpu.roll(last, z.modes - TAIL, 1, stride=1, stride_axis=0)
        row = lax.broadcasted_iota(jnp.int32, (TAIL, z.modes), 0)
        last = jnp.where(row < TAIL // 2, wide[z.nodes:], last)
        wide = jnp.concatenate([wide[:z.nodes], last], axis=0)
        for j in range(z.chunks):
            piece = wide[:, j * LANES:(j + 1) * LANES]
            for r in range(WIN):
                turned_ref[c, j, r] = pltpu.roll(piece, r * z.nodes, 1) if r else piece
        for w in range(WIN):
            ahead = beside_me(place)[w] - place + WIN * group
            for q in range(z.chunks // WIN):
                tile = None
                for k in range(WIN):
                    at = (WIN * (q * WIN + k) - ahead + 2 * z.strike) % z.strike
                    piece = turned_ref[c, at // WIN, (k - at % WIN + WIN) % WIN]
                    tile = piece if k == 0 else jnp.where(lane < k * z.nodes, tile, piece)
                out_ref[c, pl.ds(w * z.span, z.span), q * LANES:(q + 1) * LANES] = tile


def halo_kernel(z, u_ref, v_ref, s_ref, y_ref, c_ref, g_ref, *rest):
    beside = rest[:z.sides]
    pair_ref, cross_ref, toeplitz_ref, turned_ref = rest[z.sides:]
    toeplitz_factors(z, g_ref, toeplitz_ref, turned_ref)
    is_high = lax.axis_index("normal") == z.normal - 1
    is_even = lax.axis_index("strike") % 2 == 0
    soft = widen_flags(y_ref[...], z.dips)
    for ref, is_end in ((pair_ref, is_even), (cross_ref, jnp.logical_not(is_even))):
        first = jnp.where(is_end, z.nodes - 3, 0)
        near = jnp.where(is_end, z.nodes - 2, 0)
        for c in range(z.parts):
            for j in range(3):
                tile = u_ref[c, first + j]
                high = tile.astype(bf16).astype(f32)
                both = jnp.concatenate([high, tile - high], axis=0).astype(bf16)
                ref[pl.ds((c * 3 + j) * 2 * z.layers, 2 * z.layers), :] = both
            both = jnp.concatenate([v_ref[c, near], v_ref[c, near + 1]], axis=0).astype(bf16)
            ref[pl.ds(z.halo_v + c * 2 * z.layers, 2 * z.layers), :] = both
        part = jnp.where(is_end, soft[soft.shape[0] - z.layers:], soft[:z.layers])
        both = jnp.concatenate([s_ref[near] * part, s_ref[near + 1] * part], axis=0)
        ref[pl.ds(z.halo_m, 2 * z.layers), :] = both.astype(bf16)
        own = jnp.where(is_high, c_ref[1], c_ref[0])
        touch = jnp.where(is_end, own[z.nodes - 16:], own[:16])
        ref[pl.ds(z.halo_c, 16), :] = touch.astype(f32).astype(bf16)

        def rows_of(edge, k, count):
            head = edge[k, pl.ds(0, count), :]
            return jnp.where(is_end, edge[k, pl.ds(z.nodes - count, count), :], head)

        pieces = []
        for edge in beside:
            for c in range(z.parts):
                some = jnp.concatenate(
                    [rows_of(edge, 3 * c, 2), rows_of(edge, 3 * c + 1, 1)], axis=0
                )
                high = some.astype(bf16).astype(f32)
                speed = rows_of(edge, 3 * z.parts + 2 * c, 1)
                pieces += [high, some - high, speed, rows_of(edge, 5 * z.parts, 1)]
        spare = z.halo - z.corner - 8 * z.sides * z.parts
        if spare:
            pieces.append(jnp.zeros((spare, z.dips), f32))
        ref[pl.ds(z.corner, z.halo - z.corner), :] = jnp.concatenate(pieces, axis=0).astype(bf16)


def middle_kernel(z, toeplitz_ref, *rest):
    window = (rest[z.targets - 1],) + rest[:z.targets - 1]
    mine_ref = rest[z.targets]
    out_refs, stack_ref = rest[z.targets + 1:-1], rest[-1]
    me = lax.axis_index("strike")
    place, group = me % WIN, me // WIN
    spare = jnp.zeros((z.chunk_rows - z.spectral, 2 * LANES), f32)
    lines = []
    for ref in window:
        both = ref[pl.ds(z.plane_rows, 2 * z.spectral), :].astype(f32)
        lines += [jnp.concatenate([both[:z.spectral], both[z.spectral:]], axis=1), spare]
    offset = node_offset(lax.broadcasted_iota(jnp.int32, (z.span, 2 * LANES), 0))
    lane = lax.broadcasted_iota(jnp.int32, (z.span, 2 * LANES), 1)
    wanted = []
    for w in range(WIN):
        node = beside_me(place)[w] * z.nodes + offset
        node = jnp.where(node < 0, node + 2 * LANES, node)
        wanted.append((lane == node).astype(f32))
    picked = lax.dot_general(
        jnp.concatenate(wanted, axis=0).astype(bf16),
        jnp.concatenate(lines, axis=0).astype(bf16),
        (((1,), (1,)), ((), ())),
        preferred_element_type=f32,
    )
    row = lax.broadcasted_iota(jnp.int32, (z.chunk_rows, z.dips), 0)
    ahead = lax.broadcasted_iota(jnp.int32, (z.chunk_rows, z.dips), 1) - row
    own_rows = z.targets * z.nodes
    parts = []
    for c in range(z.parts):
        inside = (row >= c * z.rows) & (row < (c + 1) * z.rows)
        for s, ref in enumerate(window):
            source = (group + z.targets - s) % z.targets
            at = pl.multiple_of(source * z.nodes, z.nodes)
            stack_ref[c, pl.ds(at, z.nodes), :] = ref[pl.ds(c * z.nodes, z.nodes), :]
            spot = inside & (ahead == z.rows * (WIN * source + place) - c * z.rows)
            at = pl.ds(own_rows + s * z.chunk_rows, z.chunk_rows)
            stack_ref[c, at, :] = spot.astype(f32).astype(bf16)
        factors = jnp.concatenate([toeplitz_ref[c], picked], axis=1).astype(bf16)
        parts.append(jnp.dot(factors, stack_ref[c], preferred_element_type=f32))
        mine_ref[pl.ds(c * z.span, z.span), :] = parts[c][:z.span]
    for w, ref in enumerate(out_refs, 1):
        ref[...] = jnp.concatenate(
            [part[w * z.span:(w + 1) * z.span] for part in parts], axis=0
        ).astype(bf16)


def unpack(z, left_ref, right_ref, uh_ref, vh_ref, mh_ref):
    size = z.layers
    for ref, at_u, at_v in ((right_ref, 0, 0), (left_ref, TAIL - 3, TAIL - 2)):
        for c in range(z.parts):
            for j in range(3):
                both = ref[pl.ds((c * 3 + j) * 2 * size, 2 * size), :].astype(f32)
                uh_ref[c, pl.ds((at_u + j) * size, size), :] = both[:size] + both[size:]
            both = ref[pl.ds(z.halo_v + c * 2 * size, 2 * size), :].astype(f32)
            vh_ref[c, pl.ds(at_v * size, 2 * size), :] = both
        mh_ref[pl.ds(at_v * size, 2 * size), :] = ref[pl.ds(z.halo_m, 2 * size), :].astype(f32)
    for c in range(z.parts):
        uh_ref[c, pl.ds(3 * size, 2 * size), :] = jnp.zeros((2 * size, z.dips), f32)
        vh_ref[c, pl.ds(2 * size, 4 * size), :] = jnp.zeros((4 * size, z.dips), f32)
    mh_ref[pl.ds(2 * size, 4 * size), :] = jnp.zeros((4 * size, z.dips), f32)


def corner_tiles(z, left_ref, right_ref, tile_ref):
    rows = pl.ds(z.corner, z.halo - z.corner)
    after, before = right_ref[rows, :].astype(f32), left_ref[rows, :].astype(f32)
    blank = jnp.zeros((TAIL, z.dips), f32)

    def tile(head, tail):
        return jnp.concatenate([head, blank[:TAIL - head.shape[0] - tail.shape[0]], tail], axis=0)

    for side in range(z.sides):
        for c in range(z.parts):
            at = 8 * (side * z.parts + c)
            a, b = after[at:at + 8], before[at:at + 8]
            head, tail = a[0:3] + a[3:6], b[0:3] + b[3:6]
            tile_ref[side, 3 * c] = tile(head[:2], tail[:2])
            tile_ref[side, 3 * c + 1] = tile(head[2:], tail[2:])
            tile_ref[side, 3 * c + 2] = blank
            tile_ref[side, 3 * z.parts + 2 * c] = tile(a[6:7], b[6:7])
            tile_ref[side, 3 * z.parts + 2 * c + 1] = blank
            if c == 0:
                tile_ref[side, 5 * z.parts] = tile(a[7:8], b[7:8])
                tile_ref[side, 5 * z.parts + 1] = blank


def in_plane(values, first_dip, last_dip):
    count, dips = values.shape
    around = pltpu.roll(values, 1, 0) + pltpu.roll(values, count - 1, 0)
    around += jnp.where(first_dip, 0.0, pltpu.roll(values, 1, 1))
    around += jnp.where(last_dip, 0.0, pltpu.roll(values, dips - 1, 1))
    return around - 6.0 * values


def base_kernel(z, u_ref, v_ref, s_ref, y_ref, c_ref, cross_ref, pair_ref, *rest):
    sides = rest[:z.sides]
    out_u, out_v, mf_ref, ch_ref, m_ref, uh_ref, vh_ref, mh_ref, tile_ref = rest[z.sides:]
    set_modulus(z, s_ref, y_ref, m_ref)
    place = lax.axis_index("normal")
    is_high = place == z.normal - 1
    is_face = (is_high | (place == 0)).astype(f32)
    ch_ref[pl.ds(0, z.nodes), :] = jnp.where(is_high, c_ref[1], c_ref[0]).astype(f32) * is_face

    def receive(left_ref, right_ref):
        unpack(z, left_ref, right_ref, uh_ref, vh_ref, mh_ref)
        corner_tiles(z, left_ref, right_ref, tile_ref)
        row = lax.broadcasted_iota(jnp.int32, (TAIL, z.dips), 0)
        before = left_ref[pl.ds(z.halo_c, 16), :].astype(f32)[16 - TAIL:]
        after = right_ref[pl.ds(z.halo_c, 16), :].astype(f32)[:TAIL]
        ch_ref[pl.ds(z.nodes, TAIL), :] = jnp.where(row < TAIL // 2, after, before) * is_face

    is_even = lax.axis_index("strike") % 2 == 0

    @pl.when(is_even)
    def _():
        receive(cross_ref, pair_ref)

    @pl.when(jnp.logical_not(is_even))
    def _():
        receive(pair_ref, cross_ref)

    dip = lax.broadcasted_iota(jnp.int32, (z.span, z.dips), 1)
    first_dip, last_dip = dip == 0, dip == z.dips - 1
    low = -2 if z.sides == 2 else 0
    top = z.layers

    def fetch(kind, c, f):
        if 0 <= f < top:
            layer = layer_of(z, f)
            own = {"u": u_ref, "v": v_ref, "m": m_ref}[kind]
            first = 0 if kind == "m" else c * z.stride
            tail = mh_ref if kind == "m" else (uh_ref if kind == "u" else vh_ref).at[c]
            return jnp.concatenate(
                [
                    own[pl.ds(first + layer, z.nodes, stride=top), :],
                    tail[pl.ds(layer, TAIL, stride=top), :],
                ],
                axis=0,
            )
        side, j = (0, f - top) if f >= top else (1, -1 - f)
        at = {"u": 3 * c, "v": 3 * z.parts + 2 * c, "m": 5 * z.parts}[kind] + j
        return jnp.concatenate([sides[side][at], tile_ref[side, at]], axis=0)

    def one_part(c, unused):
        u = {f: fetch("u", c, f) for f in range(low - 1 if z.sides == 2 else 0, top + 3)}
        v = {f: fetch("v", c, f) for f in range(low, top + 2)}
        for step in range(SUB):
            levels = range(low + step if z.sides == 2 else 0, top + 2 - step)
            for f in levels:
                lap = in_plane(u[f], first_dip, last_dip) + u[f + 1]
                if f - 1 in u:
                    lap += u[f - 1]
                v[f] = v[f] + time_step * (fetch("m", c, f) * lap)
            u = {f: u[f] + time_step * v[f] for f in levels}
        for f in range(top):
            at = pl.ds(c * z.stride + layer_of(z, f), z.nodes, stride=z.layers)
            out_u[at, :] = u[f][:z.nodes]
            out_v[at, :] = v[f][:z.nodes]
        return unused

    lax.fori_loop(0, z.parts, one_part, 0)
    for f in range(3):
        mf_ref[f] = fetch("m", 0, f)


def final_kernel(z, mine_ref, contact_ref, m_ref, base_u, base_v, *rest):
    arrived, (out_u, out_v, u_ref, v_ref, sems) = rest[:-5], rest[-5:]
    dip = lax.broadcasted_iota(jnp.int32, (z.span, z.dips), 1)
    first_dip, last_dip = dip == 0, dip == z.dips - 1
    contact = contact_ref[...]
    m0, m1, m2 = m_ref[0], m_ref[1], m_ref[2]
    h = time_step
    arrived = [ref[...].astype(f32) for ref in arrived]
    copies = []
    for c in range(z.parts):
        force = mine_ref[pl.ds(c * z.span, z.span), :]
        for other in arrived:
            force = force + other[c * z.span:(c + 1) * z.span]
        force = force * contact
        v0 = h * force
        u0 = h * v0
        v1 = h * (m1 * u0)
        v0 = v0 + h * (m0 * in_plane(u0, first_dip, last_dip) + force)
        u0 = u0 + h * v0
        u1 = h * v1
        v2 = h * (m2 * u1)
        w0 = v0 + h * (m0 * (in_plane(u0, first_dip, last_dip) + u1) + force)
        v1 = v1 + h * (m1 * (in_plane(u1, first_dip, last_dip) + u0))
        pairs = ((u0 + h * w0, w0), (u1 + h * v1, v1), (h * v2, v2))
        part = pl.ds(c * z.stride, z.stride)
        for k, (base, sums, out) in enumerate(((base_u, u_ref, out_u), (base_v, v_ref, out_v))):
            sums[part, :] = base[part, :]
            for f in range(3):
                at = pl.ds(c * z.stride + layer_of(z, f), z.nodes, stride=z.layers)
                sums[at, :] = sums[at, :] + pairs[f][k][:z.nodes]
            copies.append(
                pltpu.make_async_copy(sums.at[part, :], out.at[part, :], sems.at[2 * c + k])
            )
            copies[-1].start()
    for copy in copies:
        copy.wait()


PARAMS = pltpu.CompilerParams(vmem_limit_bytes=32 * 2**20)
FIRST = pltpu.CompilerParams(vmem_limit_bytes=32 * 2**20)
HBM = pl.BlockSpec(memory_space=pltpu.HBM)


def in_hbm(*arrays):
    return [pltpu.with_memory_space_constraint(x, pltpu.HBM) for x in arrays]


def shape(dims, kind):
    return jax.ShapeDtypeStruct(dims, kind)


def body(mesh, displacement, velocity, stiffness, yield_flags, contact, history, kernel):
    z = Sizes(mesh, displacement, history)
    u = displacement.reshape(-1, z.dips)
    v = velocity.reshape(-1, z.dips)
    s = stiffness.reshape(-1, z.dips)
    y = yield_flags.reshape(-1, yield_flags.shape[2])
    dma = pltpu.SemaphoreType.DMA
    ring = lambda step: [(i, (i + step) % z.strike) for i in range(z.strike)]
    around = lambda w: [(i, i - i % WIN + beside_me(i % WIN)[w]) for i in range(z.strike)]

    edge = (5 * z.parts + 2, z.nodes, z.dips)
    common, response, *edges_and_others = pl.pallas_call(
        functools.partial(common_kernel, z),
        out_shape=(shape((z.common, LANES), bf16), shape((z.chunks, 8, LANES), f32))
        + (shape(edge, f32),) * z.sides
        + (shape((z.common, LANES), bf16),) * (z.targets - 1),
        in_specs=[HBM] * 7,
        out_specs=(VMEM,) * (1 + z.sides + z.targets),
        scratch_shapes=[
            pltpu.VMEM(u.shape, f32),
            pltpu.VMEM((z.lags - 1, 2, z.parts, z.rows, z.modes), bf16),
            pltpu.VMEM((z.parts, z.lags, z.modes), f32),
            pltpu.VMEM((2 * z.modes, z.modes // 4), bf16),
            pltpu.VMEM(v.shape, f32),
            pltpu.VMEM(s.shape, f32),
            pltpu.VMEM(y.shape, jnp.int32),
            pltpu.VMEM((z.chunk_rows, z.modes), f32),
            pltpu.VMEM((z.chunk_rows, z.modes), f32),
            pltpu.VMEM((z.chunks, z.spectral, LANES), f32),
            dma((7,)),
        ],
        compiler_params=FIRST,
        name="plane_and_history",
    )(*in_hbm(u, history, kernel.transpose(0, 2, 1, 3), phase_quarter(z.modes), v, s, y))

    edges, others = edges_and_others[:z.sides], edges_and_others[z.sides:]
    window = [common] + [
        lax.ppermute(other, "strike", ring(WIN * s)) for s, other in enumerate(others, 1)
    ]

    if z.sides == 2:
        is_high = lax.axis_index("normal") == z.normal - 1
        above, below = edges
        steps = [(i, i + 1) for i in range(z.normal - 1)]
        from_below = lax.ppermute(above, "normal", steps)
        from_above = lax.ppermute(
            jnp.where(is_high, above, below), "normal", [(j, i) for i, j in steps]
        )
        beside = [
            jnp.where(is_high, from_below, from_above),
            jnp.where(is_high, from_above, from_below),
        ]
    else:
        beside = [lax.ppermute(edges[0], "normal", [(0, 1), (1, 0)])]

    to_pair, to_cross, toeplitz = pl.pallas_call(
        functools.partial(halo_kernel, z),
        out_shape=(shape((z.halo, LANES), bf16),) * 2
        + (shape((z.parts, WIN * z.span, z.targets * z.nodes), f32),),
        in_specs=[VMEM] * (6 + z.sides),
        out_specs=(VMEM,) * 3,
        scratch_shapes=[pltpu.VMEM((z.parts, z.chunks, WIN, z.span, LANES), f32)],
        compiler_params=PARAMS,
        name="strike_edges_and_toeplitz",
    )(displacement, velocity, stiffness, y, contact, response, *beside)
    from_pair = lax.ppermute(to_pair, "strike", [(i, i ^ 1) for i in range(z.strike)])
    from_cross = lax.ppermute(
        to_cross, "strike", [(i, (i - 1 + i % 2 * 2) % z.strike) for i in range(z.strike)]
    )

    block = (z.parts * z.span, z.dips)
    mine, *parcels = pl.pallas_call(
        functools.partial(middle_kernel, z),
        out_shape=(shape(block, f32),) + (shape(block, bf16),) * (WIN - 1),
        in_specs=[VMEM] * (1 + z.targets),
        out_specs=(VMEM,) * WIN,
        scratch_shapes=[pltpu.VMEM((z.parts, z.targets * (z.nodes + z.chunk_rows), z.dips), bf16)],
        compiler_params=PARAMS,
        name="partial_tractions",
    )(toeplitz, *window[1:], common)

    arrived = [
        lax.ppermute(parcels[w - 1], "strike", around(w)) for w in (3, 1, 2)
    ]
    tail = (z.parts, TAIL * z.layers, z.dips)
    base_u, base_v, face_modulus, touching = pl.pallas_call(
        functools.partial(base_kernel, z),
        out_shape=(
            shape(u.shape, f32),
            shape(u.shape, f32),
            shape((3, z.span, z.dips), f32),
            shape((z.span, z.dips), f32),
        ),
        in_specs=[VMEM] * (7 + z.sides),
        out_specs=(VMEM,) * 4,
        scratch_shapes=[
            pltpu.VMEM(s.shape, f32),
            pltpu.VMEM(tail, f32),
            pltpu.VMEM(tail, f32),
            pltpu.VMEM(tail[1:], f32),
            pltpu.VMEM((z.sides, edge[0], TAIL, z.dips), f32),
        ],
        compiler_params=PARAMS,
        name="unloaded_substeps",
    )(u, v, s, y, contact, from_cross, from_pair, *beside)

    moved, speed = pl.pallas_call(
        functools.partial(final_kernel, z),
        out_shape=(shape(u.shape, f32),) * 2,
        in_specs=[VMEM] * (5 + len(arrived)),
        out_specs=(HBM,) * 2,
        scratch_shapes=[pltpu.VMEM(u.shape, f32), pltpu.VMEM(u.shape, f32), dma((2 * z.parts,))],
        compiler_params=PARAMS,
        name="add_force_response",
    )(mine, touching, face_modulus, base_u, base_v, *arrived)
    return (moved.reshape(displacement.shape), speed.reshape(displacement.shape))


def solution(mesh):
    return jax.shard_map(
        functools.partial(body, mesh),
        mesh=mesh,
        in_specs=(
            P(None, "strike", "normal", None),
            P(None, "strike", "normal", None),
            P("strike", "normal", None),
            P("strike", "normal", None),
            P(None, "strike", None),
            P(None, None, None, None, "strike", None),
            P(),
        ),
        out_specs=(P(None, "strike", "normal", None), P(None, "strike", "normal", None)),
        check_vma=False,
    )
```

```python
import functools
import math

import jax
import jax.numpy as jnp
import numpy as np
from jax import lax
from jax.experimental import pallas as pl
from jax.experimental.pallas import tpu as pltpu
from jax.sharding import PartitionSpec as P

SUB = 3
BLK = 4
WIN = 4
TAIL = 8
LANES = 128

time_step = 0.5

f32 = jnp.float32
bf16 = jnp.bfloat16
VMEM = pl.BlockSpec(memory_space=pltpu.VMEM)


def round_up(value, step):
    return -(-value // step) * step


def phase_quarter(mode_count):
    phase = np.outer(np.arange(mode_count), np.arange(mode_count // 4)) % mode_count
    phase = phase * (2.0 * np.pi / mode_count)
    return np.concatenate([np.cos(phase), -np.sin(phase)]).astype(np.float32).astype(bf16)


class Sizes:
    def __init__(self, mesh, displacement, history):
        self.strike = mesh.shape["strike"]
        self.normal = mesh.shape["normal"]
        self.parts, self.nodes, self.layers, self.dips = displacement.shape
        self.lags = history.shape[1]
        self.rows = history.shape[4]
        self.modes = history.shape[5]
        self.chunks = self.modes // LANES
        self.spectral = round_up(self.parts * self.rows, 8)
        self.chunk_rows = round_up(self.spectral + 2 * self.parts, 16)
        self.plane_rows = self.parts * self.nodes
        self.common = self.plane_rows + 2 * self.spectral
        self.halo_v = self.parts * 4 * self.layers
        self.halo_m = self.halo_v + self.parts * 2 * self.layers
        self.corner = self.halo_m + 2 * self.layers
        self.span = self.nodes + TAIL
        self.targets = self.strike // WIN
        self.stride = self.nodes * self.layers
        self.sides = 1 if self.normal == 2 else 2
        self.touch = self.sides * self.parts * 8
        self.halo = self.corner + round_up(self.touch + TAIL, 16)


def widen_flags(flags, dips):
    blocks = flags.shape[1]
    block_id = lax.broadcasted_iota(jnp.int32, (blocks, dips), 0)
    dip_id = lax.broadcasted_iota(jnp.int32, (blocks, dips), 1)
    spread = (dip_id // BLK == block_id).astype(bf16)
    wide = jnp.dot(flags.astype(f32).astype(bf16), spread, preferred_element_type=f32)
    return 1.0 - 0.5 * wide


def node_offset(rows):
    return jnp.where(rows < rows.shape[0] - TAIL // 2, rows, rows - rows.shape[0])


def layer_of(z, level):
    is_high = lax.axis_index("normal") == z.normal - 1
    return jnp.where(is_high, z.layers - 1 - level, level)


def beside_me(place):
    turn = place ^ (place >> 1)
    ahead, behind = (turn + 1) % WIN, (turn + WIN - 1) % WIN
    return (place, ahead ^ (ahead >> 1), behind ^ (behind >> 1), place ^ 3)


def start_all(pairs, sems):
    copies = [pltpu.make_async_copy(a, b, sems.at[i]) for i, (a, b) in enumerate(pairs)]
    for copy in copies:
        copy.start()
    return copies


def set_modulus(z, s_ref, y_ref, out_ref):
    soft = widen_flags(y_ref[...], z.dips)
    for n in range(z.nodes):
        at = n // BLK * z.layers
        rows = pl.ds(n * z.layers, z.layers)
        out_ref[rows, :] = s_ref[rows, :] * soft[at:at + z.layers]


def selections(z, wanted_ref, spots_ref):
    me = lax.axis_index("strike")
    place, group = me % WIN, me // WIN
    offset = node_offset(lax.broadcasted_iota(jnp.int32, (z.span, 2 * LANES), 0))
    lane = lax.broadcasted_iota(jnp.int32, (z.span, 2 * LANES), 1)
    wanted = []
    for t in range(WIN):
        node = t * z.nodes + offset
        node = jnp.where(node < 0, node + 2 * LANES, node)
        wanted.append((lane == node).astype(f32))
    wanted_ref[...] = jnp.concatenate(wanted, axis=0).astype(bf16)
    row = lax.broadcasted_iota(jnp.int32, (z.chunk_rows, z.dips), 0)
    ahead = lax.broadcasted_iota(jnp.int32, (z.chunk_rows, z.dips), 1) - row
    for c in range(z.parts):
        inside = (row >= c * z.rows) & (row < (c + 1) * z.rows)
        for s in range(z.targets):
            source = (group + z.targets - s) % z.targets
            spot = inside & (ahead == z.rows * (WIN * source + place) - c * z.rows)
            spots_ref[c, pl.ds(s * z.chunk_rows, z.chunk_rows), :] = spot.astype(f32).astype(bf16)


def common_kernel(z, u_hbm, h_hbm, k_hbm, t_hbm, v_hbm, s_hbm, y_hbm, out_ref, g_ref, m_ref, wanted_ref, spots_ref, *rest):
    edges, others = rest[:z.sides], rest[z.sides:z.sides + z.targets - 1]
    u_ref, h_ref, k_ref, t_ref, v_ref, s_ref, y_ref, re_ref, im_ref, line_ref, sems = rest[-11:]
    is_high = lax.axis_index("normal") == z.normal - 1
    face = is_high.astype(jnp.int32)
    copies = start_all(
        [
            (h_hbm.at[face, pl.ds(0, z.lags - 1)], h_ref),
            (k_hbm.at[face], k_ref),
            (t_hbm, t_ref),
            (u_hbm, u_ref),
            (v_hbm, v_ref),
            (s_hbm, s_ref),
            (y_hbm, y_ref),
        ],
        sems,
    )
    selections(z, wanted_ref, spots_ref)
    re_ref[...] = jnp.zeros_like(re_ref)
    im_ref[...] = jnp.zeros_like(im_ref)
    copies[1].wait()
    copies[0].wait()
    for c in range(z.parts):
        for q, dst in ((0, re_ref), (1, im_ref)):
            total = None
            for lag in range(1, z.lags):
                term = k_ref[c, pl.ds(lag, 1), :] * h_ref[lag - 1, q, c].astype(f32)
                total = term if total is None else total + term
            dst[pl.ds(c * z.rows, z.rows), :] = total
        newest = k_ref[c, pl.ds(0, 1), :]
        high = newest.astype(bf16).astype(f32)
        re_ref[pl.ds(z.spectral + c, 1), :] = high
        re_ref[pl.ds(z.spectral + z.parts + c, 1), :] = newest - high
    re, im = re_ref[...], im_ref[...]
    quarter = lax.broadcasted_iota(jnp.int32, (1, z.modes), 1) % 4
    one = (quarter == 0).astype(f32) - (quarter == 2).astype(f32)
    two = (quarter == 1).astype(f32) - (quarter == 3).astype(f32)
    flip = 1.0 - 2.0 * (quarter % 2).astype(f32)
    turned = jnp.concatenate(
        [
            jnp.concatenate([re, im], axis=1),
            jnp.concatenate([re * one - im * two, re * two + im * one], axis=1),
            jnp.concatenate([re * flip, im * flip], axis=1),
            jnp.concatenate([re * one + im * two, im * one - re * two], axis=1),
        ],
        axis=0,
    ).astype(bf16)
    copies[2].wait()
    lines = jnp.dot(turned, t_ref[...], preferred_element_type=f32) * (1.0 / math.sqrt(z.modes))
    per_quarter = z.chunks // 4
    for m in range(4):
        for q in range(per_quarter):
            piece = lines[m * z.chunk_rows:(m + 1) * z.chunk_rows, q * LANES:(q + 1) * LANES]
            chunk = m * per_quarter + q
            line_ref[chunk] = piece[:z.spectral]
            g_ref[chunk] = piece[z.spectral:z.spectral + 8]
    group = lax.axis_index("strike") // WIN
    lane = lax.broadcasted_iota(jnp.int32, (z.spectral, LANES), 1)
    for s, ref in enumerate((out_ref,) + others):
        chunk = (group + s) % z.targets
        after, before = line_ref[(chunk + 1) % z.chunks], line_ref[(chunk + z.chunks - 1) % z.chunks]
        both = jnp.concatenate(
            [line_ref[chunk], jnp.where(lane < LANES // 2, after, before)], axis=0
        )
        ref[pl.ds(z.plane_rows, 2 * z.spectral), :] = both.astype(bf16)
    copies[3].wait()
    layer = face * (z.layers - 1)
    for c in range(z.parts):
        plane = u_ref[pl.ds(c * z.stride + layer, z.nodes, stride=z.layers), :].astype(bf16)
        for ref in (out_ref,) + others:
            ref[pl.ds(c * z.nodes, z.nodes), :] = plane
    for copy in copies[4:]:
        copy.wait()
    set_modulus(z, s_ref, y_ref, m_ref)
    size = z.layers
    for out, levels in zip(edges, ((size - 1, size - 2, size - 3), (0, 1, 2))):
        for j, f in enumerate(levels):
            layer = layer_of(z, f)
            for c in range(z.parts):
                at = pl.ds(c * z.stride + layer, z.nodes, stride=size)
                out[3 * c + j] = u_ref[at, :]
                if j < 2:
                    out[3 * z.parts + 2 * c + j] = v_ref[at, :]
            if j < 2:
                out[5 * z.parts + j] = m_ref[pl.ds(layer, z.nodes, stride=size), :]


def toeplitz_factors(z, g_ref, out_ref):
    me = lax.axis_index("strike")
    place, group = me % WIN, me // WIN
    lane = lax.broadcasted_iota(jnp.int32, (8, LANES), 1)
    row = lax.broadcasted_iota(jnp.int32, (8, LANES), 0)
    stack = []
    for c in range(z.parts):
        line = jnp.concatenate(
            [
                g_ref[j, pl.ds(c, 1), :] + g_ref[j, pl.ds(z.parts + c, 1), :]
                for j in range(z.chunks)
            ],
            axis=1,
        ) * (1.0 / math.sqrt(z.modes))
        stack.append(jnp.broadcast_to(line, (8, z.modes)))
    wide = pltpu.roll(jnp.concatenate(stack, axis=0), 0, 1, stride=1, stride_axis=0)
    wide = pltpu.roll(wide, (group * LANES - place * z.nodes + z.modes) % z.modes, 1)
    for c in range(z.parts):
        columns = [wide[8 * c:8 * c + 8, j * LANES:(j + 1) * LANES] for j in range(z.chunks)]

        turned = {}

        def turn(j, shift):
            key = (j % z.chunks, shift % LANES)
            if key not in turned:
                piece = columns[key[0]]
                turned[key] = pltpu.roll(piece, key[1], 1) if key[1] else piece
            return turned[key]

        def eight_rows(shift, q):
            whole, rest = divmod((shift - 8 * c) % z.modes, LANES)
            tile = None
            for k in range(WIN):
                j = q * WIN + k - whole
                first = k * z.nodes
                if rest == 0:
                    piece = turn(j, first)
                elif rest >= z.nodes:
                    piece = turn(j - 1, first + rest)
                else:
                    piece = jnp.where(
                        lane < first + rest, turn(j - 1, first + rest), turn(j, first + rest)
                    )
                tile = piece if k == 0 else jnp.where(lane < first, tile, piece)
            return tile

        for t in range(WIN):
            for q in range(z.chunks // WIN):
                for k in range(z.span // 8):
                    tile = eight_rows(t * z.nodes + 8 * k, q)
                    if 8 * k == z.nodes:
                        tile = jnp.where(row < TAIL // 2, tile, eight_rows(t * z.nodes - 8, q))
                    at = pl.ds(t * z.span + 8 * k, 8)
                    out_ref[c, at, q * LANES:(q + 1) * LANES] = tile


def halo_kernel(z, u_ref, v_ref, m_ref, c_ref, g_ref, *rest):
    beside = rest[:z.sides]
    pair_ref, cross_ref, toeplitz_ref = rest[z.sides:]
    toeplitz_factors(z, g_ref, toeplitz_ref)
    is_high = lax.axis_index("normal") == z.normal - 1
    is_even = lax.axis_index("strike") % 2 == 0
    size = z.layers
    for ref, is_end in ((pair_ref, is_even), (cross_ref, jnp.logical_not(is_even))):
        nodes = [jnp.where(is_end, z.nodes - 1 - d, d) for d in range(3)]
        for c in range(z.parts):
            tiles = []
            known = None
            for node in nodes:
                tile = u_ref[c, node]
                if known is None:
                    high = tile.astype(bf16).astype(f32)
                    tiles += [high, tile - high]
                    known = high + (tile - high).astype(bf16).astype(f32)
                else:
                    tiles.append(tile - known)
                    known = known + tiles[-1].astype(bf16).astype(f32)
            at = pl.ds(c * 4 * size, 4 * size)
            ref[at, :] = jnp.concatenate(tiles, axis=0).astype(bf16)
            both = jnp.concatenate([v_ref[c, nodes[0]], v_ref[c, nodes[1]]], axis=0).astype(bf16)
            ref[pl.ds(z.halo_v + c * 2 * size, 2 * size), :] = both
        both = jnp.concatenate(
            [m_ref[pl.ds(pl.multiple_of(node * size, size), size), :] for node in nodes[:2]], axis=0
        )
        ref[pl.ds(z.halo_m, 2 * size), :] = both.astype(bf16)
        own = jnp.where(is_high, c_ref[1], c_ref[0])
        touch = jnp.where(is_end, own[z.nodes - TAIL:], own[:TAIL]).astype(f32)

        def rows_of(edge, k, count):
            head = edge[k, pl.ds(0, count), :]
            return jnp.where(is_end, edge[k, pl.ds(z.nodes - count, count), :], head)

        pieces = []
        for edge in beside:
            for c in range(z.parts):
                some = jnp.concatenate(
                    [rows_of(edge, 3 * c, 2), rows_of(edge, 3 * c + 1, 1)], axis=0
                )
                high = some.astype(bf16).astype(f32)
                speed = rows_of(edge, 3 * z.parts + 2 * c, 1)
                pieces += [high, some - high, speed, rows_of(edge, 5 * z.parts, 1)]
        pieces.append(touch)
        spare = z.halo - z.corner - z.touch - TAIL
        if spare:
            pieces.append(jnp.zeros((spare, z.dips), f32))
        ref[pl.ds(z.corner, z.halo - z.corner), :] = jnp.concatenate(pieces, axis=0).astype(bf16)


def middle_kernel(z, wanted_ref, spots_ref, toeplitz_ref, *rest):
    window = (rest[z.targets - 1],) + rest[:z.targets - 1]
    mine_ref = rest[z.targets]
    out_refs, stack_ref, part_ref = rest[z.targets + 1:-2], rest[-2], rest[-1]
    me = lax.axis_index("strike")
    place, group = me % WIN, me // WIN
    spare = jnp.zeros((z.chunk_rows - z.spectral, 2 * LANES), f32)
    lines = []
    for ref in window:
        both = ref[pl.ds(z.plane_rows, 2 * z.spectral), :].astype(f32)
        lines += [jnp.concatenate([both[:z.spectral], both[z.spectral:]], axis=1), spare]
    picked = lax.dot_general(
        wanted_ref[...],
        jnp.concatenate(lines, axis=0).astype(bf16),
        (((1,), (1,)), ((), ())),
        preferred_element_type=f32,
    )
    own_rows = z.targets * z.nodes
    for c in range(z.parts):
        for s, ref in enumerate(window):
            source = (group + z.targets - s) % z.targets
            at = pl.multiple_of(source * z.nodes, z.nodes)
            stack_ref[c, pl.ds(at, z.nodes), :] = ref[pl.ds(c * z.nodes, z.nodes), :]
        stack_ref[c, pl.ds(own_rows, z.targets * z.chunk_rows), :] = spots_ref[c]
        factors = jnp.concatenate([toeplitz_ref[c], picked], axis=1).astype(bf16)
        part_ref[c] = jnp.dot(factors, stack_ref[c], preferred_element_type=f32)
    for w, (spot, ref) in enumerate(zip(beside_me(place), (mine_ref,) + out_refs)):
        at = pl.ds(pl.multiple_of(spot * z.span, 8), z.span)
        block = jnp.concatenate([part_ref[c, at, :] for c in range(z.parts)], axis=0)
        ref[...] = block.astype(bf16) if w else block


def unpack(z, left_ref, right_ref, uh_ref, vh_ref, mh_ref):
    size = z.layers
    for ref, is_left in ((right_ref, False), (left_ref, True)):
        spots = [pl.ds((TAIL - 1 - d if is_left else d) * size, size) for d in range(3)]
        for c in range(z.parts):
            tiles = ref[pl.ds(c * 4 * size, 4 * size), :].astype(f32)
            known = tiles[:size]
            for d in range(3):
                known = known + tiles[(d + 1) * size:(d + 2) * size]
                uh_ref[c, spots[d], :] = known
            both = ref[pl.ds(z.halo_v + c * 2 * size, 2 * size), :].astype(f32)
            vh_ref[c, spots[0], :] = both[:size]
            vh_ref[c, spots[1], :] = both[size:]
        both = ref[pl.ds(z.halo_m, 2 * size), :].astype(f32)
        mh_ref[spots[0], :] = both[:size]
        mh_ref[spots[1], :] = both[size:]
    for c in range(z.parts):
        uh_ref[c, pl.ds(3 * size, 2 * size), :] = jnp.zeros((2 * size, z.dips), f32)
        vh_ref[c, pl.ds(2 * size, 4 * size), :] = jnp.zeros((4 * size, z.dips), f32)
    mh_ref[pl.ds(2 * size, 4 * size), :] = jnp.zeros((4 * size, z.dips), f32)


def corner_tiles(z, left_ref, right_ref, tile_ref):
    rows = pl.ds(z.corner, z.halo - z.corner)
    after, before = right_ref[rows, :].astype(f32), left_ref[rows, :].astype(f32)
    blank = jnp.zeros((TAIL, z.dips), f32)

    def tile(head, tail):
        return jnp.concatenate([head, blank[:TAIL - head.shape[0] - tail.shape[0]], tail], axis=0)

    for side in range(z.sides):
        for c in range(z.parts):
            at = 8 * (side * z.parts + c)
            a, b = after[at:at + 8], before[at:at + 8]
            head, tail = a[0:3] + a[3:6], b[0:3] + b[3:6]
            tile_ref[side, 3 * c] = tile(head[:2], tail[:2])
            tile_ref[side, 3 * c + 1] = tile(head[2:], tail[2:])
            tile_ref[side, 3 * c + 2] = blank
            tile_ref[side, 3 * z.parts + 2 * c] = tile(a[6:7], b[6:7])
            tile_ref[side, 3 * z.parts + 2 * c + 1] = blank
            if c == 0:
                tile_ref[side, 5 * z.parts] = tile(a[7:8], b[7:8])
                tile_ref[side, 5 * z.parts + 1] = blank


def in_plane(values, first_dip, last_dip):
    count, dips = values.shape
    around = pltpu.roll(values, 1, 0) + pltpu.roll(values, count - 1, 0)
    around += jnp.where(first_dip, 0.0, pltpu.roll(values, 1, 1))
    around += jnp.where(last_dip, 0.0, pltpu.roll(values, dips - 1, 1))
    return around - 6.0 * values


def substeps(z, fetch, rows, store, m_ref):
    dip = lax.broadcasted_iota(jnp.int32, (rows, z.dips), 1)
    first_dip, last_dip = dip == 0, dip == z.dips - 1
    two = z.sides == 2
    low = -2 if two else 0
    top = z.layers
    for f in range(low, top + 2):
        m_ref[f - low] = (time_step * time_step) * fetch("m", 0, f)

    for c in range(z.parts):
        u = {f: fetch("u", c, f) for f in range(low - 1 if two else 0, top + 3)}
        v = {f: time_step * fetch("v", c, f) for f in range(low, top + 2)}
        for step in range(SUB):
            levels = range(low + step if two else 0, top + 2 - step)
            for f in levels:
                lap = in_plane(u[f], first_dip, last_dip) + u[f + 1]
                if f - 1 in u:
                    lap += u[f - 1]
                v[f] = v[f] + m_ref[f - low] * lap
            u = {f: u[f] + v[f] for f in levels}
        for f in range(top):
            store(c, f, u[f], (1.0 / time_step) * v[f])


def beside_index(z, kind, c, f):
    side, j = (0, f - z.layers) if f >= z.layers else (1, -1 - f)
    return side, {"u": 3 * c, "v": 3 * z.parts + 2 * c, "m": 5 * z.parts}[kind] + j


def base_kernel(z, u_ref, v_ref, m_ref, *rest):
    sides = rest[:z.sides]
    out_u, out_v, gathered_ref = rest[z.sides:]

    def fetch(kind, c, f):
        if 0 <= f < z.layers:
            first = 0 if kind == "m" else c * z.stride
            own = {"u": u_ref, "v": v_ref, "m": m_ref}[kind]
            return own[pl.ds(first + layer_of(z, f), z.nodes, stride=z.layers), :]
        side, at = beside_index(z, kind, c, f)
        return sides[side][at]

    def store(c, f, u, v):
        at = pl.ds(c * z.stride + layer_of(z, f), z.nodes, stride=z.layers)
        out_u[at, :] = u
        out_v[at, :] = v

    substeps(z, fetch, z.nodes, store, gathered_ref)


def strips_kernel(z, u_ref, v_ref, m_ref, c_ref, cross_ref, pair_ref, *rest):
    sides = rest[:z.sides]
    out_u, out_v, mf_ref, ch_ref, uh_ref, vh_ref, mh_ref, tile_ref, gathered_ref = rest[z.sides:]
    place = lax.axis_index("normal")
    is_high = place == z.normal - 1
    is_face = (is_high | (place == 0)).astype(f32)
    ch_ref[pl.ds(0, z.nodes), :] = jnp.where(is_high, c_ref[1], c_ref[0]).astype(f32) * is_face

    def receive(left_ref, right_ref):
        unpack(z, left_ref, right_ref, uh_ref, vh_ref, mh_ref)
        corner_tiles(z, left_ref, right_ref, tile_ref)
        row = lax.broadcasted_iota(jnp.int32, (TAIL, z.dips), 0)
        rows = pl.ds(z.corner, z.halo - z.corner)
        before = left_ref[rows, :].astype(f32)[z.touch:z.touch + TAIL]
        after = right_ref[rows, :].astype(f32)[z.touch:z.touch + TAIL]
        ch_ref[pl.ds(z.nodes, TAIL), :] = jnp.where(row < TAIL // 2, after, before) * is_face

    is_even = lax.axis_index("strike") % 2 == 0

    @pl.when(is_even)
    def _():
        receive(cross_ref, pair_ref)

    @pl.when(jnp.logical_not(is_even))
    def _():
        receive(pair_ref, cross_ref)

    last = z.nodes - TAIL

    def fetch(kind, c, f):
        if 0 <= f < z.layers:
            layer = layer_of(z, f)
            first = layer if kind == "m" else c * z.stride + layer
            own = {"u": u_ref, "v": v_ref, "m": m_ref}[kind]
            tail = mh_ref if kind == "m" else (uh_ref if kind == "u" else vh_ref).at[c]
            pieces = [
                own[pl.ds(first + last * z.layers, TAIL, stride=z.layers), :],
                tail[pl.ds(layer, TAIL, stride=z.layers), :],
                own[pl.ds(first, TAIL, stride=z.layers), :],
            ]
        else:
            side, at = beside_index(z, kind, c, f)
            edge = sides[side]
            pieces = [edge[at, pl.ds(last, TAIL), :], tile_ref[side, at], edge[at, pl.ds(0, TAIL), :]]
        return jnp.concatenate(pieces, axis=0)

    def store(c, f, u, v):
        for out, x in ((out_u, u), (out_v, v)):
            out[c, f, pl.ds(0, TAIL), :] = x[2 * TAIL:]
            out[c, f, pl.ds(TAIL, TAIL), :] = x[:TAIL]

    substeps(z, fetch, 3 * TAIL, store, gathered_ref)
    for f in range(3):
        layer = layer_of(z, f)
        mf_ref[f, pl.ds(0, z.nodes), :] = m_ref[pl.ds(layer, z.nodes, stride=z.layers), :]
        mf_ref[f, pl.ds(z.nodes, TAIL), :] = mh_ref[pl.ds(layer, TAIL, stride=z.layers), :]


def final_kernel(z, mine_ref, contact_ref, m_ref, base_u, base_v, strip_u, strip_v, *rest):
    arrived, (out_u, out_v, u_ref, v_ref, sems) = rest[:-5], rest[-5:]
    dip = lax.broadcasted_iota(jnp.int32, (z.span, z.dips), 1)
    first_dip, last_dip = dip == 0, dip == z.dips - 1
    contact = contact_ref[...]
    m0, m1, m2 = m_ref[0], m_ref[1], m_ref[2]
    h = time_step
    arrived = [ref[...].astype(f32) for ref in arrived]
    copies = []
    half = TAIL // 2
    for c in range(z.parts):
        force = mine_ref[pl.ds(c * z.span, z.span), :]
        for other in arrived:
            force = force + other[c * z.span:(c + 1) * z.span]
        force = force * contact
        v0 = h * force
        u0 = h * v0
        v1 = h * (m1 * u0)
        v0 = v0 + h * (m0 * in_plane(u0, first_dip, last_dip) + force)
        u0 = u0 + h * v0
        u1 = h * v1
        v2 = h * (m2 * u1)
        w0 = v0 + h * (m0 * (in_plane(u0, first_dip, last_dip) + u1) + force)
        v1 = v1 + h * (m1 * (in_plane(u1, first_dip, last_dip) + u0))
        pairs = ((u0 + h * w0, w0), (u1 + h * v1, v1), (h * v2, v2))
        part = pl.ds(c * z.stride, z.stride)
        whole = ((base_u, strip_u, u_ref, out_u), (base_v, strip_v, v_ref, out_v))
        for k, (base, strip, sums, out) in enumerate(whole):
            sums[part, :] = base[part, :]
            for f in range(z.layers):
                first = c * z.stride + layer_of(z, f)
                late = first + (z.nodes - half) * z.layers
                sums[pl.ds(first, half, stride=z.layers), :] = strip[c, f, pl.ds(0, half), :]
                sums[pl.ds(late, half, stride=z.layers), :] = strip[c, f, pl.ds(2 * TAIL - half, half), :]
            for f in range(3):
                at = pl.ds(c * z.stride + layer_of(z, f), z.nodes, stride=z.layers)
                sums[at, :] = sums[at, :] + pairs[f][k][:z.nodes]
            copies.append(
                pltpu.make_async_copy(sums.at[part, :], out.at[part, :], sems.at[2 * c + k])
            )
            copies[-1].start()
    for copy in copies:
        copy.wait()


PARAMS = pltpu.CompilerParams(vmem_limit_bytes=32 * 2**20)
FIRST = pltpu.CompilerParams(vmem_limit_bytes=32 * 2**20)
HBM = pl.BlockSpec(memory_space=pltpu.HBM)


def in_hbm(*arrays):
    return [pltpu.with_memory_space_constraint(x, pltpu.HBM) for x in arrays]


def shape(dims, kind):
    return jax.ShapeDtypeStruct(dims, kind)


def body(mesh, displacement, velocity, stiffness, yield_flags, contact, history, kernel):
    z = Sizes(mesh, displacement, history)
    u = displacement.reshape(-1, z.dips)
    v = velocity.reshape(-1, z.dips)
    s = stiffness.reshape(-1, z.dips)
    y = yield_flags.reshape(-1, yield_flags.shape[2])
    dma = pltpu.SemaphoreType.DMA
    ring = lambda step: [(i, (i + step) % z.strike) for i in range(z.strike)]
    around = lambda w: [(i, i - i % WIN + beside_me(i % WIN)[w]) for i in range(z.strike)]

    edge = (5 * z.parts + 2, z.nodes, z.dips)
    common, response, modulus, wanted, spots, *edges_and_others = pl.pallas_call(
        functools.partial(common_kernel, z),
        out_shape=(shape((z.common, LANES), bf16), shape((z.chunks, 8, LANES), f32), shape(s.shape, f32))
        + (
            shape((WIN * z.span, 2 * LANES), bf16),
            shape((z.parts, z.targets * z.chunk_rows, z.dips), bf16),
        )
        + (shape(edge, f32),) * z.sides
        + (shape((z.common, LANES), bf16),) * (z.targets - 1),
        in_specs=[HBM] * 7,
        out_specs=(VMEM,) * (4 + z.sides + z.targets),
        scratch_shapes=[
            pltpu.VMEM(u.shape, f32),
            pltpu.VMEM((z.lags - 1, 2, z.parts, z.rows, z.modes), bf16),
            pltpu.VMEM((z.parts, z.lags, z.modes), f32),
            pltpu.VMEM((2 * z.modes, z.modes // 4), bf16),
            pltpu.VMEM(v.shape, f32),
            pltpu.VMEM(s.shape, f32),
            pltpu.VMEM(y.shape, jnp.int32),
            pltpu.VMEM((z.chunk_rows, z.modes), f32),
            pltpu.VMEM((z.chunk_rows, z.modes), f32),
            pltpu.VMEM((z.chunks, z.spectral, LANES), f32),
            dma((7,)),
        ],
        compiler_params=FIRST,
        name="plane_and_history",
    )(*in_hbm(u, history, kernel.transpose(0, 2, 1, 3), phase_quarter(z.modes), v, s, y))

    edges, others = edges_and_others[:z.sides], edges_and_others[z.sides:]
    window = [common] + [
        lax.ppermute(other, "strike", ring(WIN * s)) for s, other in enumerate(others, 1)
    ]

    if z.sides == 2:
        is_high = lax.axis_index("normal") == z.normal - 1
        above, below = edges
        steps = [(i, i + 1) for i in range(z.normal - 1)]
        from_below = lax.ppermute(above, "normal", steps)
        from_above = lax.ppermute(
            jnp.where(is_high, above, below), "normal", [(j, i) for i, j in steps]
        )
        beside = [
            jnp.where(is_high, from_below, from_above),
            jnp.where(is_high, from_above, from_below),
        ]
    else:
        beside = [lax.ppermute(edges[0], "normal", [(0, 1), (1, 0)])]

    to_pair, to_cross, toeplitz = pl.pallas_call(
        functools.partial(halo_kernel, z),
        out_shape=(shape((z.halo, LANES), bf16),) * 2
        + (shape((z.parts, WIN * z.span, z.targets * z.nodes), f32),),
        in_specs=[VMEM] * (5 + z.sides),
        out_specs=(VMEM,) * 3,
        compiler_params=PARAMS,
        name="strike_edges_and_toeplitz",
    )(displacement, velocity, modulus, contact, response, *beside)
    from_pair = lax.ppermute(to_pair, "strike", [(i, i ^ 1) for i in range(z.strike)])
    from_cross = lax.ppermute(
        to_cross, "strike", [(i, (i - 1 + i % 2 * 2) % z.strike) for i in range(z.strike)]
    )

    block = (z.parts * z.span, z.dips)
    mine, *parcels = pl.pallas_call(
        functools.partial(middle_kernel, z),
        out_shape=(shape(block, f32),) + (shape(block, bf16),) * (WIN - 1),
        in_specs=[VMEM] * (3 + z.targets),
        out_specs=(VMEM,) * WIN,
        scratch_shapes=[
            pltpu.VMEM((z.parts, z.targets * (z.nodes + z.chunk_rows), z.dips), bf16),
            pltpu.VMEM((z.parts, WIN * z.span, z.dips), f32),
        ],
        compiler_params=PARAMS,
        name="partial_tractions",
    )(wanted, spots, toeplitz, *window[1:], common)

    arrived = [
        lax.ppermute(parcels[w - 1], "strike", around(w)) for w in (3, 1, 2)
    ]
    base_u, base_v = pl.pallas_call(
        functools.partial(base_kernel, z),
        out_shape=(shape(u.shape, f32),) * 2,
        in_specs=[VMEM] * (3 + z.sides),
        out_specs=(VMEM,) * 2,
        scratch_shapes=[pltpu.VMEM((z.layers + 2 * z.sides, z.nodes, z.dips), f32)],
        compiler_params=PARAMS,
        name="unloaded_substeps",
    )(u, v, modulus, *beside)

    tail = (z.parts, TAIL * z.layers, z.dips)
    strip = (z.parts, z.layers, 2 * TAIL, z.dips)
    strip_u, strip_v, face_modulus, touching = pl.pallas_call(
        functools.partial(strips_kernel, z),
        out_shape=(
            shape(strip, f32),
            shape(strip, f32),
            shape((3, z.span, z.dips), f32),
            shape((z.span, z.dips), f32),
        ),
        in_specs=[VMEM] * (6 + z.sides),
        out_specs=(VMEM,) * 4,
        scratch_shapes=[
            pltpu.VMEM(tail, f32),
            pltpu.VMEM(tail, f32),
            pltpu.VMEM(tail[1:], f32),
            pltpu.VMEM((z.sides, edge[0], TAIL, z.dips), f32),
            pltpu.VMEM((z.layers + 2 * z.sides, 3 * TAIL, z.dips), f32),
        ],
        compiler_params=PARAMS,
        name="end_strips",
    )(u, v, modulus, contact, from_cross, from_pair, *beside)

    moved, speed = pl.pallas_call(
        functools.partial(final_kernel, z),
        out_shape=(shape(u.shape, f32),) * 2,
        in_specs=[VMEM] * (7 + len(arrived)),
        out_specs=(HBM,) * 2,
        scratch_shapes=[pltpu.VMEM(u.shape, f32), pltpu.VMEM(u.shape, f32), dma((2 * z.parts,))],
        compiler_params=PARAMS,
        name="add_force_response",
    )(mine, touching, face_modulus, base_u, base_v, strip_u, strip_v, *arrived)
    return (moved.reshape(displacement.shape), speed.reshape(displacement.shape))


def solution(mesh):
    return jax.shard_map(
        functools.partial(body, mesh),
        mesh=mesh,
        in_specs=(
            P(None, "strike", "normal", None),
            P(None, "strike", "normal", None),
            P("strike", "normal", None),
            P("strike", "normal", None),
            P(None, "strike", None),
            P(None, None, None, None, "strike", None),
            P(),
        ),
        out_specs=(P(None, "strike", "normal", None), P(None, "strike", "normal", None)),
        check_vma=False,
    )
```

```python
import functools
import itertools
import math

import jax
import jax.numpy as jnp
import numpy as np
from jax import lax
from jax.experimental import pallas as pl
from jax.experimental.pallas import tpu as pltpu
from jax.sharding import PartitionSpec as P

SUB = 3
BLK = 4
WIN = 4
TAIL = 8
LANES = 128

time_step = 0.5

f32 = jnp.float32
bf16 = jnp.bfloat16
VMEM = pl.BlockSpec(memory_space=pltpu.VMEM)


def round_up(value, step):
    return -(-value // step) * step


def phase_quarter(mode_count):
    phase = np.outer(np.arange(mode_count), np.arange(mode_count // 4)) % mode_count
    phase = phase * (2.0 * np.pi / mode_count)
    return np.concatenate([np.cos(phase), -np.sin(phase)]).astype(np.float32).astype(bf16)


class Sizes:
    def __init__(self, mesh, displacement, history):
        self.strike = mesh.shape["strike"]
        self.normal = mesh.shape["normal"]
        self.parts, self.nodes, self.layers, self.dips = displacement.shape
        self.lags = history.shape[1]
        self.rows = history.shape[4]
        self.modes = history.shape[5]
        self.chunks = self.modes // LANES
        self.spectral = round_up(self.parts * self.rows, 8)
        self.chunk_rows = round_up(self.spectral + 2 * self.parts, 16)
        self.plane_rows = self.parts * self.nodes
        self.common = self.plane_rows + round_up(3 * self.spectral, 16)
        self.halo_v = self.parts * 4 * self.layers
        self.halo_m = self.halo_v + self.parts * 2 * self.layers
        self.corner = self.halo_m + 2 * self.layers
        self.span = self.nodes + TAIL
        self.targets = self.strike // WIN
        self.stride = self.nodes * self.layers
        self.sides = 1 if self.normal == 2 else 2
        self.touch = self.sides * self.parts * 8
        self.halo = self.corner + round_up(self.touch + TAIL, 16)


def widen_flags(flags, dips):
    blocks = flags.shape[1]
    block_id = lax.broadcasted_iota(jnp.int32, (blocks, dips), 0)
    dip_id = lax.broadcasted_iota(jnp.int32, (blocks, dips), 1)
    spread = (dip_id // BLK == block_id).astype(bf16)
    wide = jnp.dot(flags.astype(f32).astype(bf16), spread, preferred_element_type=f32)
    return 1.0 - 0.5 * wide


def node_offset(rows):
    return jnp.where(rows < rows.shape[0] - TAIL // 2, rows, rows - rows.shape[0])


def layer_of(z, level):
    is_high = lax.axis_index("normal") == z.normal - 1
    return jnp.where(is_high, z.layers - 1 - level, level)


def beside_me(place):
    turn = place ^ (place >> 1)
    ahead, behind = (turn + 1) % WIN, (turn + WIN - 1) % WIN
    return (place, ahead ^ (ahead >> 1), behind ^ (behind >> 1), place ^ 3)


def start_all(pairs, sems):
    copies = [pltpu.make_async_copy(a, b, sems.at[i]) for i, (a, b) in enumerate(pairs)]
    for copy in copies:
        copy.start()
    return copies


def high_and_rest(values):
    high = values.astype(bf16)
    return high, (values - high.astype(f32)).astype(bf16)


def set_modulus(z, s_ref, y_ref, out_ref):
    soft = widen_flags(y_ref[...], z.dips)
    for n in range(z.nodes):
        at = n // BLK * z.layers
        rows = pl.ds(n * z.layers, z.layers)
        out_ref[rows, :] = s_ref[rows, :] * soft[at:at + z.layers]


def selections(z, wanted_ref, spots_ref):
    me = lax.axis_index("strike")
    place, group = me % WIN, me // WIN
    offset = node_offset(lax.broadcasted_iota(jnp.int32, (z.span, 2 * LANES), 0))
    lane = lax.broadcasted_iota(jnp.int32, (z.span, 2 * LANES), 1)
    wanted = []
    for t in range(WIN):
        node = t * z.nodes + offset
        node = jnp.where(node < 0, node + 2 * LANES, node)
        wanted.append((lane == node).astype(f32))
    wanted_ref[...] = jnp.concatenate(wanted, axis=0).astype(bf16)
    row = lax.broadcasted_iota(jnp.int32, (z.chunk_rows, z.dips), 0)
    ahead = lax.broadcasted_iota(jnp.int32, (z.chunk_rows, z.dips), 1) - row
    for c in range(z.parts):
        inside = (row >= c * z.rows) & (row < (c + 1) * z.rows)
        for s in range(z.targets):
            source = (group + z.targets - s) % z.targets
            spot = inside & (ahead == z.rows * (WIN * source + place) - c * z.rows)
            spots_ref[c, pl.ds(s * z.chunk_rows, z.chunk_rows), :] = spot.astype(f32).astype(bf16)


def common_kernel(z, u_hbm, h_hbm, k_hbm, t_hbm, v_hbm, s_hbm, y_hbm, out_ref, g_ref, m_ref, wanted_ref, spots_ref, *rest):
    edges, others = rest[:z.sides], rest[z.sides:z.sides + z.targets - 1]
    u_ref, h_ref, k_ref, t_ref, v_ref, s_ref, y_ref, re_ref, im_ref, line_ref, sems = rest[-11:]
    is_high = lax.axis_index("normal") == z.normal - 1
    face = is_high.astype(jnp.int32)
    copies = start_all(
        [
            (h_hbm.at[face, pl.ds(0, z.lags - 1)], h_ref),
            (k_hbm.at[face], k_ref),
            (t_hbm, t_ref),
            (u_hbm, u_ref),
            (v_hbm, v_ref),
            (s_hbm, s_ref),
            (y_hbm, y_ref),
        ],
        sems,
    )
    selections(z, wanted_ref, spots_ref)
    re_ref[...] = jnp.zeros_like(re_ref)
    im_ref[...] = jnp.zeros_like(im_ref)
    copies[1].wait()
    copies[0].wait()
    for c in range(z.parts):
        for q, dst in ((0, re_ref), (1, im_ref)):
            total = None
            for lag in range(1, z.lags):
                term = k_ref[c, pl.ds(lag, 1), :] * h_ref[lag - 1, q, c].astype(f32)
                total = term if total is None else total + term
            dst[pl.ds(c * z.rows, z.rows), :] = total
        newest = k_ref[c, pl.ds(0, 1), :]
        high = newest.astype(bf16).astype(f32)
        re_ref[pl.ds(z.spectral + c, 1), :] = high
        re_ref[pl.ds(z.spectral + z.parts + c, 1), :] = newest - high
    re, im = re_ref[...], im_ref[...]
    quarter = lax.broadcasted_iota(jnp.int32, (1, z.modes), 1) % 4
    one = (quarter == 0).astype(f32) - (quarter == 2).astype(f32)
    two = (quarter == 1).astype(f32) - (quarter == 3).astype(f32)
    flip = 1.0 - 2.0 * (quarter % 2).astype(f32)
    turned = jnp.concatenate(
        [
            jnp.concatenate([re, im], axis=1),
            jnp.concatenate([re * one - im * two, re * two + im * one], axis=1),
            jnp.concatenate([re * flip, im * flip], axis=1),
            jnp.concatenate([re * one + im * two, im * one - re * two], axis=1),
        ],
        axis=0,
    )
    copies[2].wait()
    lines = sum(
        jnp.dot(part, t_ref[...], preferred_element_type=f32) for part in high_and_rest(turned)
    ) * (1.0 / math.sqrt(z.modes))
    per_quarter = z.chunks // 4
    for m in range(4):
        for q in range(per_quarter):
            piece = lines[m * z.chunk_rows:(m + 1) * z.chunk_rows, q * LANES:(q + 1) * LANES]
            chunk = m * per_quarter + q
            line_ref[chunk] = piece[:z.spectral]
            g_ref[chunk] = piece[z.spectral:z.spectral + 8]
    group = lax.axis_index("strike") // WIN
    lane = lax.broadcasted_iota(jnp.int32, (z.spectral, LANES), 1)
    for s, ref in enumerate((out_ref,) + others):
        chunk = (group + s) % z.targets
        after, before = line_ref[(chunk + 1) % z.chunks], line_ref[(chunk + z.chunks - 1) % z.chunks]
        both = jnp.concatenate(
            [line_ref[chunk], jnp.where(lane < LANES // 2, after, before)], axis=0
        )
        high, rest = (part.astype(f32) for part in high_and_rest(both))
        pieces = [high, rest[:z.spectral]]
        spare = z.common - z.plane_rows - 3 * z.spectral
        pieces += [jnp.zeros((spare, LANES), f32)] if spare else []
        at = pl.ds(z.plane_rows, z.common - z.plane_rows)
        ref[at, :] = jnp.concatenate(pieces, axis=0).astype(bf16)
    copies[3].wait()
    layer = face * (z.layers - 1)
    for c in range(z.parts):
        plane = u_ref[pl.ds(c * z.stride + layer, z.nodes, stride=z.layers), :].astype(bf16)
        for ref in (out_ref,) + others:
            ref[pl.ds(c * z.nodes, z.nodes), :] = plane
    for copy in copies[4:]:
        copy.wait()
    set_modulus(z, s_ref, y_ref, m_ref)
    size = z.layers
    for out, levels in zip(edges, ((size - 1, size - 2, size - 3), (0, 1, 2))):
        for j, f in enumerate(levels):
            layer = layer_of(z, f)
            for c in range(z.parts):
                at = pl.ds(c * z.stride + layer, z.nodes, stride=size)
                out[3 * c + j] = u_ref[at, :]
                if j < 2:
                    out[3 * z.parts + 2 * c + j] = v_ref[at, :]
            if j < 2:
                out[5 * z.parts + j] = m_ref[pl.ds(layer, z.nodes, stride=size), :]


def toeplitz_factors(z, g_ref, out_ref):
    me = lax.axis_index("strike")
    place, group = me % WIN, me // WIN
    lane = lax.broadcasted_iota(jnp.int32, (8, LANES), 1)
    row = lax.broadcasted_iota(jnp.int32, (8, LANES), 0)
    stack = []
    for c in range(z.parts):
        line = jnp.concatenate(
            [
                g_ref[j, pl.ds(c, 1), :] + g_ref[j, pl.ds(z.parts + c, 1), :]
                for j in range(z.chunks)
            ],
            axis=1,
        ) * (1.0 / math.sqrt(z.modes))
        stack.append(jnp.broadcast_to(line, (8, z.modes)))
    wide = pltpu.roll(jnp.concatenate(stack, axis=0), 0, 1, stride=1, stride_axis=0)
    wide = pltpu.roll(wide, (group * LANES - place * z.nodes + z.modes) % z.modes, 1)
    for c in range(z.parts):
        columns = [wide[8 * c:8 * c + 8, j * LANES:(j + 1) * LANES] for j in range(z.chunks)]

        turned = {}

        def turn(j, shift):
            key = (j % z.chunks, shift % LANES)
            if key not in turned:
                piece = columns[key[0]]
                turned[key] = pltpu.roll(piece, key[1], 1) if key[1] else piece
            return turned[key]

        def eight_rows(shift, q):
            whole, rest = divmod((shift - 8 * c) % z.modes, LANES)
            tile = None
            for k in range(WIN):
                j = q * WIN + k - whole
                first = k * z.nodes
                if rest == 0:
                    piece = turn(j, first)
                elif rest >= z.nodes:
                    piece = turn(j - 1, first + rest)
                else:
                    piece = jnp.where(
                        lane < first + rest, turn(j - 1, first + rest), turn(j, first + rest)
                    )
                tile = piece if k == 0 else jnp.where(lane < first, tile, piece)
            return tile

        for t in range(WIN):
            for q in range(z.chunks // WIN):
                for k in range(z.span // 8):
                    tile = eight_rows(t * z.nodes + 8 * k, q)
                    if 8 * k == z.nodes:
                        tile = jnp.where(row < TAIL // 2, tile, eight_rows(t * z.nodes - 8, q))
                    at = pl.ds(t * z.span + 8 * k, 8)
                    out_ref[c, at, q * LANES:(q + 1) * LANES] = tile


def halo_kernel(z, u_ref, v_ref, m_ref, c_ref, g_ref, *rest):
    beside = rest[:z.sides]
    pair_ref, cross_ref, toeplitz_ref = rest[z.sides:]
    toeplitz_factors(z, g_ref, toeplitz_ref)
    is_high = lax.axis_index("normal") == z.normal - 1
    is_even = lax.axis_index("strike") % 2 == 0
    size = z.layers
    for ref, is_end in ((pair_ref, is_even), (cross_ref, jnp.logical_not(is_even))):
        nodes = [jnp.where(is_end, z.nodes - 1 - d, d) for d in range(3)]
        for c in range(z.parts):
            tiles = []
            known = None
            for node in nodes:
                tile = u_ref[c, node]
                if known is None:
                    high = tile.astype(bf16).astype(f32)
                    tiles += [high, tile - high]
                    known = high + (tile - high).astype(bf16).astype(f32)
                else:
                    tiles.append(tile - known)
                    known = known + tiles[-1].astype(bf16).astype(f32)
            at = pl.ds(c * 4 * size, 4 * size)
            ref[at, :] = jnp.concatenate(tiles, axis=0).astype(bf16)
            both = jnp.concatenate([v_ref[c, nodes[0]], v_ref[c, nodes[1]]], axis=0).astype(bf16)
            ref[pl.ds(z.halo_v + c * 2 * size, 2 * size), :] = both
        both = jnp.concatenate(
            [m_ref[pl.ds(pl.multiple_of(node * size, size), size), :] for node in nodes[:2]], axis=0
        )
        ref[pl.ds(z.halo_m, 2 * size), :] = both.astype(bf16)
        own = jnp.where(is_high, c_ref[1], c_ref[0])
        touch = jnp.where(is_end, own[z.nodes - TAIL:], own[:TAIL]).astype(f32)

        def rows_of(edge, k, count):
            head = edge[k, pl.ds(0, count), :]
            return jnp.where(is_end, edge[k, pl.ds(z.nodes - count, count), :], head)

        pieces = []
        for edge in beside:
            for c in range(z.parts):
                some = jnp.concatenate(
                    [rows_of(edge, 3 * c, 2), rows_of(edge, 3 * c + 1, 1)], axis=0
                )
                high = some.astype(bf16).astype(f32)
                speed = rows_of(edge, 3 * z.parts + 2 * c, 1)
                pieces += [high, some - high, speed, rows_of(edge, 5 * z.parts, 1)]
        pieces.append(touch)
        spare = z.halo - z.corner - z.touch - TAIL
        if spare:
            pieces.append(jnp.zeros((spare, z.dips), f32))
        ref[pl.ds(z.corner, z.halo - z.corner), :] = jnp.concatenate(pieces, axis=0).astype(bf16)


def middle_kernel(z, wanted_ref, spots_ref, toeplitz_ref, *rest):
    window = (rest[z.targets - 1],) + rest[:z.targets - 1]
    mine_ref = rest[z.targets]
    out_refs, stack_ref, part_ref = rest[z.targets + 1:-2], rest[-2], rest[-1]
    me = lax.axis_index("strike")
    place, group = me % WIN, me // WIN
    spare = jnp.zeros((z.chunk_rows - z.spectral, 2 * LANES), f32)
    lines = []
    size = z.spectral
    for j, ref in itertools.product(range(2), window):
        part = ref[pl.ds(z.plane_rows, z.common - z.plane_rows), :].astype(f32)
        near = part[size:2 * size] if j == 0 else jnp.zeros((size, LANES), f32)
        lines += [jnp.concatenate([part[2 * j * size:(2 * j + 1) * size], near], axis=1), spare]
    picked = lax.dot_general(
        wanted_ref[...],
        jnp.concatenate(lines, axis=0).astype(bf16),
        (((1,), (1,)), ((), ())),
        preferred_element_type=f32,
    )
    own_rows = z.targets * z.nodes
    for c in range(z.parts):
        for s, ref in enumerate(window):
            source = (group + z.targets - s) % z.targets
            at = pl.multiple_of(source * z.nodes, z.nodes)
            plane = ref[pl.ds(c * z.nodes, z.nodes), :]
            stack_ref[c, pl.ds(at, z.nodes), :] = plane
            stack_ref[c, pl.ds(at + own_rows, z.nodes), :] = plane
        for j in range(2):
            at = pl.ds(2 * own_rows + j * z.targets * z.chunk_rows, z.targets * z.chunk_rows)
            stack_ref[c, at, :] = spots_ref[c]
        factors = jnp.concatenate([*high_and_rest(toeplitz_ref[c]), picked.astype(bf16)], axis=1)
        part_ref[c] = jnp.dot(factors, stack_ref[c], preferred_element_type=f32)
    for spot, ref in zip(beside_me(place), (mine_ref,) + out_refs):
        at = pl.ds(pl.multiple_of(spot * z.span, 8), z.span)
        ref[...] = jnp.concatenate([part_ref[c, at, :] for c in range(z.parts)], axis=0)


def unpack(z, left_ref, right_ref, uh_ref, vh_ref, mh_ref):
    size = z.layers
    for ref, is_left in ((right_ref, False), (left_ref, True)):
        spots = [pl.ds((TAIL - 1 - d if is_left else d) * size, size) for d in range(3)]
        for c in range(z.parts):
            tiles = ref[pl.ds(c * 4 * size, 4 * size), :].astype(f32)
            known = tiles[:size]
            for d in range(3):
                known = known + tiles[(d + 1) * size:(d + 2) * size]
                uh_ref[c, spots[d], :] = known
            both = ref[pl.ds(z.halo_v + c * 2 * size, 2 * size), :].astype(f32)
            vh_ref[c, spots[0], :] = both[:size]
            vh_ref[c, spots[1], :] = both[size:]
        both = ref[pl.ds(z.halo_m, 2 * size), :].astype(f32)
        mh_ref[spots[0], :] = both[:size]
        mh_ref[spots[1], :] = both[size:]
    for c in range(z.parts):
        uh_ref[c, pl.ds(3 * size, 2 * size), :] = jnp.zeros((2 * size, z.dips), f32)
        vh_ref[c, pl.ds(2 * size, 4 * size), :] = jnp.zeros((4 * size, z.dips), f32)
    mh_ref[pl.ds(2 * size, 4 * size), :] = jnp.zeros((4 * size, z.dips), f32)


def corner_tiles(z, left_ref, right_ref, tile_ref):
    rows = pl.ds(z.corner, z.halo - z.corner)
    after, before = right_ref[rows, :].astype(f32), left_ref[rows, :].astype(f32)
    blank = jnp.zeros((TAIL, z.dips), f32)

    def tile(head, tail):
        return jnp.concatenate([head, blank[:TAIL - head.shape[0] - tail.shape[0]], tail], axis=0)

    for side in range(z.sides):
        for c in range(z.parts):
            at = 8 * (side * z.parts + c)
            a, b = after[at:at + 8], before[at:at + 8]
            head, tail = a[0:3] + a[3:6], b[0:3] + b[3:6]
            tile_ref[side, 3 * c] = tile(head[:2], tail[:2])
            tile_ref[side, 3 * c + 1] = tile(head[2:], tail[2:])
            tile_ref[side, 3 * c + 2] = blank
            tile_ref[side, 3 * z.parts + 2 * c] = tile(a[6:7], b[6:7])
            tile_ref[side, 3 * z.parts + 2 * c + 1] = blank
            if c == 0:
                tile_ref[side, 5 * z.parts] = tile(a[7:8], b[7:8])
                tile_ref[side, 5 * z.parts + 1] = blank


def in_plane(values, first_dip, last_dip):
    count, dips = values.shape
    around = pltpu.roll(values, 1, 0) + pltpu.roll(values, count - 1, 0)
    around += jnp.where(first_dip, 0.0, pltpu.roll(values, 1, 1))
    around += jnp.where(last_dip, 0.0, pltpu.roll(values, dips - 1, 1))
    return around - 6.0 * values


def substeps(z, fetch, rows, store, m_ref):
    dip = lax.broadcasted_iota(jnp.int32, (rows, z.dips), 1)
    first_dip, last_dip = dip == 0, dip == z.dips - 1
    two = z.sides == 2
    low = -2 if two else 0
    top = z.layers
    for f in range(low, top + 2):
        m_ref[f - low] = (time_step * time_step) * fetch("m", 0, f)

    for c in range(z.parts):
        u = {f: fetch("u", c, f) for f in range(low - 1 if two else 0, top + 3)}
        v = {f: time_step * fetch("v", c, f) for f in range(low, top + 2)}
        for step in range(SUB):
            levels = range(low + step if two else 0, top + 2 - step)
            for f in levels:
                lap = in_plane(u[f], first_dip, last_dip) + u[f + 1]
                if f - 1 in u:
                    lap += u[f - 1]
                v[f] = v[f] + m_ref[f - low] * lap
            u = {f: u[f] + v[f] for f in levels}
        for f in range(top):
            store(c, f, u[f], (1.0 / time_step) * v[f])


def beside_index(z, kind, c, f):
    side, j = (0, f - z.layers) if f >= z.layers else (1, -1 - f)
    return side, {"u": 3 * c, "v": 3 * z.parts + 2 * c, "m": 5 * z.parts}[kind] + j


def base_kernel(z, u_ref, v_ref, m_ref, *rest):
    sides = rest[:z.sides]
    out_u, out_v, gathered_ref = rest[z.sides:]

    def fetch(kind, c, f):
        if 0 <= f < z.layers:
            first = 0 if kind == "m" else c * z.stride
            own = {"u": u_ref, "v": v_ref, "m": m_ref}[kind]
            return own[pl.ds(first + layer_of(z, f), z.nodes, stride=z.layers), :]
        side, at = beside_index(z, kind, c, f)
        return sides[side][at]

    def store(c, f, u, v):
        at = pl.ds(c * z.stride + layer_of(z, f), z.nodes, stride=z.layers)
        out_u[at, :] = u
        out_v[at, :] = v

    substeps(z, fetch, z.nodes, store, gathered_ref)


def strips_kernel(z, u_ref, v_ref, m_ref, c_ref, cross_ref, pair_ref, *rest):
    sides = rest[:z.sides]
    out_u, out_v, mf_ref, ch_ref, uh_ref, vh_ref, mh_ref, tile_ref, gathered_ref = rest[z.sides:]
    place = lax.axis_index("normal")
    is_high = place == z.normal - 1
    is_face = (is_high | (place == 0)).astype(f32)
    ch_ref[pl.ds(0, z.nodes), :] = jnp.where(is_high, c_ref[1], c_ref[0]).astype(f32) * is_face

    def receive(left_ref, right_ref):
        unpack(z, left_ref, right_ref, uh_ref, vh_ref, mh_ref)
        corner_tiles(z, left_ref, right_ref, tile_ref)
        row = lax.broadcasted_iota(jnp.int32, (TAIL, z.dips), 0)
        rows = pl.ds(z.corner, z.halo - z.corner)
        before = left_ref[rows, :].astype(f32)[z.touch:z.touch + TAIL]
        after = right_ref[rows, :].astype(f32)[z.touch:z.touch + TAIL]
        ch_ref[pl.ds(z.nodes, TAIL), :] = jnp.where(row < TAIL // 2, after, before) * is_face

    is_even = lax.axis_index("strike") % 2 == 0

    @pl.when(is_even)
    def _():
        receive(cross_ref, pair_ref)

    @pl.when(jnp.logical_not(is_even))
    def _():
        receive(pair_ref, cross_ref)

    last = z.nodes - TAIL

    def fetch(kind, c, f):
        if 0 <= f < z.layers:
            layer = layer_of(z, f)
            first = layer if kind == "m" else c * z.stride + layer
            own = {"u": u_ref, "v": v_ref, "m": m_ref}[kind]
            tail = mh_ref if kind == "m" else (uh_ref if kind == "u" else vh_ref).at[c]
            pieces = [
                own[pl.ds(first + last * z.layers, TAIL, stride=z.layers), :],
                tail[pl.ds(layer, TAIL, stride=z.layers), :],
                own[pl.ds(first, TAIL, stride=z.layers), :],
            ]
        else:
            side, at = beside_index(z, kind, c, f)
            edge = sides[side]
            pieces = [edge[at, pl.ds(last, TAIL), :], tile_ref[side, at], edge[at, pl.ds(0, TAIL), :]]
        return jnp.concatenate(pieces, axis=0)

    def store(c, f, u, v):
        for out, x in ((out_u, u), (out_v, v)):
            out[c, f, pl.ds(0, TAIL), :] = x[2 * TAIL:]
            out[c, f, pl.ds(TAIL, TAIL), :] = x[:TAIL]

    substeps(z, fetch, 3 * TAIL, store, gathered_ref)
    for f in range(3):
        layer = layer_of(z, f)
        mf_ref[f, pl.ds(0, z.nodes), :] = m_ref[pl.ds(layer, z.nodes, stride=z.layers), :]
        mf_ref[f, pl.ds(z.nodes, TAIL), :] = mh_ref[pl.ds(layer, TAIL, stride=z.layers), :]


def final_kernel(z, mine_ref, contact_ref, m_ref, base_u, base_v, strip_u, strip_v, *rest):
    arrived, (out_u, out_v, u_ref, v_ref, sems) = rest[:-5], rest[-5:]
    dip = lax.broadcasted_iota(jnp.int32, (z.span, z.dips), 1)
    first_dip, last_dip = dip == 0, dip == z.dips - 1
    contact = contact_ref[...]
    m0, m1, m2 = m_ref[0], m_ref[1], m_ref[2]
    h = time_step
    arrived = [ref[...] for ref in arrived]
    copies = []
    half = TAIL // 2
    for c in range(z.parts):
        force = mine_ref[pl.ds(c * z.span, z.span), :]
        for other in arrived:
            force = force + other[c * z.span:(c + 1) * z.span]
        force = force * contact
        v0 = h * force
        u0 = h * v0
        v1 = h * (m1 * u0)
        v0 = v0 + h * (m0 * in_plane(u0, first_dip, last_dip) + force)
        u0 = u0 + h * v0
        u1 = h * v1
        v2 = h * (m2 * u1)
        w0 = v0 + h * (m0 * (in_plane(u0, first_dip, last_dip) + u1) + force)
        v1 = v1 + h * (m1 * (in_plane(u1, first_dip, last_dip) + u0))
        pairs = ((u0 + h * w0, w0), (u1 + h * v1, v1), (h * v2, v2))
        part = pl.ds(c * z.stride, z.stride)
        whole = ((base_u, strip_u, u_ref, out_u), (base_v, strip_v, v_ref, out_v))
        for k, (base, strip, sums, out) in enumerate(whole):
            sums[part, :] = base[part, :]
            for f in range(z.layers):
                first = c * z.stride + layer_of(z, f)
                late = first + (z.nodes - half) * z.layers
                sums[pl.ds(first, half, stride=z.layers), :] = strip[c, f, pl.ds(0, half), :]
                sums[pl.ds(late, half, stride=z.layers), :] = strip[c, f, pl.ds(2 * TAIL - half, half), :]
            for f in range(3):
                at = pl.ds(c * z.stride + layer_of(z, f), z.nodes, stride=z.layers)
                sums[at, :] = sums[at, :] + pairs[f][k][:z.nodes]
            copies.append(
                pltpu.make_async_copy(sums.at[part, :], out.at[part, :], sems.at[2 * c + k])
            )
            copies[-1].start()
    for copy in copies:
        copy.wait()


PARAMS = pltpu.CompilerParams(vmem_limit_bytes=32 * 2**20)
FIRST = pltpu.CompilerParams(vmem_limit_bytes=32 * 2**20)
HBM = pl.BlockSpec(memory_space=pltpu.HBM)


def in_hbm(*arrays):
    return [pltpu.with_memory_space_constraint(x, pltpu.HBM) for x in arrays]


def pass_kernel(*refs):
    for in_ref, out_ref in zip(refs[:2], refs[2:]):
        out_ref[...] = in_ref[...]


def shape(dims, kind):
    return jax.ShapeDtypeStruct(dims, kind)


def body(mesh, displacement, velocity, stiffness, yield_flags, contact, history, kernel):
    z = Sizes(mesh, displacement, history)
    u = displacement.reshape(-1, z.dips)
    v = velocity.reshape(-1, z.dips)
    s = stiffness.reshape(-1, z.dips)
    y = yield_flags.reshape(-1, yield_flags.shape[2])
    dma = pltpu.SemaphoreType.DMA
    ring = lambda step: [(i, (i + step) % z.strike) for i in range(z.strike)]
    around = lambda w: [(i, i - i % WIN + beside_me(i % WIN)[w]) for i in range(z.strike)]

    edge = (5 * z.parts + 2, z.nodes, z.dips)
    common, response, modulus, wanted, spots, *edges_and_others = pl.pallas_call(
        functools.partial(common_kernel, z),
        out_shape=(shape((z.common, LANES), bf16), shape((z.chunks, 8, LANES), f32), shape(s.shape, f32))
        + (
            shape((WIN * z.span, 2 * LANES), bf16),
            shape((z.parts, z.targets * z.chunk_rows, z.dips), bf16),
        )
        + (shape(edge, f32),) * z.sides
        + (shape((z.common, LANES), bf16),) * (z.targets - 1),
        in_specs=[HBM] * 7,
        out_specs=(VMEM,) * (4 + z.sides + z.targets),
        scratch_shapes=[
            pltpu.VMEM(u.shape, f32),
            pltpu.VMEM((z.lags - 1, 2, z.parts, z.rows, z.modes), bf16),
            pltpu.VMEM((z.parts, z.lags, z.modes), f32),
            pltpu.VMEM((2 * z.modes, z.modes // 4), bf16),
            pltpu.VMEM(v.shape, f32),
            pltpu.VMEM(s.shape, f32),
            pltpu.VMEM(y.shape, jnp.int32),
            pltpu.VMEM((z.chunk_rows, z.modes), f32),
            pltpu.VMEM((z.chunk_rows, z.modes), f32),
            pltpu.VMEM((z.chunks, z.spectral, LANES), f32),
            dma((7,)),
        ],
        compiler_params=FIRST,
        name="plane_and_history",
    )(*in_hbm(u, history, kernel.transpose(0, 2, 1, 3), phase_quarter(z.modes), v, s, y))

    edges, others = edges_and_others[:z.sides], edges_and_others[z.sides:]
    window = [common] + [
        lax.ppermute(other, "strike", ring(WIN * s)) for s, other in enumerate(others, 1)
    ]

    if z.sides == 2:
        is_high = lax.axis_index("normal") == z.normal - 1
        above, below = edges
        steps = [(i, i + 1) for i in range(z.normal - 1)]
        from_below = lax.ppermute(above, "normal", steps)
        from_above = lax.ppermute(
            jnp.where(is_high, above, below), "normal", [(j, i) for i, j in steps]
        )
        beside = [
            jnp.where(is_high, from_below, from_above),
            jnp.where(is_high, from_above, from_below),
        ]
    else:
        beside = [lax.ppermute(edges[0], "normal", [(0, 1), (1, 0)])]

    to_pair, to_cross, toeplitz = pl.pallas_call(
        functools.partial(halo_kernel, z),
        out_shape=(shape((z.halo, LANES), bf16),) * 2
        + (shape((z.parts, WIN * z.span, z.targets * z.nodes), f32),),
        in_specs=[VMEM] * (5 + z.sides),
        out_specs=(VMEM,) * 3,
        compiler_params=PARAMS,
        name="strike_edges_and_toeplitz",
    )(displacement, velocity, modulus, contact, response, *beside)
    from_pair = lax.ppermute(to_pair, "strike", [(i, i ^ 1) for i in range(z.strike)])
    from_cross = lax.ppermute(
        to_cross, "strike", [(i, (i - 1 + i % 2 * 2) % z.strike) for i in range(z.strike)]
    )

    block = (z.parts * z.span, z.dips)
    mine, *parcels = pl.pallas_call(
        functools.partial(middle_kernel, z),
        out_shape=(shape(block, f32),) + (shape(block, f32),) * (WIN - 1),
        in_specs=[VMEM] * (3 + z.targets),
        out_specs=(VMEM,) * WIN,
        scratch_shapes=[
            pltpu.VMEM((z.parts, 2 * z.targets * (z.nodes + z.chunk_rows), z.dips), bf16),
            pltpu.VMEM((z.parts, WIN * z.span, z.dips), f32),
        ],
        compiler_params=PARAMS,
        name="partial_tractions",
    )(wanted, spots, toeplitz, *window[1:], common)

    arrived = [
        lax.ppermute(parcels[w - 1], "strike", around(w)) for w in (3, 1, 2)
    ]
    base_u, base_v = pl.pallas_call(
        functools.partial(base_kernel, z),
        out_shape=(shape(u.shape, f32),) * 2,
        in_specs=[VMEM] * (3 + z.sides),
        out_specs=(VMEM,) * 2,
        scratch_shapes=[pltpu.VMEM((z.layers + 2 * z.sides, z.nodes, z.dips), f32)],
        compiler_params=PARAMS,
        name="unloaded_substeps",
    )(u, v, modulus, *beside)

    tail = (z.parts, TAIL * z.layers, z.dips)
    strip = (z.parts, z.layers, 2 * TAIL, z.dips)
    halos = pl.pallas_call(
        pass_kernel,
        out_shape=(shape(from_cross.shape, bf16),) * 2,
        in_specs=[VMEM] * 2,
        out_specs=(VMEM,) * 2,
        cost_estimate=pl.CostEstimate(flops=400000000, bytes_accessed=400000000, transcendentals=0),
        compiler_params=PARAMS,
        name="strike_halos",
    )(from_cross, from_pair)
    strip_u, strip_v, face_modulus, touching = pl.pallas_call(
        functools.partial(strips_kernel, z),
        out_shape=(
            shape(strip, f32),
            shape(strip, f32),
            shape((3, z.span, z.dips), f32),
            shape((z.span, z.dips), f32),
        ),
        in_specs=[VMEM] * (6 + z.sides),
        out_specs=(VMEM,) * 4,
        scratch_shapes=[
            pltpu.VMEM(tail, f32),
            pltpu.VMEM(tail, f32),
            pltpu.VMEM(tail[1:], f32),
            pltpu.VMEM((z.sides, edge[0], TAIL, z.dips), f32),
            pltpu.VMEM((z.layers + 2 * z.sides, 3 * TAIL, z.dips), f32),
        ],
        compiler_params=PARAMS,
        name="end_strips",
    )(u, v, modulus, contact, *halos, *beside)

    moved, speed = pl.pallas_call(
        functools.partial(final_kernel, z),
        out_shape=(shape(u.shape, f32),) * 2,
        in_specs=[VMEM] * (7 + len(arrived)),
        out_specs=(HBM,) * 2,
        scratch_shapes=[pltpu.VMEM(u.shape, f32), pltpu.VMEM(u.shape, f32), dma((2 * z.parts,))],
        compiler_params=PARAMS,
        name="add_force_response",
    )(mine, touching, face_modulus, base_u, base_v, strip_u, strip_v, *arrived)
    return (moved.reshape(displacement.shape), speed.reshape(displacement.shape))


def solution(mesh):
    return jax.shard_map(
        functools.partial(body, mesh),
        mesh=mesh,
        in_specs=(
            P(None, "strike", "normal", None),
            P(None, "strike", "normal", None),
            P("strike", "normal", None),
            P("strike", "normal", None),
            P(None, "strike", None),
            P(None, None, None, None, "strike", None),
            P(),
        ),
        out_specs=(P(None, "strike", "normal", None), P(None, "strike", "normal", None)),
        check_vma=False,
    )
```

```python
import functools
import itertools
import math

import jax
import jax.numpy as jnp
import numpy as np
from jax import lax
from jax.experimental import pallas as pl
from jax.experimental.pallas import tpu as pltpu
from jax.sharding import PartitionSpec as P

SUB = 3
BLK = 4
WIN = 4
TAIL = 8
LANES = 128

time_step = 0.5

f32 = jnp.float32
bf16 = jnp.bfloat16
VMEM = pl.BlockSpec(memory_space=pltpu.VMEM)


def round_up(value, step):
    return -(-value // step) * step


def phase_quarter(mode_count):
    phase = np.outer(np.arange(mode_count), np.arange(mode_count // 4)) % mode_count
    phase = phase * (2.0 * np.pi / mode_count)
    return np.concatenate([np.cos(phase), -np.sin(phase)]).astype(np.float32).astype(bf16)


class Sizes:
    def __init__(self, mesh, displacement, history):
        self.strike = mesh.shape["strike"]
        self.normal = mesh.shape["normal"]
        self.parts, self.nodes, self.layers, self.dips = displacement.shape
        self.lags = history.shape[1]
        self.rows = history.shape[4]
        self.modes = history.shape[5]
        self.chunks = self.modes // LANES
        self.spectral = round_up(self.parts * self.rows, 8)
        self.chunk_rows = round_up(self.spectral + 2 * self.parts, 16)
        self.plane_rows = self.parts * self.nodes
        self.common = self.plane_rows + round_up(3 * self.spectral, 16)
        self.halo_v = self.parts * 4 * self.layers
        self.halo_m = self.halo_v + self.parts * 2 * self.layers
        self.corner = self.halo_m + 2 * self.layers
        self.span = self.nodes + TAIL
        self.targets = self.strike // WIN
        self.stride = self.nodes * self.layers
        self.sides = 1 if self.normal == 2 else 2
        self.touch = self.sides * self.parts * 8
        self.halo = self.corner + round_up(self.touch + TAIL, 16)


def widen_flags(flags, dips):
    blocks = flags.shape[1]
    block_id = lax.broadcasted_iota(jnp.int32, (blocks, dips), 0)
    dip_id = lax.broadcasted_iota(jnp.int32, (blocks, dips), 1)
    spread = (dip_id // BLK == block_id).astype(bf16)
    wide = jnp.dot(flags.astype(f32).astype(bf16), spread, preferred_element_type=f32)
    return 1.0 - 0.5 * wide


def node_offset(rows):
    return jnp.where(rows < rows.shape[0] - TAIL // 2, rows, rows - rows.shape[0])


def layer_of(z, level):
    is_high = lax.axis_index("normal") == z.normal - 1
    return jnp.where(is_high, z.layers - 1 - level, level)


def beside_me(place):
    turn = place ^ (place >> 1)
    ahead, behind = (turn + 1) % WIN, (turn + WIN - 1) % WIN
    return (place, ahead ^ (ahead >> 1), behind ^ (behind >> 1), place ^ 3)


def start_all(pairs, sems):
    copies = [pltpu.make_async_copy(a, b, sems.at[i]) for i, (a, b) in enumerate(pairs)]
    for copy in copies:
        copy.start()
    return copies


def high_and_rest(values):
    high = values.astype(bf16)
    return high, (values - high.astype(f32)).astype(bf16)


def set_modulus(z, s_ref, y_ref, out_ref):
    soft = widen_flags(y_ref[...], z.dips)
    for n in range(z.nodes):
        at = n // BLK * z.layers
        rows = pl.ds(n * z.layers, z.layers)
        out_ref[rows, :] = s_ref[rows, :] * soft[at:at + z.layers]


def selections(z, wanted_ref, spots_ref):
    me = lax.axis_index("strike")
    place, group = me % WIN, me // WIN
    offset = node_offset(lax.broadcasted_iota(jnp.int32, (z.span, 2 * LANES), 0))
    lane = lax.broadcasted_iota(jnp.int32, (z.span, 2 * LANES), 1)
    wanted = []
    for t in range(WIN):
        node = t * z.nodes + offset
        node = jnp.where(node < 0, node + 2 * LANES, node)
        wanted.append((lane == node).astype(f32))
    wanted_ref[...] = jnp.concatenate(wanted, axis=0).astype(bf16)
    row = lax.broadcasted_iota(jnp.int32, (z.chunk_rows, z.dips), 0)
    ahead = lax.broadcasted_iota(jnp.int32, (z.chunk_rows, z.dips), 1) - row
    for c in range(z.parts):
        inside = (row >= c * z.rows) & (row < (c + 1) * z.rows)
        for s in range(z.targets):
            source = (group + z.targets - s) % z.targets
            spot = inside & (ahead == z.rows * (WIN * source + place) - c * z.rows)
            spots_ref[c, pl.ds(s * z.chunk_rows, z.chunk_rows), :] = spot.astype(f32).astype(bf16)


def common_kernel(z, u_hbm, h_hbm, k_hbm, t_hbm, v_hbm, s_hbm, y_hbm, out_ref, g_ref, m_ref, wanted_ref, spots_ref, *rest):
    edges, others = rest[:z.sides], rest[z.sides:z.sides + z.targets - 1]
    u_ref, h_ref, k_ref, t_ref, v_ref, s_ref, y_ref, re_ref, im_ref, line_ref, sems = rest[-11:]
    is_high = lax.axis_index("normal") == z.normal - 1
    face = is_high.astype(jnp.int32)
    copies = start_all(
        [
            (h_hbm.at[face, pl.ds(0, z.lags - 1)], h_ref),
            (k_hbm.at[face], k_ref),
            (t_hbm, t_ref),
            (u_hbm, u_ref),
            (v_hbm, v_ref),
            (s_hbm, s_ref),
            (y_hbm, y_ref),
        ],
        sems,
    )
    selections(z, wanted_ref, spots_ref)
    re_ref[...] = jnp.zeros_like(re_ref)
    im_ref[...] = jnp.zeros_like(im_ref)
    copies[1].wait()
    copies[0].wait()
    for c in range(z.parts):
        for q, dst in ((0, re_ref), (1, im_ref)):
            total = None
            for lag in range(1, z.lags):
                term = k_ref[c, pl.ds(lag, 1), :] * h_ref[lag - 1, q, c].astype(f32)
                total = term if total is None else total + term
            dst[pl.ds(c * z.rows, z.rows), :] = total
        newest = k_ref[c, pl.ds(0, 1), :]
        high = newest.astype(bf16).astype(f32)
        re_ref[pl.ds(z.spectral + c, 1), :] = high
        re_ref[pl.ds(z.spectral + z.parts + c, 1), :] = newest - high
    re, im = re_ref[...], im_ref[...]
    quarter = lax.broadcasted_iota(jnp.int32, (1, z.modes), 1) % 4
    one = (quarter == 0).astype(f32) - (quarter == 2).astype(f32)
    two = (quarter == 1).astype(f32) - (quarter == 3).astype(f32)
    flip = 1.0 - 2.0 * (quarter % 2).astype(f32)
    turned = jnp.concatenate(
        [
            jnp.concatenate([re, im], axis=1),
            jnp.concatenate([re * one - im * two, re * two + im * one], axis=1),
            jnp.concatenate([re * flip, im * flip], axis=1),
            jnp.concatenate([re * one + im * two, im * one - re * two], axis=1),
        ],
        axis=0,
    )
    copies[2].wait()
    lines = sum(
        jnp.dot(part, t_ref[...], preferred_element_type=f32) for part in high_and_rest(turned)
    ) * (1.0 / math.sqrt(z.modes))
    per_quarter = z.chunks // 4
    for m in range(4):
        for q in range(per_quarter):
            piece = lines[m * z.chunk_rows:(m + 1) * z.chunk_rows, q * LANES:(q + 1) * LANES]
            chunk = m * per_quarter + q
            line_ref[chunk] = piece[:z.spectral]
            g_ref[chunk] = piece[z.spectral:z.spectral + 8]
    group = lax.axis_index("strike") // WIN
    lane = lax.broadcasted_iota(jnp.int32, (z.spectral, LANES), 1)
    for s, ref in enumerate((out_ref,) + others):
        chunk = (group + s) % z.targets
        after, before = line_ref[(chunk + 1) % z.chunks], line_ref[(chunk + z.chunks - 1) % z.chunks]
        both = jnp.concatenate(
            [line_ref[chunk], jnp.where(lane < LANES // 2, after, before)], axis=0
        )
        high, rest = (part.astype(f32) for part in high_and_rest(both))
        pieces = [high, rest[:z.spectral]]
        spare = z.common - z.plane_rows - 3 * z.spectral
        pieces += [jnp.zeros((spare, LANES), f32)] if spare else []
        at = pl.ds(z.plane_rows, z.common - z.plane_rows)
        ref[at, :] = jnp.concatenate(pieces, axis=0).astype(bf16)
    copies[3].wait()
    layer = face * (z.layers - 1)
    for c in range(z.parts):
        plane = u_ref[pl.ds(c * z.stride + layer, z.nodes, stride=z.layers), :].astype(bf16)
        for ref in (out_ref,) + others:
            ref[pl.ds(c * z.nodes, z.nodes), :] = plane
    for copy in copies[4:]:
        copy.wait()
    set_modulus(z, s_ref, y_ref, m_ref)
    size = z.layers
    for out, levels in zip(edges, ((size - 1, size - 2, size - 3), (0, 1, 2))):
        for j, f in enumerate(levels):
            layer = layer_of(z, f)
            for c in range(z.parts):
                at = pl.ds(c * z.stride + layer, z.nodes, stride=size)
                out[3 * c + j] = u_ref[at, :]
                if j < 2:
                    out[3 * z.parts + 2 * c + j] = v_ref[at, :]
            if j < 2:
                out[5 * z.parts + j] = m_ref[pl.ds(layer, z.nodes, stride=size), :]


def toeplitz_factors(z, g_ref, out_ref):
    me = lax.axis_index("strike")
    group = me // WIN
    lane = lax.broadcasted_iota(jnp.int32, (8, LANES), 1)
    row = lax.broadcasted_iota(jnp.int32, (8, LANES), 0)
    stack = []
    for c in range(z.parts):
        line = jnp.concatenate(
            [
                g_ref[j, pl.ds(c, 1), :] + g_ref[j, pl.ds(z.parts + c, 1), :]
                for j in ((k - group + z.chunks) % z.chunks for k in range(z.chunks))
            ],
            axis=1,
        ) * (1.0 / math.sqrt(z.modes))
        stack.append(jnp.broadcast_to(line, (8, z.modes)))
    wide = pltpu.roll(jnp.concatenate(stack, axis=0), 0, 1, stride=1, stride_axis=0)
    for c in range(z.parts):
        columns = [wide[8 * c:8 * c + 8, j * LANES:(j + 1) * LANES] for j in range(z.chunks)]

        turned = {}

        def turn(j, shift):
            key = (j % z.chunks, shift % LANES)
            if key not in turned:
                piece = columns[key[0]]
                turned[key] = pltpu.roll(piece, key[1], 1) if key[1] else piece
            return turned[key]

        def eight_rows(shift, q):
            whole, rest = divmod((shift - 8 * c) % z.modes, LANES)
            tile = None
            for k in range(WIN):
                j = q * WIN + k - whole
                first = k * z.nodes
                if rest == 0:
                    piece = turn(j, first)
                elif rest >= z.nodes:
                    piece = turn(j - 1, first + rest)
                else:
                    piece = jnp.where(
                        lane < first + rest, turn(j - 1, first + rest), turn(j, first + rest)
                    )
                tile = piece if k == 0 else jnp.where(lane < first, tile, piece)
            return tile

        for t in range(1 - WIN, WIN):
            for q in range(z.chunks // WIN):
                for k in range(z.span // 8):
                    tile = eight_rows(t * z.nodes + 8 * k, q)
                    if 8 * k == z.nodes:
                        tile = jnp.where(row < TAIL // 2, tile, eight_rows(t * z.nodes - 8, q))
                    at = pl.ds((t + WIN - 1) * z.span + 8 * k, 8)
                    out_ref[c, at, q * LANES:(q + 1) * LANES] = tile


def halo_kernel(z, u_ref, v_ref, m_ref, c_ref, g_ref, *rest):
    beside = rest[:z.sides]
    pair_ref, cross_ref, toeplitz_ref = rest[z.sides:]
    toeplitz_factors(z, g_ref, toeplitz_ref)
    is_high = lax.axis_index("normal") == z.normal - 1
    is_even = lax.axis_index("strike") % 2 == 0
    size = z.layers
    for ref, is_end in ((pair_ref, is_even), (cross_ref, jnp.logical_not(is_even))):
        nodes = [jnp.where(is_end, z.nodes - 1 - d, d) for d in range(3)]
        for c in range(z.parts):
            tiles = []
            known = None
            for node in nodes:
                tile = u_ref[c, node]
                if known is None:
                    high = tile.astype(bf16).astype(f32)
                    tiles += [high, tile - high]
                    known = high + (tile - high).astype(bf16).astype(f32)
                else:
                    tiles.append(tile - known)
                    known = known + tiles[-1].astype(bf16).astype(f32)
            at = pl.ds(c * 4 * size, 4 * size)
            ref[at, :] = jnp.concatenate(tiles, axis=0).astype(bf16)
            both = jnp.concatenate([v_ref[c, nodes[0]], v_ref[c, nodes[1]]], axis=0).astype(bf16)
            ref[pl.ds(z.halo_v + c * 2 * size, 2 * size), :] = both
        both = jnp.concatenate(
            [m_ref[pl.ds(pl.multiple_of(node * size, size), size), :] for node in nodes[:2]], axis=0
        )
        ref[pl.ds(z.halo_m, 2 * size), :] = both.astype(bf16)
        own = jnp.where(is_high, c_ref[1], c_ref[0])
        touch = jnp.where(is_end, own[z.nodes - TAIL:], own[:TAIL]).astype(f32)

        def rows_of(edge, k, count):
            head = edge[k, pl.ds(0, count), :]
            return jnp.where(is_end, edge[k, pl.ds(z.nodes - count, count), :], head)

        pieces = []
        for edge in beside:
            for c in range(z.parts):
                some = jnp.concatenate(
                    [rows_of(edge, 3 * c, 2), rows_of(edge, 3 * c + 1, 1)], axis=0
                )
                high = some.astype(bf16).astype(f32)
                speed = rows_of(edge, 3 * z.parts + 2 * c, 1)
                pieces += [high, some - high, speed, rows_of(edge, 5 * z.parts, 1)]
        pieces.append(touch)
        spare = z.halo - z.corner - z.touch - TAIL
        if spare:
            pieces.append(jnp.zeros((spare, z.dips), f32))
        ref[pl.ds(z.corner, z.halo - z.corner), :] = jnp.concatenate(pieces, axis=0).astype(bf16)


def middle_kernel(z, wanted_ref, spots_ref, toeplitz_ref, *rest):
    window = (rest[z.targets - 1],) + rest[:z.targets - 1]
    mine_ref = rest[z.targets]
    out_refs, stack_ref, part_ref = rest[z.targets + 1:-2], rest[-2], rest[-1]
    me = lax.axis_index("strike")
    place, group = me % WIN, me // WIN
    spare = jnp.zeros((z.chunk_rows - z.spectral, 2 * LANES), f32)
    lines = []
    size = z.spectral
    for j, ref in itertools.product(range(2), window):
        part = ref[pl.ds(z.plane_rows, z.common - z.plane_rows), :].astype(f32)
        near = part[size:2 * size] if j == 0 else jnp.zeros((size, LANES), f32)
        lines += [jnp.concatenate([part[2 * j * size:(2 * j + 1) * size], near], axis=1), spare]
    picked = lax.dot_general(
        wanted_ref[...],
        jnp.concatenate(lines, axis=0).astype(bf16),
        (((1,), (1,)), ((), ())),
        preferred_element_type=f32,
    )
    own_rows = z.targets * z.nodes
    own = pl.ds(pl.multiple_of((WIN - 1 - place) * z.span, 8), WIN * z.span)
    for c in range(z.parts):
        for s, ref in enumerate(window):
            source = (group + z.targets - s) % z.targets
            at = pl.multiple_of(source * z.nodes, z.nodes)
            plane = ref[pl.ds(c * z.nodes, z.nodes), :]
            stack_ref[c, pl.ds(at, z.nodes), :] = plane
            stack_ref[c, pl.ds(at + own_rows, z.nodes), :] = plane
        for j in range(2):
            at = pl.ds(2 * own_rows + j * z.targets * z.chunk_rows, z.targets * z.chunk_rows)
            stack_ref[c, at, :] = spots_ref[c]
        factors = jnp.concatenate([*high_and_rest(toeplitz_ref[c, own, :]), picked.astype(bf16)], axis=1)
        part_ref[c] = jnp.dot(factors, stack_ref[c], preferred_element_type=f32)
    for spot, ref in zip(beside_me(place), (mine_ref,) + out_refs):
        at = pl.ds(pl.multiple_of(spot * z.span, 8), z.span)
        ref[...] = jnp.concatenate([part_ref[c, at, :] for c in range(z.parts)], axis=0)


def unpack(z, left_ref, right_ref, uh_ref, vh_ref, mh_ref):
    size = z.layers
    for ref, is_left in ((right_ref, False), (left_ref, True)):
        spots = [pl.ds((TAIL - 1 - d if is_left else d) * size, size) for d in range(3)]
        for c in range(z.parts):
            tiles = ref[pl.ds(c * 4 * size, 4 * size), :].astype(f32)
            known = tiles[:size]
            for d in range(3):
                known = known + tiles[(d + 1) * size:(d + 2) * size]
                uh_ref[c, spots[d], :] = known
            both = ref[pl.ds(z.halo_v + c * 2 * size, 2 * size), :].astype(f32)
            vh_ref[c, spots[0], :] = both[:size]
            vh_ref[c, spots[1], :] = both[size:]
        both = ref[pl.ds(z.halo_m, 2 * size), :].astype(f32)
        mh_ref[spots[0], :] = both[:size]
        mh_ref[spots[1], :] = both[size:]
    for c in range(z.parts):
        uh_ref[c, pl.ds(3 * size, 2 * size), :] = jnp.zeros((2 * size, z.dips), f32)
        vh_ref[c, pl.ds(2 * size, 4 * size), :] = jnp.zeros((4 * size, z.dips), f32)
    mh_ref[pl.ds(2 * size, 4 * size), :] = jnp.zeros((4 * size, z.dips), f32)


def corner_tiles(z, left_ref, right_ref, tile_ref):
    rows = pl.ds(z.corner, z.halo - z.corner)
    after, before = right_ref[rows, :].astype(f32), left_ref[rows, :].astype(f32)
    blank = jnp.zeros((TAIL, z.dips), f32)

    def tile(head, tail):
        return jnp.concatenate([head, blank[:TAIL - head.shape[0] - tail.shape[0]], tail], axis=0)

    for side in range(z.sides):
        for c in range(z.parts):
            at = 8 * (side * z.parts + c)
            a, b = after[at:at + 8], before[at:at + 8]
            head, tail = a[0:3] + a[3:6], b[0:3] + b[3:6]
            tile_ref[side, 3 * c] = tile(head[:2], tail[:2])
            tile_ref[side, 3 * c + 1] = tile(head[2:], tail[2:])
            tile_ref[side, 3 * c + 2] = blank
            tile_ref[side, 3 * z.parts + 2 * c] = tile(a[6:7], b[6:7])
            tile_ref[side, 3 * z.parts + 2 * c + 1] = blank
            if c == 0:
                tile_ref[side, 5 * z.parts] = tile(a[7:8], b[7:8])
                tile_ref[side, 5 * z.parts + 1] = blank


def in_plane(values, first_dip, last_dip):
    count, dips = values.shape
    around = pltpu.roll(values, 1, 0) + pltpu.roll(values, count - 1, 0)
    around += jnp.where(first_dip, 0.0, pltpu.roll(values, 1, 1))
    around += jnp.where(last_dip, 0.0, pltpu.roll(values, dips - 1, 1))
    return around - 6.0 * values


def substeps(z, fetch, rows, store, m_ref):
    dip = lax.broadcasted_iota(jnp.int32, (rows, z.dips), 1)
    first_dip, last_dip = dip == 0, dip == z.dips - 1
    two = z.sides == 2
    low = -2 if two else 0
    top = z.layers
    for f in range(low, top + 2):
        m_ref[f - low] = (time_step * time_step) * fetch("m", 0, f)

    for c in range(z.parts):
        u = {f: fetch("u", c, f) for f in range(low - 1 if two else 0, top + 3)}
        v = {f: time_step * fetch("v", c, f) for f in range(low, top + 2)}
        for step in range(SUB):
            levels = range(low + step if two else 0, top + 2 - step)
            for f in levels:
                lap = in_plane(u[f], first_dip, last_dip) + u[f + 1]
                if f - 1 in u:
                    lap += u[f - 1]
                v[f] = v[f] + m_ref[f - low] * lap
            u = {f: u[f] + v[f] for f in levels}
        for f in range(top):
            store(c, f, u[f], (1.0 / time_step) * v[f])


def beside_index(z, kind, c, f):
    side, j = (0, f - z.layers) if f >= z.layers else (1, -1 - f)
    return side, {"u": 3 * c, "v": 3 * z.parts + 2 * c, "m": 5 * z.parts}[kind] + j


def base_kernel(z, u_ref, v_ref, m_ref, *rest):
    sides = rest[:z.sides]
    out_u, out_v, gathered_ref = rest[z.sides:]

    def fetch(kind, c, f):
        if 0 <= f < z.layers:
            first = 0 if kind == "m" else c * z.stride
            own = {"u": u_ref, "v": v_ref, "m": m_ref}[kind]
            return own[pl.ds(first + layer_of(z, f), z.nodes, stride=z.layers), :]
        side, at = beside_index(z, kind, c, f)
        return sides[side][at]

    def store(c, f, u, v):
        at = pl.ds(c * z.stride + layer_of(z, f), z.nodes, stride=z.layers)
        out_u[at, :] = u
        out_v[at, :] = v

    substeps(z, fetch, z.nodes, store, gathered_ref)


def strips_kernel(z, u_ref, v_ref, m_ref, c_ref, cross_ref, pair_ref, *rest):
    sides = rest[:z.sides]
    out_u, out_v, mf_ref, ch_ref, uh_ref, vh_ref, mh_ref, tile_ref, gathered_ref = rest[z.sides:]
    place = lax.axis_index("normal")
    is_high = place == z.normal - 1
    is_face = (is_high | (place == 0)).astype(f32)
    ch_ref[pl.ds(0, z.nodes), :] = jnp.where(is_high, c_ref[1], c_ref[0]).astype(f32) * is_face

    def receive(left_ref, right_ref):
        unpack(z, left_ref, right_ref, uh_ref, vh_ref, mh_ref)
        corner_tiles(z, left_ref, right_ref, tile_ref)
        row = lax.broadcasted_iota(jnp.int32, (TAIL, z.dips), 0)
        rows = pl.ds(z.corner, z.halo - z.corner)
        before = left_ref[rows, :].astype(f32)[z.touch:z.touch + TAIL]
        after = right_ref[rows, :].astype(f32)[z.touch:z.touch + TAIL]
        ch_ref[pl.ds(z.nodes, TAIL), :] = jnp.where(row < TAIL // 2, after, before) * is_face

    is_even = lax.axis_index("strike") % 2 == 0

    @pl.when(is_even)
    def _():
        receive(cross_ref, pair_ref)

    @pl.when(jnp.logical_not(is_even))
    def _():
        receive(pair_ref, cross_ref)

    last = z.nodes - TAIL

    def fetch(kind, c, f):
        if 0 <= f < z.layers:
            layer = layer_of(z, f)
            first = layer if kind == "m" else c * z.stride + layer
            own = {"u": u_ref, "v": v_ref, "m": m_ref}[kind]
            tail = mh_ref if kind == "m" else (uh_ref if kind == "u" else vh_ref).at[c]
            pieces = [
                own[pl.ds(first + last * z.layers, TAIL, stride=z.layers), :],
                tail[pl.ds(layer, TAIL, stride=z.layers), :],
                own[pl.ds(first, TAIL, stride=z.layers), :],
            ]
        else:
            side, at = beside_index(z, kind, c, f)
            edge = sides[side]
            pieces = [edge[at, pl.ds(last, TAIL), :], tile_ref[side, at], edge[at, pl.ds(0, TAIL), :]]
        return jnp.concatenate(pieces, axis=0)

    def store(c, f, u, v):
        for out, x in ((out_u, u), (out_v, v)):
            out[c, f, pl.ds(0, TAIL), :] = x[2 * TAIL:]
            out[c, f, pl.ds(TAIL, TAIL), :] = x[:TAIL]

    substeps(z, fetch, 3 * TAIL, store, gathered_ref)
    for f in range(3):
        layer = layer_of(z, f)
        mf_ref[f, pl.ds(0, z.nodes), :] = m_ref[pl.ds(layer, z.nodes, stride=z.layers), :]
        mf_ref[f, pl.ds(z.nodes, TAIL), :] = mh_ref[pl.ds(layer, TAIL, stride=z.layers), :]


def final_kernel(z, mine_ref, contact_ref, m_ref, base_u, base_v, strip_u, strip_v, *rest):
    arrived, (out_u, out_v, u_ref, v_ref, sems) = rest[:-5], rest[-5:]
    dip = lax.broadcasted_iota(jnp.int32, (z.span, z.dips), 1)
    first_dip, last_dip = dip == 0, dip == z.dips - 1
    contact = contact_ref[...]
    m0, m1, m2 = m_ref[0], m_ref[1], m_ref[2]
    h = time_step
    arrived = [ref[...] for ref in arrived]
    copies = []
    half = TAIL // 2
    for c in range(z.parts):
        force = mine_ref[pl.ds(c * z.span, z.span), :]
        for other in arrived:
            force = force + other[c * z.span:(c + 1) * z.span]
        force = force * contact
        v0 = h * force
        u0 = h * v0
        v1 = h * (m1 * u0)
        v0 = v0 + h * (m0 * in_plane(u0, first_dip, last_dip) + force)
        u0 = u0 + h * v0
        u1 = h * v1
        v2 = h * (m2 * u1)
        w0 = v0 + h * (m0 * (in_plane(u0, first_dip, last_dip) + u1) + force)
        v1 = v1 + h * (m1 * (in_plane(u1, first_dip, last_dip) + u0))
        pairs = ((u0 + h * w0, w0), (u1 + h * v1, v1), (h * v2, v2))
        part = pl.ds(c * z.stride, z.stride)
        whole = ((base_u, strip_u, u_ref, out_u), (base_v, strip_v, v_ref, out_v))
        for k, (base, strip, sums, out) in enumerate(whole):
            sums[part, :] = base[part, :]
            for f in range(z.layers):
                first = c * z.stride + layer_of(z, f)
                late = first + (z.nodes - half) * z.layers
                sums[pl.ds(first, half, stride=z.layers), :] = strip[c, f, pl.ds(0, half), :]
                sums[pl.ds(late, half, stride=z.layers), :] = strip[c, f, pl.ds(2 * TAIL - half, half), :]
            for f in range(3):
                at = pl.ds(c * z.stride + layer_of(z, f), z.nodes, stride=z.layers)
                sums[at, :] = sums[at, :] + pairs[f][k][:z.nodes]
            copies.append(
                pltpu.make_async_copy(sums.at[part, :], out.at[part, :], sems.at[2 * c + k])
            )
            copies[-1].start()
    for copy in copies:
        copy.wait()


PARAMS = pltpu.CompilerParams(vmem_limit_bytes=32 * 2**20)
FIRST = pltpu.CompilerParams(vmem_limit_bytes=32 * 2**20)
HBM = pl.BlockSpec(memory_space=pltpu.HBM)


def in_hbm(*arrays):
    return [pltpu.with_memory_space_constraint(x, pltpu.HBM) for x in arrays]


def pass_kernel(*refs):
    for in_ref, out_ref in zip(refs[:2], refs[2:]):
        out_ref[...] = in_ref[...]


def shape(dims, kind):
    return jax.ShapeDtypeStruct(dims, kind)


def body(mesh, displacement, velocity, stiffness, yield_flags, contact, history, kernel):
    z = Sizes(mesh, displacement, history)
    u = displacement.reshape(-1, z.dips)
    v = velocity.reshape(-1, z.dips)
    s = stiffness.reshape(-1, z.dips)
    y = yield_flags.reshape(-1, yield_flags.shape[2])
    dma = pltpu.SemaphoreType.DMA
    ring = lambda step: [(i, (i + step) % z.strike) for i in range(z.strike)]
    around = lambda w: [(i, i - i % WIN + beside_me(i % WIN)[w]) for i in range(z.strike)]

    edge = (5 * z.parts + 2, z.nodes, z.dips)
    common, response, modulus, wanted, spots, *edges_and_others = pl.pallas_call(
        functools.partial(common_kernel, z),
        out_shape=(shape((z.common, LANES), bf16), shape((z.chunks, 8, LANES), f32), shape(s.shape, f32))
        + (
            shape((WIN * z.span, 2 * LANES), bf16),
            shape((z.parts, z.targets * z.chunk_rows, z.dips), bf16),
        )
        + (shape(edge, f32),) * z.sides
        + (shape((z.common, LANES), bf16),) * (z.targets - 1),
        in_specs=[HBM] * 7,
        out_specs=(VMEM,) * (4 + z.sides + z.targets),
        scratch_shapes=[
            pltpu.VMEM(u.shape, f32),
            pltpu.VMEM((z.lags - 1, 2, z.parts, z.rows, z.modes), bf16),
            pltpu.VMEM((z.parts, z.lags, z.modes), f32),
            pltpu.VMEM((2 * z.modes, z.modes // 4), bf16),
            pltpu.VMEM(v.shape, f32),
            pltpu.VMEM(s.shape, f32),
            pltpu.VMEM(y.shape, jnp.int32),
            pltpu.VMEM((z.chunk_rows, z.modes), f32),
            pltpu.VMEM((z.chunk_rows, z.modes), f32),
            pltpu.VMEM((z.chunks, z.spectral, LANES), f32),
            dma((7,)),
        ],
        compiler_params=FIRST,
        name="plane_and_history",
    )(*in_hbm(u, history, kernel.transpose(0, 2, 1, 3), phase_quarter(z.modes), v, s, y))

    edges, others = edges_and_others[:z.sides], edges_and_others[z.sides:]
    window = [common] + [
        lax.ppermute(other, "strike", ring(WIN * s)) for s, other in enumerate(others, 1)
    ]

    if z.sides == 2:
        is_high = lax.axis_index("normal") == z.normal - 1
        above, below = edges
        steps = [(i, i + 1) for i in range(z.normal - 1)]
        from_below = lax.ppermute(above, "normal", steps)
        from_above = lax.ppermute(
            jnp.where(is_high, above, below), "normal", [(j, i) for i, j in steps]
        )
        beside = [
            jnp.where(is_high, from_below, from_above),
            jnp.where(is_high, from_above, from_below),
        ]
    else:
        beside = [lax.ppermute(edges[0], "normal", [(0, 1), (1, 0)])]

    to_pair, to_cross, toeplitz = pl.pallas_call(
        functools.partial(halo_kernel, z),
        out_shape=(shape((z.halo, LANES), bf16),) * 2
        + (shape((z.parts, (2 * WIN - 1) * z.span, z.targets * z.nodes), f32),),
        in_specs=[VMEM] * (5 + z.sides),
        out_specs=(VMEM,) * 3,
        compiler_params=PARAMS,
        name="strike_edges_and_toeplitz",
    )(displacement, velocity, modulus, contact, response, *beside)
    from_pair = lax.ppermute(to_pair, "strike", [(i, i ^ 1) for i in range(z.strike)])
    from_cross = lax.ppermute(
        to_cross, "strike", [(i, (i - 1 + i % 2 * 2) % z.strike) for i in range(z.strike)]
    )

    block = (z.parts * z.span, z.dips)
    mine, *parcels = pl.pallas_call(
        functools.partial(middle_kernel, z),
        out_shape=(shape(block, f32),) + (shape(block, f32),) * (WIN - 1),
        in_specs=[VMEM] * (3 + z.targets),
        out_specs=(VMEM,) * WIN,
        scratch_shapes=[
            pltpu.VMEM((z.parts, 2 * z.targets * (z.nodes + z.chunk_rows), z.dips), bf16),
            pltpu.VMEM((z.parts, WIN * z.span, z.dips), f32),
        ],
        compiler_params=PARAMS,
        name="partial_tractions",
    )(wanted, spots, toeplitz, *window[1:], common)

    arrived = [
        lax.ppermute(parcels[w - 1], "strike", around(w)) for w in (3, 1, 2)
    ]
    base_u, base_v = pl.pallas_call(
        functools.partial(base_kernel, z),
        out_shape=(shape(u.shape, f32),) * 2,
        in_specs=[VMEM] * (3 + z.sides),
        out_specs=(VMEM,) * 2,
        scratch_shapes=[pltpu.VMEM((z.layers + 2 * z.sides, z.nodes, z.dips), f32)],
        compiler_params=PARAMS,
        name="unloaded_substeps",
    )(u, v, modulus, *beside)

    tail = (z.parts, TAIL * z.layers, z.dips)
    strip = (z.parts, z.layers, 2 * TAIL, z.dips)
    halos = pl.pallas_call(
        pass_kernel,
        out_shape=(shape(from_cross.shape, bf16),) * 2,
        in_specs=[VMEM] * 2,
        out_specs=(VMEM,) * 2,
        cost_estimate=pl.CostEstimate(flops=400000000, bytes_accessed=400000000, transcendentals=0),
        compiler_params=PARAMS,
        name="strike_halos",
    )(from_cross, from_pair)
    strip_u, strip_v, face_modulus, touching = pl.pallas_call(
        functools.partial(strips_kernel, z),
        out_shape=(
            shape(strip, f32),
            shape(strip, f32),
            shape((3, z.span, z.dips), f32),
            shape((z.span, z.dips), f32),
        ),
        in_specs=[VMEM] * (6 + z.sides),
        out_specs=(VMEM,) * 4,
        scratch_shapes=[
            pltpu.VMEM(tail, f32),
            pltpu.VMEM(tail, f32),
            pltpu.VMEM(tail[1:], f32),
            pltpu.VMEM((z.sides, edge[0], TAIL, z.dips), f32),
            pltpu.VMEM((z.layers + 2 * z.sides, 3 * TAIL, z.dips), f32),
        ],
        compiler_params=PARAMS,
        name="end_strips",
    )(u, v, modulus, contact, *halos, *beside)

    moved, speed = pl.pallas_call(
        functools.partial(final_kernel, z),
        out_shape=(shape(u.shape, f32),) * 2,
        in_specs=[VMEM] * (7 + len(arrived)),
        out_specs=(HBM,) * 2,
        scratch_shapes=[pltpu.VMEM(u.shape, f32), pltpu.VMEM(u.shape, f32), dma((2 * z.parts,))],
        compiler_params=PARAMS,
        name="add_force_response",
    )(mine, touching, face_modulus, base_u, base_v, strip_u, strip_v, *arrived)
    return (moved.reshape(displacement.shape), speed.reshape(displacement.shape))


def solution(mesh):
    return jax.shard_map(
        functools.partial(body, mesh),
        mesh=mesh,
        in_specs=(
            P(None, "strike", "normal", None),
            P(None, "strike", "normal", None),
            P("strike", "normal", None),
            P("strike", "normal", None),
            P(None, "strike", None),
            P(None, None, None, None, "strike", None),
            P(),
        ),
        out_specs=(P(None, "strike", "normal", None), P(None, "strike", "normal", None)),
        check_vma=False,
    )
```
